32 devices in a mesh: section: 2 (over x), dp: 16 (over z, y, core).
Axes of the slice: x: 2, y: 2, z: 4, core: 2. Of those that a mesh axis runs over, the one named last changes fastest.
Arguments:
- saved: bfloat16 [2, 2, 2048, 4096], P('section', None, 'dp'), may hold values from -6 to 6
- top_grad: bfloat16 [2, 2048, 4096], P(None, 'dp'), may hold values from -0.4375 to 0.4375
- gains: float32 [2, 2, 4096], P('section'), may hold values from 0.1 to 1.9
- adapter_in: bfloat16 [2, 2, 4096, 32], P('section'), may hold values from -0.09375 to 0.09375
- adapter_out: bfloat16 [2, 2, 32, 4096], P('section'), may hold values from -1 to 1
Outputs:
- grad_in: float32 [2, 4096, 32], P('section', 'dp')
- grad_out: float32 [2, 32, 4096], P('section', None, 'dp')
The draws below stay inside these ranges and needn't reach their ends.
All inputs are finite; a program needn't handle non-finite values.
Results may differ from the reference program's by a relative error of at most 0.014.
Values may be sent and summed in bfloat16 or wider, within the bound.
No kernel may reach another device: no remote copies, remote signals or barrier semaphores. Data moves between devices by JAX's collectives and lax.ppermute only.
A program may use at most 64 MiB of HBM per device.

```python
import jax
import jax.numpy as jnp
from jax import lax

D = 4096
RANK = 32
SECTIONS = 2
TOKENS = 2048
N_SECTION = 2


def raised(array, own_key, source, target, blocks, factor):
    def block_of(position):
        return (jnp.arange(array.shape[position]) // (array.shape[position] // blocks)).reshape((-1,) + (1,) * (array.ndim - 1 - position))

    first = jax.random.permutation(own_key, blocks)[block_of(target)]
    second = (block_of(target) + blocks // 2) % blocks
    return jnp.where((block_of(source) == first) | (block_of(source) == second), factor * array, array)


def shard_levels(stream_key, extent, split, low, largest):
    level = 1.0
    for position, shards_of in split:
        heights = jax.random.uniform(jax.random.fold_in(jax.random.fold_in(stream_key, 6), position), (shards_of,), jnp.float32, low / len(split), largest / len(split))
        level = level * jnp.repeat(jnp.exp(heights), extent[position] // shards_of).reshape((-1,) + (1,) * (len(extent) - 1 - position))
    return level


def bell_draw(stream_key, extent, width, bound, pieces=(), kind=jnp.bfloat16):
    loudness = shard_levels(stream_key, extent, pieces, -0.22, 0.18) if pieces else 1.0
    entries = jax.random.normal(stream_key, extent, jnp.float32) * width * loudness
    return jnp.minimum(jnp.maximum(entries, -bound), bound).astype(kind)


def heavy_noise(own_key, dims, spread, reach, split, heavy, dtype=jnp.bfloat16):
    drawn = spread * jax.random.normal(own_key, dims, jnp.float32)
    if split:
        drawn = drawn * shard_levels(own_key, dims, split, -0.22, 0.18)
    return jnp.clip(raised(drawn, jax.random.fold_in(own_key, 3), *heavy), -reach, reach).astype(dtype)


def setup_inputs(seed: int = 0) -> dict:
    arg_keys = jax.random.split(jax.random.key(seed), 6)
    return {
        "saved": bell_draw(arg_keys[0], (SECTIONS, 2, TOKENS, D), 1.0, 6.0, ((0, 2), (2, 16))),
        "top_grad": heavy_noise(arg_keys[1], (2, TOKENS, D), (TOKENS ** -0.5), 0.4375, ((1, 16),), (1, 2, 16, 2.0)),
        "gains": jnp.clip(1.0 + 0.18 * jax.random.normal(arg_keys[2], (SECTIONS, 2, D), jnp.float32), 0.1, 1.9),
        "adapter_in": bell_draw(arg_keys[3], (SECTIONS, 2, D, RANK), D ** -0.5, 0.09375, ((0, 2),)),
        "adapter_out": bell_draw(arg_keys[4], (SECTIONS, 2, RANK, D), RANK ** -0.5, 1.0, ((0, 2),)),
    }


EPS = 1e-05

def section_back(x, upstream, gain, weight_in, weight_out):
    xf = x.astype(jnp.float32)
    scale = lax.rsqrt(lax.optimization_barrier(jnp.mean(xf * xf, axis=-1, keepdims=True)) + EPS)
    normed = xf * scale
    hidden = (normed * gain).astype(jnp.bfloat16)
    pre = jnp.dot(hidden, weight_in, preferred_element_type=jnp.float32)
    sig = jax.nn.sigmoid(pre)
    active = (pre * sig).astype(jnp.bfloat16)
    delta_act = jnp.dot(upstream, weight_out.T, preferred_element_type=jnp.float32)
    delta_pre = (delta_act * sig * (1.0 + pre * (1.0 - sig))).astype(jnp.bfloat16)
    delta_hidden = jnp.dot(delta_pre, weight_in.T, preferred_element_type=jnp.float32)
    delta_norm = delta_hidden * gain
    inner = lax.optimization_barrier(jnp.mean(delta_norm * normed, axis=-1, keepdims=True))
    result = (upstream.astype(jnp.float32) + scale * (delta_norm - normed * inner)).astype(jnp.bfloat16)
    term_in = jnp.dot(hidden.T, delta_pre, preferred_element_type=jnp.float32)
    term_out = jnp.dot(active.T, upstream, preferred_element_type=jnp.float32)
    return (result, term_in, term_out)

def reference(saved, top_grad, gains, adapter_in, adapter_out):
    sections = N_SECTION
    sums_in = [jnp.zeros((D, RANK), jnp.float32) for j in range(sections)]
    sums_out = [jnp.zeros((RANK, D), jnp.float32) for j in range(sections)]
    for replica in range(2):
        upstream = top_grad[replica]
        for j in reversed(range(sections)):
            where = j if replica == 0 else sections - 1 - j
            upstream, term_in, term_out = section_back(saved[where, replica], upstream, gains[where, replica], adapter_in[where, replica], adapter_out[where, replica])
            sums_in[j] = sums_in[j] + term_in
            sums_out[j] = sums_out[j] + term_out
    return (jnp.stack(sums_in), jnp.stack(sums_out))
```

```python
from functools import partial

import jax
import jax.numpy as jnp
from jax import lax
from jax.experimental import pallas as pl
from jax.experimental.pallas import tpu as pltpu
from jax.sharding import PartitionSpec as P

EPS = 1e-05
VMEM_BYTES = 48 * 1024 * 1024
F32 = jnp.float32
BF16 = jnp.bfloat16


def nn(a, b):
    return lax.dot_general(a, b, (((1,), (0,)), ((), ())), preferred_element_type=F32)


def nt(a, b):
    return lax.dot_general(a, b, (((1,), (1,)), ((), ())), preferred_element_type=F32)


def tn(a, b):
    return lax.dot_general(a, b, (((0,), (0,)), ((), ())), preferred_element_type=F32)


def as_row(column):
    count = column.shape[0]
    return jnp.transpose(jnp.broadcast_to(column, (count, count)))[0:1, :]


def silu_slope(pre):
    sig = jax.nn.sigmoid(pre)
    return sig, sig * (1.0 + pre * (1.0 - sig))


def project(x_ref, gain_ref, w_ref, xg_ref, step):
    tokens, width = x_ref.shape
    squares = jnp.zeros((tokens, 128), F32)
    pre = jnp.zeros((w_ref.shape[0], tokens), F32)
    for c in range(0, width, step):
        x = x_ref[:, c : c + step].astype(F32)
        for k in range(0, step, 128):
            part = x[:, k : k + 128]
            squares += part * part
        xg = (x * gain_ref[:, c : c + step]).astype(BF16)
        xg_ref[:, c : c + step] = xg
        pre += nt(w_ref[:, c : c + step], xg)
    mean = jnp.sum(squares, axis=1, keepdims=True) * (1.0 / width)
    scale = lax.rsqrt(mean + EPS)
    return scale, pre


def upper_kernel(
    share, place_ref, saved, top, gains, w_in, w_out,
    out_ref, flow_ref, xg0_ref, low_ref,
    x1, x0, g, gain1, gain0, wi1, wi0, wo1, xg1, sems,
):
    place = place_ref[0]
    upper, lower = 1 - place, place
    copies = [
        (gains.at[0, pl.ds(upper, 1)], gain1),
        (w_in.at[0, upper], wi1),
        (saved.at[0, upper], x1),
        (w_out.at[0, upper], wo1),
        (top.at[upper], g),
        (gains.at[0, pl.ds(lower, 1)], gain0),
        (w_in.at[0, lower], wi0),
        (saved.at[0, lower], x0),
    ]
    copies = [pltpu.make_async_copy(a, b, sems.at[i]) for i, (a, b) in enumerate(copies)]
    for copy in copies:
        copy.start()
    width = x1.shape[1]
    rank = wi1.shape[0]
    step = share
    for copy in copies[0:3]:
        copy.wait()
    scale1, raw1 = project(x1, gain1, wi1, xg1, step)
    for copy in copies[3:5]:
        copy.wait()
    delta = jnp.zeros(raw1.shape, F32)
    for c in range(0, width, step):
        delta += nt(wo1[:, c : c + step], g[:, c : c + step])
    row1 = as_row(scale1)
    pre1 = raw1 * row1
    sig, slope = silu_slope(pre1)
    act1 = (pre1 * sig).astype(BF16)
    da1 = (delta * slope).astype(BF16)
    da1f = da1.astype(F32)
    inner = jnp.sum(da1f * pre1, axis=0, keepdims=True) * (1.0 / width)
    das1 = (da1f * row1).astype(BF16)
    pull = jnp.transpose(jnp.broadcast_to(inner * row1 * row1, (x1.shape[0],) * 2))[:, 0:1]
    for copy in copies[5:8]:
        copy.wait()
    scale0, raw0 = project(x0, gain0, wi0, xg0_ref, step)
    row0 = as_row(scale0)
    pre0 = raw0 * row0
    sig0, slope0 = silu_slope(pre0)
    low_ref[0] = (pre0 * sig0).astype(BF16).astype(F32)
    low_ref[1] = slope0
    low_ref[2] = jnp.broadcast_to(row0, raw0.shape)
    for i, c in enumerate(range(0, width, step)):
        cols = slice(c, c + step)
        dn = tn(da1, wi1[:, cols]) * gain1[:, cols]
        flow = g[:, cols].astype(F32) + scale1 * dn - pull * x1[:, cols].astype(F32)
        flow_ref[:, cols] = flow.astype(BF16)
        out_ref[i, 0:rank] = nn(das1, xg1[:, cols]).astype(BF16)
        out_ref[i, rank : 2 * rank] = nn(act1, g[:, cols]).astype(BF16)


def flow_kernel(share, flow_ref, w_ref, low_ref, send_ref):
    width = flow_ref.shape[1]
    rank = w_ref.shape[0]
    delta = jnp.zeros((rank, flow_ref.shape[0]), F32)
    for c in range(0, width, share):
        delta += nt(w_ref[:, c : c + share], flow_ref[:, c : c + share])
    send_ref[0] = low_ref[0]
    send_ref[1] = delta


def lower_kernel(share, _, flow_ref, xg0_ref, low_ref, got_ref, out_ref):
    width = flow_ref.shape[1]
    rank = got_ref.shape[1]
    act0 = got_ref[0].astype(BF16)
    da0 = (got_ref[1] * low_ref[1]).astype(BF16)
    das0 = (da0.astype(F32) * low_ref[2]).astype(BF16)
    for i, c in enumerate(range(0, width, share)):
        cols = slice(c, c + share)
        out_ref[i, 0:rank] = nn(das0, xg0_ref[:, cols]).astype(BF16)
        out_ref[i, rank : 2 * rank] = nn(act0, flow_ref[:, cols]).astype(BF16)


def sum_kernel(got_ref, in_ref, out_ref):
    rank = in_ref.shape[1]
    total = got_ref[0].astype(F32)
    for i in range(1, got_ref.shape[0]):
        total += got_ref[i].astype(F32)
    in_ref[0] = total[0:rank]
    out_ref[0] = total[rank : 2 * rank]


def params():
    return pltpu.CompilerParams(vmem_limit_bytes=VMEM_BYTES)


def whole():
    return pl.BlockSpec(memory_space=pltpu.VMEM)


def pair_on_device(saved, top_grad, gains, adapter_in, adapter_out):
    place = lax.axis_index("section")
    count = lax.axis_size("dp")
    tokens, width = saved.shape[2:]
    rank = adapter_in.shape[3]
    share = width // count
    swap = [(0, 1), (1, 0)]
    adapter_in = jnp.swapaxes(adapter_in, 2, 3)
    any_space = pl.BlockSpec(memory_space=pl.ANY)
    partner_out = lax.ppermute(
        lax.dynamic_index_in_dim(adapter_out[0], place, 0, keepdims=False), "section", swap
    )
    blocks = jax.ShapeDtypeStruct((2 * count, 2 * rank, share), BF16)
    wide = jax.ShapeDtypeStruct((tokens, width), BF16)
    out, flow, xg0, low = pl.pallas_call(
        partial(upper_kernel, share),
        grid=(1,),
        in_specs=[pl.BlockSpec(memory_space=pltpu.SMEM)] + [any_space] * 5,
        out_specs=[
            pl.BlockSpec((count, 2 * rank, share), lambda i: (1, 0, 0)),
            whole(),
            whole(),
            whole(),
        ],
        out_shape=[blocks, wide, wide, jax.ShapeDtypeStruct((3, rank, tokens), F32)],
        scratch_shapes=[pltpu.VMEM((tokens, width), BF16)] * 3
        + [pltpu.VMEM((1, width), F32)] * 2
        + [pltpu.VMEM((rank, width), BF16)] * 3
        + [pltpu.VMEM((tokens, width), BF16), pltpu.SemaphoreType.DMA((8,))],
        compiler_params=params(),
        cost_estimate=pl.CostEstimate(
            flops=12 * tokens * width * rank, bytes_accessed=12 * tokens * width, transcendentals=0
        ),
        name="upper",
    )(place.astype(jnp.int32)[None], saved, top_grad, gains, adapter_in, adapter_out)
    send = pl.pallas_call(
        partial(flow_kernel, share),
        in_specs=[whole()] * 3,
        out_specs=whole(),
        out_shape=jax.ShapeDtypeStruct((2, rank, tokens), F32),
        compiler_params=params(),
        name="flow",
    )(flow, partner_out, low)
    got = lax.ppermute(send, "section", swap)
    out = pl.pallas_call(
        partial(lower_kernel, share),
        grid=(1,),
        in_specs=[any_space] + [whole()] * 4,
        out_specs=pl.BlockSpec((count, 2 * rank, share), lambda i: (0, 0, 0)),
        out_shape=blocks,
        input_output_aliases={0: 0},
        compiler_params=params(),
        name="lower",
    )(out, flow, xg0, low, got)
    got = lax.all_to_all(out, ("section", "dp"), 0, 0, tiled=True)
    total_in, total_out = pl.pallas_call(
        sum_kernel,
        in_specs=[whole()],
        out_specs=[whole()] * 2,
        out_shape=[jax.ShapeDtypeStruct((1, rank, share), F32)] * 2,
        compiler_params=params(),
        name="total",
    )(got)
    return (jnp.swapaxes(total_in, 1, 2), total_out)


def section_back(x, gain, weight_in, weight_out, upstream):
    xf = x.astype(F32)
    scale = lax.rsqrt(jnp.mean(xf * xf, axis=-1, keepdims=True) + EPS)
    normed = xf * scale
    hidden = (normed * gain).astype(BF16)
    pre = jnp.dot(hidden, weight_in, preferred_element_type=F32)
    sig, slope = silu_slope(pre)
    active = (pre * sig).astype(BF16)
    delta_act = jnp.dot(upstream, weight_out.T, preferred_element_type=F32)
    delta_pre = (delta_act * slope).astype(BF16)
    delta_norm = jnp.dot(delta_pre, weight_in.T, preferred_element_type=F32) * gain
    inner = jnp.mean(delta_norm * normed, axis=-1, keepdims=True)
    result = (upstream.astype(F32) + scale * (delta_norm - normed * inner)).astype(BF16)
    term_in = jnp.dot(hidden.T, delta_pre, preferred_element_type=F32)
    term_out = jnp.dot(active.T, upstream, preferred_element_type=F32)
    return (result, term_in, term_out)


def relay_on_device(saved, top_grad, gains, adapter_in, adapter_out):
    sections = lax.axis_size("section")
    place = lax.axis_index("section")
    width = top_grad.shape[2]
    rank = adapter_in.shape[3]
    zero_in = jnp.zeros((width, rank), F32)
    zero_out = jnp.zeros((rank, width), F32)

    def step(turn, flows, sums):
        leaving, added = [], []
        for replica in (0, 1):
            serves = place == (sections - 1 - turn if replica == 0 else turn)
            result, term_in, term_out = lax.cond(
                serves,
                partial(
                    section_back,
                    saved[0, replica],
                    gains[0, replica],
                    adapter_in[0, replica],
                    adapter_out[0, replica],
                ),
                lambda flow: (flow, zero_in, zero_out),
                flows[replica],
            )
            leaving.append(result)
            added += [sums[2 * replica] + term_in, sums[2 * replica + 1] + term_out]
        return leaving, added

    down = [(i, i - 1) for i in range(1, sections)]
    up = [(i, i + 1) for i in range(sections - 1)]

    def turn_and_pass(turn, carry):
        leaving, sums = step(turn, carry[0], carry[1])
        return (
            [lax.ppermute(leaving[0], "section", down), lax.ppermute(leaving[1], "section", up)],
            sums,
        )

    start = ([top_grad[0], top_grad[1]], [zero_in, zero_out, zero_in, zero_out])
    flows, sums = lax.fori_loop(0, sections - 1, turn_and_pass, start)
    _, sums = step(sections - 1, flows, sums)
    shares = [
        lax.psum_scatter(term, "dp", scatter_dimension=i % 2, tiled=True)
        for i, term in enumerate(sums)
    ]
    mirror = [(i, sections - 1 - i) for i in range(sections)]
    total_in = shares[0] + lax.ppermute(shares[2], "section", mirror)
    total_out = shares[1] + lax.ppermute(shares[3], "section", mirror)
    return (total_in[None], total_out[None])


def solution(mesh):
    in_specs = (
        P("section", None, "dp", None),
        P(None, "dp", None),
        P("section", None, None),
        P("section", None, None, None),
        P("section", None, None, None),
    )
    out_specs = (P("section", "dp", None), P("section", None, "dp"))

    def run(saved, *others):
        share = saved.shape[3] // mesh.shape["dp"]
        pair = mesh.shape["section"] == 2 and share % 128 == 0
        on_device = pair_on_device if pair else relay_on_device
        return jax.shard_map(
            on_device, mesh=mesh, in_specs=in_specs, out_specs=out_specs, check_vma=False
        )(saved, *others)

    return run
```

```python
from functools import partial

import jax
import jax.numpy as jnp
from jax import lax
from jax.experimental import pallas as pl
from jax.experimental.pallas import tpu as pltpu
from jax.sharding import PartitionSpec as P

EPS = 1e-05
VMEM_BYTES = 24 * 1024 * 1024
F32 = jnp.float32
BF16 = jnp.bfloat16


def nn(a, b):
    return lax.dot_general(a, b, (((1,), (0,)), ((), ())), preferred_element_type=F32)


def nt(a, b):
    return lax.dot_general(a, b, (((1,), (1,)), ((), ())), preferred_element_type=F32)


def tn(a, b):
    return lax.dot_general(a, b, (((0,), (0,)), ((), ())), preferred_element_type=F32)


def as_row(column):
    count = column.shape[0]
    return jnp.transpose(jnp.broadcast_to(column, (count, count)))[0:1, :]


def silu_slope(pre):
    sig = jax.nn.sigmoid(pre)
    return sig, sig * (1.0 + pre * (1.0 - sig))


def project(x_ref, gain_ref, w_ref, xg_ref, step):
    tokens, width = x_ref.shape
    squares = jnp.zeros((tokens, 128), F32)
    pre = jnp.zeros((w_ref.shape[0], tokens), F32)
    for c in range(0, width, step):
        x = x_ref[:, c : c + step].astype(F32)
        for k in range(0, step, 128):
            part = x[:, k : k + 128]
            squares += part * part
        xg = (x * gain_ref[:, c : c + step]).astype(BF16)
        xg_ref[:, c : c + step] = xg
        pre += nt(w_ref[:, c : c + step], xg)
    mean = jnp.sum(squares, axis=1, keepdims=True) * (1.0 / width)
    scale = lax.rsqrt(mean + EPS)
    return scale, pre


def split_terms(share, index, das, xg_ref, act, flow_ref, keep_ref, send_ref):
    rank = das.shape[0]
    core = index % 2
    for i in range(keep_ref.shape[0]):
        for to_ref, number in ((keep_ref, core), (send_ref, 1 - core)):
            cols = pl.ds(pl.multiple_of((2 * i + number) * share, share), share)
            to_ref[i, 0:rank] = nn(das, xg_ref[:, cols]).astype(BF16)
            to_ref[i, rank : 2 * rank] = nn(act, flow_ref[:, cols]).astype(BF16)


def upper_kernel(
    share, place_ref, index_ref, saved, top, gains, w_in, w_out,
    keep_ref, send_ref, flow_ref, xg0_ref, low_ref,
    x1, x0, g, gain1, gain0, wi1, wi0, wo1, xg1, sems,
):
    place = place_ref[0]
    upper, lower = 1 - place, place
    copies = [
        (gains.at[0, pl.ds(upper, 1)], gain1),
        (w_in.at[0, upper], wi1),
        (saved.at[0, upper], x1),
        (w_out.at[0, upper], wo1),
        (top.at[upper], g),
        (gains.at[0, pl.ds(lower, 1)], gain0),
        (w_in.at[0, lower], wi0),
        (saved.at[0, lower], x0),
    ]
    copies = [pltpu.make_async_copy(a, b, sems.at[i]) for i, (a, b) in enumerate(copies)]
    for copy in copies:
        copy.start()
    width = x1.shape[1]
    rank = wi1.shape[0]
    step = share
    for copy in copies[0:3]:
        copy.wait()
    scale1, raw1 = project(x1, gain1, wi1, xg1, step)
    for copy in copies[3:5]:
        copy.wait()
    delta = jnp.zeros(raw1.shape, F32)
    for c in range(0, width, step):
        delta += nt(wo1[:, c : c + step], g[:, c : c + step])
    row1 = as_row(scale1)
    pre1 = raw1 * row1
    sig, slope = silu_slope(pre1)
    act1 = (pre1 * sig).astype(BF16)
    da1 = (delta * slope).astype(BF16)
    da1f = da1.astype(F32)
    inner = jnp.sum(da1f * pre1, axis=0, keepdims=True) * (1.0 / width)
    das1 = (da1f * row1).astype(BF16)
    pull = jnp.transpose(jnp.broadcast_to(inner * row1 * row1, (x1.shape[0],) * 2))[:, 0:1]
    for copy in copies[5:8]:
        copy.wait()
    scale0, raw0 = project(x0, gain0, wi0, xg0_ref, step)
    row0 = as_row(scale0)
    pre0 = raw0 * row0
    sig0, slope0 = silu_slope(pre0)
    low_ref[0] = (pre0 * sig0).astype(BF16).astype(F32)
    low_ref[1] = slope0
    low_ref[2] = jnp.broadcast_to(row0, raw0.shape)
    for c in range(0, width, step):
        cols = slice(c, c + step)
        dn = tn(da1, wi1[:, cols]) * gain1[:, cols]
        flow = g[:, cols].astype(F32) + scale1 * dn - pull * x1[:, cols].astype(F32)
        flow_ref[:, cols] = flow.astype(BF16)
    split_terms(share, index_ref[0], das1, xg1, act1, g, keep_ref, send_ref)


def flow_kernel(share, flow_ref, w_ref, low_ref, send_ref):
    width = flow_ref.shape[1]
    rank = w_ref.shape[0]
    delta = jnp.zeros((rank, flow_ref.shape[0]), F32)
    for c in range(0, width, share):
        delta += nt(w_ref[:, c : c + share], flow_ref[:, c : c + share])
    send_ref[0] = low_ref[0]
    send_ref[1] = delta


def lower_kernel(share, index_ref, flow_ref, xg0_ref, low_ref, got_ref, keep_ref, send_ref):
    act0 = got_ref[0].astype(BF16)
    da0 = (got_ref[1] * low_ref[1]).astype(BF16)
    das0 = (da0.astype(F32) * low_ref[2]).astype(BF16)
    split_terms(share, index_ref[0], das0, xg0_ref, act0, flow_ref, keep_ref, send_ref)


def chip_kernel(keep1, got1, keep0, got0, out_ref):
    chips = keep1.shape[0]
    for i in range(chips):
        out_ref[i] = (keep0[i].astype(F32) + got0[i].astype(F32)).astype(BF16)
        out_ref[chips + i] = (keep1[i].astype(F32) + got1[i].astype(F32)).astype(BF16)


def total_kernel(got, in_ref, out_ref):
    rank = in_ref.shape[1]
    total = got[0].astype(F32)
    for i in range(1, got.shape[0]):
        total += got[i].astype(F32)
    in_ref[0] = total[0:rank]
    out_ref[0] = total[rank : 2 * rank]


def params():
    return pltpu.CompilerParams(vmem_limit_bytes=VMEM_BYTES)


def whole():
    return pl.BlockSpec(memory_space=pltpu.VMEM)


def pair_on_device(saved, top_grad, gains, adapter_in, adapter_out):
    place = lax.axis_index("section")
    count = lax.axis_size("dp")
    tokens, width = saved.shape[2:]
    rank = adapter_in.shape[3]
    share = width // count
    swap = [(0, 1), (1, 0)]
    adapter_in = jnp.swapaxes(adapter_in, 2, 3)
    partner_out = lax.ppermute(
        lax.dynamic_index_in_dim(adapter_out[0], place, 0, keepdims=False), "section", swap
    )
    index = lax.axis_index("dp")
    saved, top_grad, gains, adapter_in, adapter_out = [
        pltpu.with_memory_space_constraint(a, pltpu.HBM)
        for a in (saved, top_grad, gains, adapter_in, adapter_out)
    ]
    place_ref = place.astype(jnp.int32)[None]
    index_ref = index.astype(jnp.int32)[None]
    scalar = pl.BlockSpec(memory_space=pltpu.SMEM)
    chips = count // 2
    blocks = jax.ShapeDtypeStruct((chips, 2 * rank, share), BF16)
    wide = jax.ShapeDtypeStruct((tokens, width), BF16)

    def swapped(array, over_section, bits):
        pairs = [
            (s * count + d, (s ^ over_section) * count + (d ^ bits))
            for s in range(2)
            for d in range(count)
        ]
        return lax.ppermute(array, ("section", "dp"), pairs)

    keep1, send1, flow, xg0, low = pl.pallas_call(
        partial(upper_kernel, share),
        in_specs=[scalar] * 2 + [pl.BlockSpec(memory_space=pltpu.HBM)] * 5,
        out_specs=[whole()] * 5,
        out_shape=[blocks, blocks, wide, wide, jax.ShapeDtypeStruct((3, rank, tokens), F32)],
        scratch_shapes=[pltpu.VMEM((tokens, width), BF16)] * 3
        + [pltpu.VMEM((1, width), F32)] * 2
        + [pltpu.VMEM((rank, width), BF16)] * 3
        + [pltpu.VMEM((tokens, width), BF16), pltpu.SemaphoreType.DMA((8,))],
        compiler_params=params(),
        cost_estimate=pl.CostEstimate(
            flops=12 * tokens * width * rank, bytes_accessed=12 * tokens * width, transcendentals=0
        ),
        name="upper",
    )(place_ref, index_ref, saved, top_grad, gains, adapter_in, adapter_out)
    got1 = swapped(send1, 0, 1)
    send = pl.pallas_call(
        partial(flow_kernel, share),
        in_specs=[whole()] * 3,
        out_specs=whole(),
        out_shape=jax.ShapeDtypeStruct((2, rank, tokens), F32),
        compiler_params=params(),
        name="flow",
    )(flow, partner_out, low)
    got = lax.ppermute(send, "section", swap)
    keep0, send0 = pl.pallas_call(
        partial(lower_kernel, share),
        in_specs=[scalar] + [whole()] * 4,
        out_specs=[whole()] * 2,
        out_shape=[blocks] * 2,
        compiler_params=params(),
        name="lower",
    )(index_ref, flow, xg0, low, got)
    got0 = swapped(send0, 0, 1)
    sums = pl.pallas_call(
        chip_kernel,
        in_specs=[whole()] * 4,
        out_specs=whole(),
        out_shape=jax.ShapeDtypeStruct((2 * chips, 2 * rank, share), BF16),
        compiler_params=params(),
        name="chip",
    )(keep1, got1, keep0, got0)
    groups = [[s * count + 2 * i + core for s in range(2) for i in range(chips)] for core in range(2)]
    sums = lax.all_to_all(
        sums, ("section", "dp"), 0, 0, axis_index_groups=groups, tiled=True
    )
    total_in, total_out = pl.pallas_call(
        total_kernel,
        in_specs=[whole()],
        out_specs=[whole()] * 2,
        out_shape=[jax.ShapeDtypeStruct((1, rank, share), F32)] * 2,
        compiler_params=params(),
        name="total",
    )(sums)
    return (jnp.swapaxes(total_in, 1, 2), total_out)


def section_back(x, gain, weight_in, weight_out, upstream):
    xf = x.astype(F32)
    scale = lax.rsqrt(jnp.mean(xf * xf, axis=-1, keepdims=True) + EPS)
    normed = xf * scale
    hidden = (normed * gain).astype(BF16)
    pre = jnp.dot(hidden, weight_in, preferred_element_type=F32)
    sig, slope = silu_slope(pre)
    active = (pre * sig).astype(BF16)
    delta_act = jnp.dot(upstream, weight_out.T, preferred_element_type=F32)
    delta_pre = (delta_act * slope).astype(BF16)
    delta_norm = jnp.dot(delta_pre, weight_in.T, preferred_element_type=F32) * gain
    inner = jnp.mean(delta_norm * normed, axis=-1, keepdims=True)
    result = (upstream.astype(F32) + scale * (delta_norm - normed * inner)).astype(BF16)
    term_in = jnp.dot(hidden.T, delta_pre, preferred_element_type=F32)
    term_out = jnp.dot(active.T, upstream, preferred_element_type=F32)
    return (result, term_in, term_out)


def relay_on_device(saved, top_grad, gains, adapter_in, adapter_out):
    sections = lax.axis_size("section")
    place = lax.axis_index("section")
    width = top_grad.shape[2]
    rank = adapter_in.shape[3]
    zero_in = jnp.zeros((width, rank), F32)
    zero_out = jnp.zeros((rank, width), F32)

    def step(turn, flows, sums):
        leaving, added = [], []
        for replica in (0, 1):
            serves = place == (sections - 1 - turn if replica == 0 else turn)
            result, term_in, term_out = lax.cond(
                serves,
                partial(
                    section_back,
                    saved[0, replica],
                    gains[0, replica],
                    adapter_in[0, replica],
                    adapter_out[0, replica],
                ),
                lambda flow: (flow, zero_in, zero_out),
                flows[replica],
            )
            leaving.append(result)
            added += [sums[2 * replica] + term_in, sums[2 * replica + 1] + term_out]
        return leaving, added

    down = [(i, i - 1) for i in range(1, sections)]
    up = [(i, i + 1) for i in range(sections - 1)]

    def turn_and_pass(turn, carry):
        leaving, sums = step(turn, carry[0], carry[1])
        return (
            [lax.ppermute(leaving[0], "section", down), lax.ppermute(leaving[1], "section", up)],
            sums,
        )

    start = ([top_grad[0], top_grad[1]], [zero_in, zero_out, zero_in, zero_out])
    flows, sums = lax.fori_loop(0, sections - 1, turn_and_pass, start)
    _, sums = step(sections - 1, flows, sums)
    shares = [
        lax.psum_scatter(term, "dp", scatter_dimension=i % 2, tiled=True)
        for i, term in enumerate(sums)
    ]
    mirror = [(i, sections - 1 - i) for i in range(sections)]
    total_in = shares[0] + lax.ppermute(shares[2], "section", mirror)
    total_out = shares[1] + lax.ppermute(shares[3], "section", mirror)
    return (total_in[None], total_out[None])


def solution(mesh):
    in_specs = (
        P("section", None, "dp", None),
        P(None, "dp", None),
        P("section", None, None),
        P("section", None, None, None),
        P("section", None, None, None),
    )
    out_specs = (P("section", "dp", None), P("section", None, "dp"))

    def run(saved, *others):
        share = saved.shape[3] // mesh.shape["dp"]
        count = mesh.shape["dp"]
        pair = mesh.shape["section"] == 2 and share % 128 == 0
        pair = pair and count % 2 == 0
        on_device = pair_on_device if pair else relay_on_device
        return jax.shard_map(
            on_device, mesh=mesh, in_specs=in_specs, out_specs=out_specs, check_vma=False
        )(saved, *others)

    return run
```

```python
from functools import partial

import jax
import jax.numpy as jnp
from jax import lax
from jax.experimental import pallas as pl
from jax.experimental.pallas import tpu as pltpu
from jax.sharding import PartitionSpec as P

EPS = 1e-05
VMEM_BYTES = 24 * 1024 * 1024
F32 = jnp.float32
BF16 = jnp.bfloat16


def nn(a, b):
    return lax.dot_general(a, b, (((1,), (0,)), ((), ())), preferred_element_type=F32)


def nt(a, b):
    return lax.dot_general(a, b, (((1,), (1,)), ((), ())), preferred_element_type=F32)


def tn(a, b):
    return lax.dot_general(a, b, (((0,), (0,)), ((), ())), preferred_element_type=F32)


def as_row(column):
    count = column.shape[0]
    return jnp.transpose(jnp.broadcast_to(column, (count, count)))[0:1, :]


def silu_slope(pre):
    sig = jax.nn.sigmoid(pre)
    return sig, sig * (1.0 + pre * (1.0 - sig))


def project(x_ref, gain_ref, w_ref, xg_ref, step):
    tokens, width = x_ref.shape
    squares = jnp.zeros((tokens, 128), F32)
    pre = jnp.zeros((w_ref.shape[0], tokens), F32)
    for c in range(0, width, step):
        x = x_ref[:, c : c + step].astype(F32)
        for k in range(0, step, 128):
            part = x[:, k : k + 128]
            squares += part * part
        xg = (x * gain_ref[:, c : c + step]).astype(BF16)
        xg_ref[:, c : c + step] = xg
        pre += nt(w_ref[:, c : c + step], xg)
    mean = jnp.sum(squares, axis=1, keepdims=True) * (1.0 / width)
    scale = lax.rsqrt(mean + EPS)
    return scale, pre


def fill(index, matrix, wide_ref, keep_ref, send_ref, first):
    count, _, share = keep_ref.shape[0] // 2, *keep_ref.shape[1:]
    core = index % 2
    for i in range(count):
        for to_ref, number in ((keep_ref, core), (send_ref, 1 - core)):
            cols = pl.ds(pl.multiple_of((2 * i + number) * share, share), share)
            to_ref[first + i] = nn(matrix, wide_ref[:, cols]).astype(BF16)


def start_all(sems, *pairs):
    copies = [pltpu.make_async_copy(a, b, sems.at[i]) for i, (a, b) in enumerate(pairs)]
    for copy in copies:
        copy.start()
    return copies


def front_kernel(step, place_ref, saved, gains, w_in, act_ref, low_ref, xg_ref, x, gain, wi, sems):
    lower = place_ref[0]
    copies = start_all(
        sems,
        (gains.at[0, pl.ds(lower, 1)], gain),
        (w_in.at[0, lower], wi),
        (saved.at[0, lower], x),
    )
    for copy in copies:
        copy.wait()
    scale, raw = project(x, gain, wi, xg_ref, step)
    row = as_row(scale)
    pre = raw * row
    sig, slope = silu_slope(pre)
    act_ref[...] = (pre * sig).astype(BF16)
    low_ref[0] = slope
    low_ref[1] = jnp.broadcast_to(row, raw.shape)


def upper_kernel(
    step, place_ref, saved, top, gains, w_in, w_out,
    flow_ref, xg_ref, das_ref, act_ref,
    x, g, gain, wi, wo, sems,
):
    upper = 1 - place_ref[0]
    copies = start_all(
        sems,
        (gains.at[0, pl.ds(upper, 1)], gain),
        (w_in.at[0, upper], wi),
        (saved.at[0, upper], x),
        (w_out.at[0, upper], wo),
        (top.at[upper], g),
    )
    width = x.shape[1]
    for copy in copies[0:3]:
        copy.wait()
    scale, raw = project(x, gain, wi, xg_ref, step)
    for copy in copies[3:5]:
        copy.wait()
    delta = jnp.zeros(raw.shape, F32)
    for c in range(0, width, step):
        delta += nt(wo[:, c : c + step], g[:, c : c + step])
    row = as_row(scale)
    pre = raw * row
    sig, slope = silu_slope(pre)
    da = (delta * slope).astype(BF16)
    daf = da.astype(F32)
    inner = jnp.sum(daf * pre, axis=0, keepdims=True) * (1.0 / width)
    act_ref[...] = (pre * sig).astype(BF16)
    das_ref[...] = (daf * row).astype(BF16)
    pull = jnp.transpose(jnp.broadcast_to(inner * row * row, (x.shape[0],) * 2))[:, 0:1]
    for c in range(0, width, step):
        cols = slice(c, c + step)
        dn = tn(da, wi[:, cols]) * gain[:, cols]
        flow = g[:, cols].astype(F32) + scale * dn - pull * x[:, cols].astype(F32)
        flow_ref[:, cols] = flow.astype(BF16)


def terms_kernel(
    place_ref, index_ref, flow_ref, xg1_ref, das1_ref, act1_ref, act0_ref, top,
    keep_out, send_out, keep_in, send_in,
    g, sems,
):
    index = index_ref[0]
    copy = pltpu.make_async_copy(top.at[1 - place_ref[0]], g, sems.at[0])
    copy.start()
    fill(index, act0_ref[...], flow_ref, keep_out, send_out, 0)
    chips = keep_out.shape[0] // 2
    copy.wait()
    fill(index, act1_ref[...], g, keep_out, send_out, chips)
    core = index % 2
    share = keep_in.shape[2]
    for i in range(chips):
        for to_ref, number in ((keep_in, core), (send_in, 1 - core)):
            cols = pl.ds(pl.multiple_of((2 * i + number) * share, share), share)
            to_ref[i] = nn(das1_ref[...], xg1_ref[:, cols]).astype(BF16)


def flow_kernel(step, flow_ref, w_ref, send_ref):
    width = flow_ref.shape[1]
    delta = jnp.zeros(send_ref.shape, F32)
    for c in range(0, width, step):
        delta += nt(w_ref[:, c : c + step], flow_ref[:, c : c + step])
    send_ref[...] = delta


def lower_kernel(index_ref, xg0_ref, low_ref, got_ref, keep1, send1, keep_ref, send_ref):
    da = (got_ref[...] * low_ref[0]).astype(BF16)
    das = (da.astype(F32) * low_ref[1]).astype(BF16)
    fill(index_ref[0], das, xg0_ref, keep_ref, send_ref, 0)
    chips = keep1.shape[0]
    keep_ref[chips : 2 * chips] = keep1[...]
    send_ref[chips : 2 * chips] = send1[...]


def halves_kernel(place_ref, keep, got, own_ref, send_ref):
    half = own_ref.shape[2]
    first = place_ref[0] == 0
    for i in range(keep.shape[0]):
        total = (keep[i].astype(F32) + got[i].astype(F32)).astype(BF16)
        left, right = total[:, 0:half], total[:, half : 2 * half]
        own_ref[i] = jnp.where(first, left, right)
        send_ref[i] = jnp.where(first, right, left)


def gather_kernel(keep, got, own, partner, out_ref):
    rank, half = own.shape[1:]
    for i in range(keep.shape[0]):
        total = (keep[i].astype(F32) + got[i].astype(F32)).astype(BF16)
        out_ref[i, 0:rank] = total[:, 0:half]
        out_ref[i, rank : 2 * rank] = total[:, half : 2 * half]
        out_ref[i, 2 * rank : 3 * rank] = (own[i].astype(F32) + partner[i].astype(F32)).astype(BF16)


def total_kernel(got, in_ref, out_ref):
    rank = in_ref.shape[1]
    half = in_ref.shape[2] // 2
    count = got.shape[0]

    def summed(numbers, first):
        return sum(got[i, first : first + rank].astype(F32) for i in numbers)

    in_ref[0, :, 0:half] = summed(range(count), 0)
    in_ref[0, :, half : 2 * half] = summed(range(count), rank)
    out_ref[0, :, 0:half] = summed(range(count // 2), 2 * rank)
    out_ref[0, :, half : 2 * half] = summed(range(count // 2, count), 2 * rank)


def params():
    return pltpu.CompilerParams(vmem_limit_bytes=VMEM_BYTES)


def whole():
    return pl.BlockSpec(memory_space=pltpu.VMEM)


def local(kernel, name, out_shapes, *operands, scratch=()):
    spaces = {"scalar": pltpu.SMEM, "far": pltpu.HBM, "near": pltpu.VMEM}
    out = pl.pallas_call(
        kernel,
        in_specs=[pl.BlockSpec(memory_space=spaces[kind]) for kind, _ in operands],
        out_specs=[pl.BlockSpec(memory_space=pltpu.VMEM)] * len(out_shapes),
        out_shape=[jax.ShapeDtypeStruct(shape, dtype) for shape, dtype in out_shapes],
        scratch_shapes=list(scratch),
        compiler_params=pltpu.CompilerParams(vmem_limit_bytes=VMEM_BYTES),
        name=name,
    )(*[array for _, array in operands])
    return out if len(out) > 1 else out[0]


def near(*arrays):
    return [("near", array) for array in arrays]


def pair_on_device(saved, top_grad, gains, adapter_in, adapter_out):
    count = lax.axis_size("dp")
    tokens, width = saved.shape[2:]
    rank = adapter_in.shape[3]
    share = width // count
    half = share // 2
    chips = count // 2
    place = ("scalar", lax.axis_index("section").astype(jnp.int32)[None])
    index = ("scalar", lax.axis_index("dp").astype(jnp.int32)[None])
    saved, top, gains, w_in, w_out = [
        ("far", pltpu.with_memory_space_constraint(a, pltpu.HBM))
        for a in (saved, top_grad, gains, jnp.swapaxes(adapter_in, 2, 3), adapter_out)
    ]

    def swapped(array, over_section, bits):
        pairs = [
            (s * count + d, (s ^ over_section) * count + (d ^ bits))
            for s in range(2)
            for d in range(count)
        ]
        return lax.ppermute(array, ("section", "dp"), pairs)

    wide = pltpu.VMEM((tokens, width), BF16)
    thin = pltpu.VMEM((rank, width), BF16)
    gain = pltpu.VMEM((1, width), F32)
    sems = pltpu.SemaphoreType.DMA
    wide_out = ((tokens, width), BF16)
    thin_out = ((rank, tokens), BF16)

    mine = lax.dynamic_index_in_dim(
        adapter_out[0], lax.axis_index("section"), 0, keepdims=False
    )
    partner_out = swapped(mine, 1, 0)
    act0, low, xg0 = local(
        partial(front_kernel, share), "front",
        [thin_out, ((2, rank, tokens), F32), wide_out],
        place, saved, gains, w_in, scratch=[wide, gain, thin, sems((3,))],
    )
    partner_act0 = swapped(act0, 1, 0)
    flow, xg1, das1, act1 = local(
        partial(upper_kernel, share), "upper",
        [wide_out, wide_out, thin_out, thin_out],
        place, saved, top, gains, w_in, w_out,
        scratch=[wide, wide, gain, thin, thin, sems((5,))],
    )
    both = ((2 * chips, rank, share), BF16)
    one = ((chips, rank, share), BF16)
    core = lax.axis_index("dp") % 2

    def parts(m, w):
        t = nn(m, w).astype(BF16).reshape(rank, chips, 2, share).transpose(2, 1, 0, 3)
        k = lax.dynamic_index_in_dim(t, core, 0, keepdims=False)
        return k, lax.dynamic_index_in_dim(t, 1 - core, 0, keepdims=False)

    k0, s0 = parts(partner_act0, flow)
    g1 = lax.dynamic_index_in_dim(top_grad, 1 - lax.axis_index("section"), 0, keepdims=False)
    k1, s1 = parts(act1, g1)
    keep1, send1 = parts(das1, xg1)
    keep_out = jnp.concatenate([k0, k1])
    send_out = jnp.concatenate([s0, s1])
    got_out = swapped(send_out, 0, 1)
    delta = nt(partner_out, flow)
    partner_delta = swapped(delta, 1, 0)
    halves = ((2 * chips, rank, half), BF16)
    total_out = (keep_out.astype(F32) + got_out.astype(F32)).astype(BF16)
    first = lax.axis_index("section") == 0
    left, right = total_out[:, :, 0:half], total_out[:, :, half:]
    own_half = jnp.where(first, left, right)
    send_half = jnp.where(first, right, left)
    partner_half = swapped(send_half, 1, 0)
    da = (partner_delta * low[0]).astype(BF16)
    das = (da.astype(F32) * low[1]).astype(BF16)
    t0 = nn(das, xg0).astype(BF16).reshape(rank, chips, 2, share).transpose(2, 1, 0, 3)
    core = lax.axis_index("dp") % 2
    k0 = lax.dynamic_index_in_dim(t0, core, 0, keepdims=False)
    s0 = lax.dynamic_index_in_dim(t0, 1 - core, 0, keepdims=False)
    keep_in = jnp.concatenate([k0, keep1])
    send_in = jnp.concatenate([s0, send1])
    got_in = swapped(send_in, 0, 1)
    total_in = (keep_in.astype(F32) + got_in.astype(F32)).astype(BF16)
    sums = jnp.concatenate(
        [
            total_in[:, :, 0:half],
            total_in[:, :, half:],
            (own_half.astype(F32) + partner_half.astype(F32)).astype(BF16),
        ],
        1,
    )
    groups = [
        [s * count + 2 * i + core for s in range(2) for i in range(chips)] for core in range(2)
    ]
    sums = lax.all_to_all(sums, ("section", "dp"), 0, 0, axis_index_groups=groups, tiled=True)
    sums = sums.astype(F32)
    total_in = jnp.concatenate([sums[:, 0:rank].sum(0), sums[:, rank:2*rank].sum(0)], 1)[None]
    total_out = jnp.concatenate([sums[:chips, 2*rank:].sum(0), sums[chips:, 2*rank:].sum(0)], 1)[None]
    return (jnp.swapaxes(total_in, 1, 2), total_out)


def section_back(x, gain, weight_in, weight_out, upstream):
    xf = x.astype(F32)
    scale = lax.rsqrt(jnp.mean(xf * xf, axis=-1, keepdims=True) + EPS)
    normed = xf * scale
    hidden = (normed * gain).astype(BF16)
    pre = jnp.dot(hidden, weight_in, preferred_element_type=F32)
    sig, slope = silu_slope(pre)
    active = (pre * sig).astype(BF16)
    delta_act = jnp.dot(upstream, weight_out.T, preferred_element_type=F32)
    delta_pre = (delta_act * slope).astype(BF16)
    delta_norm = jnp.dot(delta_pre, weight_in.T, preferred_element_type=F32) * gain
    inner = jnp.mean(delta_norm * normed, axis=-1, keepdims=True)
    result = (upstream.astype(F32) + scale * (delta_norm - normed * inner)).astype(BF16)
    term_in = jnp.dot(hidden.T, delta_pre, preferred_element_type=F32)
    term_out = jnp.dot(active.T, upstream, preferred_element_type=F32)
    return (result, term_in, term_out)


def relay_on_device(saved, top_grad, gains, adapter_in, adapter_out):
    sections = lax.axis_size("section")
    place = lax.axis_index("section")
    width = top_grad.shape[2]
    rank = adapter_in.shape[3]
    zero_in = jnp.zeros((width, rank), F32)
    zero_out = jnp.zeros((rank, width), F32)

    def step(turn, flows, sums):
        leaving, added = [], []
        for replica in (0, 1):
            serves = place == (sections - 1 - turn if replica == 0 else turn)
            result, term_in, term_out = lax.cond(
                serves,
                partial(
                    section_back,
                    saved[0, replica],
                    gains[0, replica],
                    adapter_in[0, replica],
                    adapter_out[0, replica],
                ),
                lambda flow: (flow, zero_in, zero_out),
                flows[replica],
            )
            leaving.append(result)
            added += [sums[2 * replica] + term_in, sums[2 * replica + 1] + term_out]
        return leaving, added

    down = [(i, i - 1) for i in range(1, sections)]
    up = [(i, i + 1) for i in range(sections - 1)]

    def turn_and_pass(turn, carry):
        leaving, sums = step(turn, carry[0], carry[1])
        return (
            [lax.ppermute(leaving[0], "section", down), lax.ppermute(leaving[1], "section", up)],
            sums,
        )

    start = ([top_grad[0], top_grad[1]], [zero_in, zero_out, zero_in, zero_out])
    flows, sums = lax.fori_loop(0, sections - 1, turn_and_pass, start)
    _, sums = step(sections - 1, flows, sums)
    shares = [
        lax.psum_scatter(term, "dp", scatter_dimension=i % 2, tiled=True)
        for i, term in enumerate(sums)
    ]
    mirror = [(i, sections - 1 - i) for i in range(sections)]
    total_in = shares[0] + lax.ppermute(shares[2], "section", mirror)
    total_out = shares[1] + lax.ppermute(shares[3], "section", mirror)
    return (total_in[None], total_out[None])


def solution(mesh):
    in_specs = (
        P("section", None, "dp", None),
        P(None, "dp", None),
        P("section", None, None),
        P("section", None, None, None),
        P("section", None, None, None),
    )
    out_specs = (P("section", "dp", None), P("section", None, "dp"))

    def run(saved, *others):
        share = saved.shape[3] // mesh.shape["dp"]
        count = mesh.shape["dp"]
        pair = mesh.shape["section"] == 2 and share % 256 == 0
        pair = pair and count % 2 == 0
        on_device = pair_on_device if pair else relay_on_device
        return jax.shard_map(
            on_device, mesh=mesh, in_specs=in_specs, out_specs=out_specs, check_vma=False
        )(saved, *others)

    return run
```

```python
from functools import partial

import jax
import jax.numpy as jnp
from jax import lax
from jax.experimental import pallas as pl
from jax.experimental.pallas import tpu as pltpu
from jax.sharding import PartitionSpec as P

EPS = 1e-05
VMEM_BYTES = 24 * 1024 * 1024
F32 = jnp.float32
BF16 = jnp.bfloat16


def nn(a, b):
    return lax.dot_general(a, b, (((1,), (0,)), ((), ())), preferred_element_type=F32)


def nt(a, b):
    return lax.dot_general(a, b, (((1,), (1,)), ((), ())), preferred_element_type=F32)


def tn(a, b):
    return lax.dot_general(a, b, (((0,), (0,)), ((), ())), preferred_element_type=F32)


def as_row(column):
    count = column.shape[0]
    return jnp.transpose(jnp.broadcast_to(column, (count, count)))[0:1, :]


def silu_slope(pre):
    sig = jax.nn.sigmoid(pre)
    return sig, sig * (1.0 + pre * (1.0 - sig))


def project(x_ref, gain_ref, w_ref, xg_ref, step):
    tokens, width = x_ref.shape
    squares = jnp.zeros((tokens, 128), F32)
    pre = jnp.zeros((w_ref.shape[0], tokens), F32)
    for c in range(0, width, step):
        x = x_ref[:, c : c + step].astype(F32)
        for k in range(0, step, 128):
            part = x[:, k : k + 128]
            squares += part * part
        xg = (x * gain_ref[:, c : c + step]).astype(BF16)
        xg_ref[:, c : c + step] = xg
        pre += nt(w_ref[:, c : c + step], xg)
    mean = jnp.sum(squares, axis=1, keepdims=True) * (1.0 / width)
    scale = lax.rsqrt(mean + EPS)
    return scale, pre


def split_terms(share, index, das, xg_ref, act, flow_ref, keep_ref, send_ref):
    rank = das.shape[0]
    core = index % 2
    for i in range(keep_ref.shape[0]):
        for to_ref, number in ((keep_ref, core), (send_ref, 1 - core)):
            cols = pl.ds(pl.multiple_of((2 * i + number) * share, share), share)
            to_ref[i, 0:rank] = nn(das, xg_ref[:, cols]).astype(BF16)
            to_ref[i, rank : 2 * rank] = nn(act, flow_ref[:, cols]).astype(BF16)


def upper_kernel(
    share, place_ref, index_ref, saved, top, gains, w_in, w_out,
    keep_ref, send_ref, flow_ref, xg0_ref, act0_ref, low_ref,
    x1, x0, g, gain1, gain0, wi1, wi0, wo1, xg1, sems,
):
    place = place_ref[0]
    upper, lower = 1 - place, place
    copies = [
        (gains.at[0, pl.ds(upper, 1)], gain1),
        (w_in.at[0, upper], wi1),
        (saved.at[0, upper], x1),
        (w_out.at[0, upper], wo1),
        (top.at[upper], g),
        (gains.at[0, pl.ds(lower, 1)], gain0),
        (w_in.at[0, lower], wi0),
        (saved.at[0, lower], x0),
    ]
    copies = [pltpu.make_async_copy(a, b, sems.at[i]) for i, (a, b) in enumerate(copies)]
    for copy in copies:
        copy.start()
    width = x1.shape[1]
    rank = wi1.shape[0]
    step = share
    for copy in copies[0:3]:
        copy.wait()
    scale1, raw1 = project(x1, gain1, wi1, xg1, step)
    for copy in copies[3:5]:
        copy.wait()
    delta = jnp.zeros(raw1.shape, F32)
    for c in range(0, width, step):
        delta += nt(wo1[:, c : c + step], g[:, c : c + step])
    row1 = as_row(scale1)
    pre1 = raw1 * row1
    sig, slope = silu_slope(pre1)
    act1 = (pre1 * sig).astype(BF16)
    da1 = (delta * slope).astype(BF16)
    da1f = da1.astype(F32)
    inner = jnp.sum(da1f * pre1, axis=0, keepdims=True) * (1.0 / width)
    das1 = (da1f * row1).astype(BF16)
    pull = jnp.transpose(jnp.broadcast_to(inner * row1 * row1, (x1.shape[0],) * 2))[:, 0:1]
    for copy in copies[5:8]:
        copy.wait()
    scale0, raw0 = project(x0, gain0, wi0, xg0_ref, step)
    row0 = as_row(scale0)
    pre0 = raw0 * row0
    sig0, slope0 = silu_slope(pre0)
    act0_ref[...] = (pre0 * sig0).astype(BF16)
    low_ref[0] = slope0
    low_ref[1] = jnp.broadcast_to(row0, raw0.shape)
    for c in range(0, width, step):
        cols = slice(c, c + step)
        dn = tn(da1, wi1[:, cols]) * gain1[:, cols]
        flow = g[:, cols].astype(F32) + scale1 * dn - pull * x1[:, cols].astype(F32)
        flow_ref[:, cols] = flow.astype(BF16)
    split_terms(share, index_ref[0], das1, xg1, act1, g, keep_ref, send_ref)


def pick_kernel(place_ref, index_ref, w_out, out_ref, sems):
    half = out_ref.shape[1]
    cols = pl.ds(pl.multiple_of((index_ref[0] % 2) * half, half), half)
    copy = pltpu.make_async_copy(w_out.at[0, place_ref[0], :, cols], out_ref, sems.at[0])
    copy.start()
    copy.wait()


def flow_kernel(share, index_ref, flow_ref, own_ref, other_ref, act0_ref, send_ref):
    half = own_ref.shape[1]
    core = index_ref[0] % 2
    delta = jnp.zeros(act0_ref.shape, F32)
    for w_ref, number in ((own_ref, core), (other_ref, 1 - core)):
        for c in range(0, half, share):
            cols = pl.ds(pl.multiple_of(number * half + c, share), share)
            delta += nt(w_ref[:, c : c + share], flow_ref[:, cols])
    send_ref[0] = act0_ref[...]
    send_ref[1] = delta.astype(BF16)


def lower_kernel(share, index_ref, flow_ref, xg0_ref, low_ref, got_ref, keep_ref, send_ref):
    da0 = (got_ref[1].astype(F32) * low_ref[0]).astype(BF16)
    das0 = (da0.astype(F32) * low_ref[1]).astype(BF16)
    split_terms(share, index_ref[0], das0, xg0_ref, got_ref[0], flow_ref, keep_ref, send_ref)


def plane_kernel(
    place_ref, index_ref, keep1, got1, keep0, got0, own_ref, first_ref, second_ref, across
):
    row = (index_ref[0] // 2) % 2

    def order(near, far, along_x, along_y):
        for i in range(own_ref.shape[0]):
            for to_ref, (keep, got), number in (
                (across, far, 1 - row),
                (along_x, far, row),
                (along_y, near, 1 - row),
                (own_ref, near, row),
            ):
                block = 2 * i + number
                to_ref[i] = (keep[block].astype(F32) + got[block].astype(F32)).astype(BF16)

    for place, near, far in (
        (1, (keep1, got1), (keep0, got0)),
        (0, (keep0, got0), (keep1, got1)),
    ):
        for core, ways in ((0, (second_ref, first_ref)), (1, (first_ref, second_ref))):
            pl.when((place_ref[0] == place) & (index_ref[0] % 2 == core))(
                partial(order, near, far, *ways)
            )


def layer_kernel(index_ref, own, got_a, got_b, got_c, *out_refs):
    layer = index_ref[0] // 4
    for k, out_ref in enumerate(out_refs):
        block = layer ^ k
        total = own[block].astype(F32) + got_a[block].astype(F32)
        total += got_b[block].astype(F32) + got_c[block].astype(F32)
        out_ref[...] = total.astype(BF16)


def total_kernel(*refs):
    *got, in_ref, out_ref = refs
    rank = in_ref.shape[1]
    total = got[0][...].astype(F32)
    for ref in got[1:]:
        total += ref[...].astype(F32)
    in_ref[0] = total[0:rank]
    out_ref[0] = total[rank : 2 * rank]


def params():
    return pltpu.CompilerParams(vmem_limit_bytes=VMEM_BYTES)


def whole():
    return pl.BlockSpec(memory_space=pltpu.VMEM)


def pair_on_device(saved, top_grad, gains, adapter_in, adapter_out):
    place = lax.axis_index("section")
    count = lax.axis_size("dp")
    tokens, width = saved.shape[2:]
    rank = adapter_in.shape[3]
    share = width // count
    adapter_in = jnp.swapaxes(adapter_in, 2, 3)
    saved, top_grad, gains, adapter_in, adapter_out = [
        pltpu.with_memory_space_constraint(a, pltpu.HBM)
        for a in (saved, top_grad, gains, adapter_in, adapter_out)
    ]
    place_ref = place.astype(jnp.int32)[None]
    index_ref = lax.axis_index("dp").astype(jnp.int32)[None]
    scalar = pl.BlockSpec(memory_space=pltpu.SMEM)
    chips, layers = count // 2, count // 4
    blocks = jax.ShapeDtypeStruct((chips, 2 * rank, share), BF16)
    fourth = jax.ShapeDtypeStruct((layers, 2 * rank, share), BF16)
    block = jax.ShapeDtypeStruct((2 * rank, share), BF16)
    wide = jax.ShapeDtypeStruct((tokens, width), BF16)

    def swapped(array, *ways):
        pairs = []
        for s in range(2):
            for d in range(count):
                over_section, bits = ways[d % len(ways)]
                pairs.append((s * count + d, (s ^ over_section) * count + (d ^ bits)))
        return lax.ppermute(array, ("section", "dp"), pairs)

    mine = pl.pallas_call(
        pick_kernel,
        in_specs=[scalar] * 2 + [pl.BlockSpec(memory_space=pltpu.HBM)],
        out_specs=whole(),
        out_shape=jax.ShapeDtypeStruct((rank, width // 2), BF16),
        scratch_shapes=[pltpu.SemaphoreType.DMA((1,))],
        compiler_params=params(),
        name="pick",
    )(place_ref, index_ref, adapter_out)
    partner_half = swapped(mine, (1, 0))
    keep1, send1, flow, xg0, act0, low = pl.pallas_call(
        partial(upper_kernel, share),
        in_specs=[scalar] * 2 + [pl.BlockSpec(memory_space=pltpu.HBM)] * 5,
        out_specs=[whole()] * 6,
        out_shape=[
            blocks, blocks, wide, wide,
            jax.ShapeDtypeStruct((rank, tokens), BF16),
            jax.ShapeDtypeStruct((2, rank, tokens), F32),
        ],
        scratch_shapes=[pltpu.VMEM((tokens, width), BF16)] * 3
        + [pltpu.VMEM((1, width), F32)] * 2
        + [pltpu.VMEM((rank, width), BF16)] * 3
        + [pltpu.VMEM((tokens, width), BF16), pltpu.SemaphoreType.DMA((8,))],
        compiler_params=params(),
        cost_estimate=pl.CostEstimate(
            flops=12 * tokens * width * rank, bytes_accessed=12 * tokens * width, transcendentals=0
        ),
        name="upper",
    )(place_ref, index_ref, saved, top_grad, gains, adapter_in, adapter_out)
    partner_half, flow = lax.optimization_barrier((partner_half, flow))
    partner_other = swapped(partner_half, (0, 1))
    got1 = swapped(send1, (0, 1))
    send = pl.pallas_call(
        partial(flow_kernel, share),
        in_specs=[scalar] + [whole()] * 4,
        out_specs=whole(),
        out_shape=jax.ShapeDtypeStruct((2, rank, tokens), BF16),
        compiler_params=params(),
        name="flow",
    )(index_ref, flow, partner_half, partner_other, act0)
    got = swapped(send, (1, 0))
    keep0, send0 = pl.pallas_call(
        partial(lower_kernel, share),
        in_specs=[scalar] + [whole()] * 4,
        out_specs=[whole()] * 2,
        out_shape=[blocks] * 2,
        compiler_params=params(),
        name="lower",
    )(index_ref, flow, xg0, low, got)
    got0 = swapped(send0, (0, 1))
    own, first, second, across = pl.pallas_call(
        plane_kernel,
        in_specs=[scalar] * 2 + [whole()] * 4,
        out_specs=[whole()] * 4,
        out_shape=[fourth] * 4,
        compiler_params=params(),
        name="plane",
    )(place_ref, index_ref, keep1, got1, keep0, got0)
    first = swapped(first, (0, 2), (1, 0))
    second = swapped(second, (1, 0), (0, 2))
    across = swapped(across, (1, 2))
    mine, *others = pl.pallas_call(
        layer_kernel,
        in_specs=[scalar] + [whole()] * 4,
        out_specs=[whole()] * layers,
        out_shape=[block] * layers,
        compiler_params=params(),
        name="layer",
    )(index_ref, own, first, second, across)
    others = [swapped(other, (0, 4 * k)) for k, other in enumerate(others, 1)]
    total_in, total_out = pl.pallas_call(
        total_kernel,
        in_specs=[whole()] * layers,
        out_specs=[whole()] * 2,
        out_shape=[jax.ShapeDtypeStruct((1, rank, share), F32)] * 2,
        compiler_params=params(),
        name="total",
    )(mine, *others[::-1])
    return (jnp.swapaxes(total_in, 1, 2), total_out)


def section_back(x, gain, weight_in, weight_out, upstream):
    xf = x.astype(F32)
    scale = lax.rsqrt(jnp.mean(xf * xf, axis=-1, keepdims=True) + EPS)
    normed = xf * scale
    hidden = (normed * gain).astype(BF16)
    pre = jnp.dot(hidden, weight_in, preferred_element_type=F32)
    sig, slope = silu_slope(pre)
    active = (pre * sig).astype(BF16)
    delta_act = jnp.dot(upstream, weight_out.T, preferred_element_type=F32)
    delta_pre = (delta_act * slope).astype(BF16)
    delta_norm = jnp.dot(delta_pre, weight_in.T, preferred_element_type=F32) * gain
    inner = jnp.mean(delta_norm * normed, axis=-1, keepdims=True)
    result = (upstream.astype(F32) + scale * (delta_norm - normed * inner)).astype(BF16)
    term_in = jnp.dot(hidden.T, delta_pre, preferred_element_type=F32)
    term_out = jnp.dot(active.T, upstream, preferred_element_type=F32)
    return (result, term_in, term_out)


def relay_on_device(saved, top_grad, gains, adapter_in, adapter_out):
    sections = lax.axis_size("section")
    place = lax.axis_index("section")
    width = top_grad.shape[2]
    rank = adapter_in.shape[3]
    zero_in = jnp.zeros((width, rank), F32)
    zero_out = jnp.zeros((rank, width), F32)

    def step(turn, flows, sums):
        leaving, added = [], []
        for replica in (0, 1):
            serves = place == (sections - 1 - turn if replica == 0 else turn)
            result, term_in, term_out = lax.cond(
                serves,
                partial(
                    section_back,
                    saved[0, replica],
                    gains[0, replica],
                    adapter_in[0, replica],
                    adapter_out[0, replica],
                ),
                lambda flow: (flow, zero_in, zero_out),
                flows[replica],
            )
            leaving.append(result)
            added += [sums[2 * replica] + term_in, sums[2 * replica + 1] + term_out]
        return leaving, added

    down = [(i, i - 1) for i in range(1, sections)]
    up = [(i, i + 1) for i in range(sections - 1)]

    def turn_and_pass(turn, carry):
        leaving, sums = step(turn, carry[0], carry[1])
        return (
            [lax.ppermute(leaving[0], "section", down), lax.ppermute(leaving[1], "section", up)],
            sums,
        )

    start = ([top_grad[0], top_grad[1]], [zero_in, zero_out, zero_in, zero_out])
    flows, sums = lax.fori_loop(0, sections - 1, turn_and_pass, start)
    _, sums = step(sections - 1, flows, sums)
    shares = [
        lax.psum_scatter(term, "dp", scatter_dimension=i % 2, tiled=True)
        for i, term in enumerate(sums)
    ]
    mirror = [(i, sections - 1 - i) for i in range(sections)]
    total_in = shares[0] + lax.ppermute(shares[2], "section", mirror)
    total_out = shares[1] + lax.ppermute(shares[3], "section", mirror)
    return (total_in[None], total_out[None])


def solution(mesh):
    in_specs = (
        P("section", None, "dp", None),
        P(None, "dp", None),
        P("section", None, None),
        P("section", None, None, None),
        P("section", None, None, None),
    )
    out_specs = (P("section", "dp", None), P("section", None, "dp"))

    def run(saved, *others):
        share = saved.shape[3] // mesh.shape["dp"]
        count = mesh.shape["dp"]
        pair = mesh.shape["section"] == 2 and share % 128 == 0
        pair = pair and count >= 4 and count & (count - 1) == 0
        on_device = pair_on_device if pair else relay_on_device
        return jax.shard_map(
            on_device, mesh=mesh, in_specs=in_specs, out_specs=out_specs, check_vma=False
        )(saved, *others)

    return run
```

```python
from functools import partial

import jax
import jax.numpy as jnp
from jax import lax
from jax.experimental import pallas as pl
from jax.experimental.pallas import tpu as pltpu
from jax.sharding import PartitionSpec as P

EPS = 1e-05
VMEM_BYTES = 24 * 1024 * 1024
F32 = jnp.float32
BF16 = jnp.bfloat16


def nn(a, b):
    return lax.dot_general(a, b, (((1,), (0,)), ((), ())), preferred_element_type=F32)


def nt(a, b):
    return lax.dot_general(a, b, (((1,), (1,)), ((), ())), preferred_element_type=F32)


def tn(a, b):
    return lax.dot_general(a, b, (((0,), (0,)), ((), ())), preferred_element_type=F32)


def as_row(column):
    count = column.shape[0]
    return jnp.transpose(jnp.broadcast_to(column, (count, count)))[0:1, :]


def silu_slope(pre):
    sig = jax.nn.sigmoid(pre)
    return sig, sig * (1.0 + pre * (1.0 - sig))


def project(x_ref, gain_ref, w_ref, xg_ref, step):
    tokens, width = x_ref.shape
    squares = jnp.zeros((tokens, 128), F32)
    pre = jnp.zeros((w_ref.shape[0], tokens), F32)
    for c in range(0, width, step):
        x = x_ref[:, c : c + step].astype(F32)
        for k in range(0, step, 128):
            part = x[:, k : k + 128]
            squares += part * part
        xg = (x * gain_ref[:, c : c + step]).astype(BF16)
        xg_ref[:, c : c + step] = xg
        pre += nt(w_ref[:, c : c + step], xg)
    mean = jnp.sum(squares, axis=1, keepdims=True) * (1.0 / width)
    scale = lax.rsqrt(mean + EPS)
    return scale, pre


def split_terms(share, index, das, xg_ref, act, flow_ref, keep_ref, send_ref):
    rank = das.shape[0]
    core = index % 2
    for i in range(keep_ref.shape[0]):
        for to_ref, number in ((keep_ref, core), (send_ref, 1 - core)):
            cols = pl.ds(pl.multiple_of((2 * i + number) * share, share), share)
            to_ref[i, 0:rank] = nn(das, xg_ref[:, cols]).astype(BF16)
            to_ref[i, rank : 2 * rank] = nn(act, flow_ref[:, cols]).astype(BF16)


def upper_kernel(
    share, place_ref, index_ref, saved, top, gains, w_in, w_out,
    keep_ref, send_ref, flow_ref, xg0_ref, act0_ref, low_ref,
    x1, x0, g, gain1, gain0, wi1, wi0, wo1, xg1, sems,
):
    place = place_ref[0]
    upper, lower = 1 - place, place
    copies = [
        (gains.at[0, pl.ds(upper, 1)], gain1),
        (w_in.at[0, upper], wi1),
        (saved.at[0, upper], x1),
        (w_out.at[0, upper], wo1),
        (top.at[upper], g),
        (gains.at[0, pl.ds(lower, 1)], gain0),
        (w_in.at[0, lower], wi0),
        (saved.at[0, lower], x0),
    ]
    copies = [pltpu.make_async_copy(a, b, sems.at[i]) for i, (a, b) in enumerate(copies)]
    for copy in copies:
        copy.start()
    width = x1.shape[1]
    rank = wi1.shape[0]
    step = share
    for copy in copies[0:3]:
        copy.wait()
    scale1, raw1 = project(x1, gain1, wi1, xg1, step)
    for copy in copies[3:5]:
        copy.wait()
    delta = jnp.zeros(raw1.shape, F32)
    for c in range(0, width, step):
        delta += nt(wo1[:, c : c + step], g[:, c : c + step])
    row1 = as_row(scale1)
    pre1 = raw1 * row1
    sig, slope = silu_slope(pre1)
    act1 = (pre1 * sig).astype(BF16)
    da1 = (delta * slope).astype(BF16)
    da1f = da1.astype(F32)
    inner = jnp.sum(da1f * pre1, axis=0, keepdims=True) * (1.0 / width)
    das1 = (da1f * row1).astype(BF16)
    pull = jnp.transpose(jnp.broadcast_to(inner * row1 * row1, (x1.shape[0],) * 2))[:, 0:1]
    for copy in copies[5:8]:
        copy.wait()
    scale0, raw0 = project(x0, gain0, wi0, xg0_ref, step)
    row0 = as_row(scale0)
    pre0 = raw0 * row0
    sig0, slope0 = silu_slope(pre0)
    act0_ref[...] = (pre0 * sig0).astype(BF16)
    low_ref[0] = slope0
    low_ref[1] = jnp.broadcast_to(row0, raw0.shape)
    for c in range(0, width, step):
        cols = slice(c, c + step)
        dn = tn(da1, wi1[:, cols]) * gain1[:, cols]
        flow = g[:, cols].astype(F32) + scale1 * dn - pull * x1[:, cols].astype(F32)
        flow_ref[:, cols] = flow.astype(BF16)
    split_terms(share, index_ref[0], das1, xg1, act1, g, keep_ref, send_ref)


def pick_kernel(place_ref, index_ref, w_out, out_ref, sems):
    half = out_ref.shape[1]
    cols = pl.ds(pl.multiple_of((index_ref[0] % 2) * half, half), half)
    copy = pltpu.make_async_copy(w_out.at[0, place_ref[0], :, cols], out_ref, sems.at[0])
    copy.start()
    copy.wait()


def flow_kernel(share, index_ref, flow_ref, own_ref, other_ref, act0_ref, send_ref):
    half = own_ref.shape[1]
    core = index_ref[0] % 2
    delta = jnp.zeros(act0_ref.shape, F32)
    for w_ref, number in ((own_ref, core), (other_ref, 1 - core)):
        for c in range(0, half, share):
            cols = pl.ds(pl.multiple_of(number * half + c, share), share)
            delta += nt(w_ref[:, c : c + share], flow_ref[:, cols])
    send_ref[0] = act0_ref[...]
    send_ref[1] = delta.astype(BF16)


def lower_kernel(
    share, index_ref, flow_ref, xg0_ref, low_ref, got_ref, keep1, got1, keep_ref, send_ref, sum_ref
):
    da0 = (got_ref[1].astype(F32) * low_ref[0]).astype(BF16)
    das0 = (da0.astype(F32) * low_ref[1]).astype(BF16)
    split_terms(share, index_ref[0], das0, xg0_ref, got_ref[0], flow_ref, keep_ref, send_ref)
    for i in range(sum_ref.shape[0]):
        sum_ref[i] = (keep1[i].astype(F32) + got1[i].astype(F32)).astype(BF16)


def plane_kernel(sum1, keep0, got0, out_ref):
    layers = out_ref.shape[1]
    for row in range(2):
        for i in range(layers):
            block = 2 * i + row
            out_ref[row, i] = (keep0[block].astype(F32) + got0[block].astype(F32)).astype(BF16)
            out_ref[2 + row, i] = sum1[block]


def layer_kernel(got, out_ref):
    for i in range(out_ref.shape[0]):
        out_ref[i] = sum(got[k, i].astype(F32) for k in range(got.shape[0])).astype(BF16)


def total_kernel(got, in_ref, out_ref):
    rank = in_ref.shape[1]
    total = sum(got[i].astype(F32) for i in range(got.shape[0]))
    in_ref[0] = total[0:rank]
    out_ref[0] = total[rank : 2 * rank]


def params():
    return pltpu.CompilerParams(vmem_limit_bytes=VMEM_BYTES)


def whole():
    return pl.BlockSpec(memory_space=pltpu.VMEM)


def pair_on_device(saved, top_grad, gains, adapter_in, adapter_out):
    place = lax.axis_index("section")
    count = lax.axis_size("dp")
    tokens, width = saved.shape[2:]
    rank = adapter_in.shape[3]
    share = width // count
    adapter_in = jnp.swapaxes(adapter_in, 2, 3)
    saved, top_grad, gains, adapter_in, adapter_out = [
        pltpu.with_memory_space_constraint(a, pltpu.HBM)
        for a in (saved, top_grad, gains, adapter_in, adapter_out)
    ]
    place_ref = place.astype(jnp.int32)[None]
    index_ref = lax.axis_index("dp").astype(jnp.int32)[None]
    scalar = pl.BlockSpec(memory_space=pltpu.SMEM)
    chips, layers = count // 2, count // 4
    blocks = jax.ShapeDtypeStruct((chips, 2 * rank, share), BF16)
    wide = jax.ShapeDtypeStruct((tokens, width), BF16)

    def swapped(array, *ways):
        pairs = []
        for s in range(2):
            for d in range(count):
                over_section, bits = ways[d % len(ways)]
                pairs.append((s * count + d, (s ^ over_section) * count + (d ^ bits)))
        return lax.ppermute(array, ("section", "dp"), pairs)

    mine = pl.pallas_call(
        pick_kernel,
        in_specs=[scalar] * 2 + [pl.BlockSpec(memory_space=pltpu.HBM)],
        out_specs=whole(),
        out_shape=jax.ShapeDtypeStruct((rank, width // 2), BF16),
        scratch_shapes=[pltpu.SemaphoreType.DMA((1,))],
        compiler_params=params(),
        name="pick",
    )(place_ref, index_ref, adapter_out)
    partner_half = swapped(mine, (1, 0))
    keep1, send1, flow, xg0, act0, low = pl.pallas_call(
        partial(upper_kernel, share),
        in_specs=[scalar] * 2 + [pl.BlockSpec(memory_space=pltpu.HBM)] * 5,
        out_specs=[whole()] * 6,
        out_shape=[
            blocks, blocks, wide, wide,
            jax.ShapeDtypeStruct((rank, tokens), BF16),
            jax.ShapeDtypeStruct((2, rank, tokens), F32),
        ],
        scratch_shapes=[pltpu.VMEM((tokens, width), BF16)] * 3
        + [pltpu.VMEM((1, width), F32)] * 2
        + [pltpu.VMEM((rank, width), BF16)] * 3
        + [pltpu.VMEM((tokens, width), BF16), pltpu.SemaphoreType.DMA((8,))],
        compiler_params=params(),
        cost_estimate=pl.CostEstimate(
            flops=12 * tokens * width * rank, bytes_accessed=12 * tokens * width, transcendentals=0
        ),
        name="upper",
    )(place_ref, index_ref, saved, top_grad, gains, adapter_in, adapter_out)
    partner_half, flow = lax.optimization_barrier((partner_half, flow))
    partner_other = swapped(partner_half, (0, 1))
    got1 = swapped(send1, (0, 1))
    send = pl.pallas_call(
        partial(flow_kernel, share),
        in_specs=[scalar] + [whole()] * 4,
        out_specs=whole(),
        out_shape=jax.ShapeDtypeStruct((2, rank, tokens), BF16),
        compiler_params=params(),
        name="flow",
    )(index_ref, flow, partner_half, partner_other, act0)
    got = swapped(send, (1, 0))
    keep0, send0, sum1 = pl.pallas_call(
        partial(lower_kernel, share),
        in_specs=[scalar] + [whole()] * 6,
        out_specs=[whole()] * 3,
        out_shape=[blocks] * 3,
        compiler_params=params(),
        name="lower",
    )(index_ref, flow, xg0, low, got, keep1, got1)
    got0 = swapped(send0, (0, 1))
    number = lambda s, z, y, core: s * count + 4 * z + 2 * y + core
    planes = [
        [number(s, z, y, core) for s in range(2) for y in range(2)]
        for z in range(layers)
        for core in range(2)
    ]
    columns = [
        [number(s, z, y, core) for z in range(layers)]
        for s in range(2)
        for y in range(2)
        for core in range(2)
    ]

    def dealt(blocks, groups):
        return lax.all_to_all(
            blocks, ("section", "dp"), 0, 0, axis_index_groups=groups, tiled=True
        )

    sums = pl.pallas_call(
        plane_kernel,
        in_specs=[whole()] * 3,
        out_specs=whole(),
        out_shape=jax.ShapeDtypeStruct((4, layers, 2 * rank, share), BF16),
        compiler_params=params(),
        name="plane",
    )(sum1, keep0, got0)
    sums = pl.pallas_call(
        layer_kernel,
        in_specs=[whole()],
        out_specs=whole(),
        out_shape=jax.ShapeDtypeStruct((layers, 2 * rank, share), BF16),
        compiler_params=params(),
        name="layer",
    )(dealt(sums, planes))
    total_in, total_out = pl.pallas_call(
        total_kernel,
        in_specs=[whole()],
        out_specs=[whole()] * 2,
        out_shape=[jax.ShapeDtypeStruct((1, rank, share), F32)] * 2,
        compiler_params=params(),
        name="total",
    )(dealt(sums, columns))
    return (jnp.swapaxes(total_in, 1, 2), total_out)


def section_back(x, gain, weight_in, weight_out, upstream):
    xf = x.astype(F32)
    scale = lax.rsqrt(jnp.mean(xf * xf, axis=-1, keepdims=True) + EPS)
    normed = xf * scale
    hidden = (normed * gain).astype(BF16)
    pre = jnp.dot(hidden, weight_in, preferred_element_type=F32)
    sig, slope = silu_slope(pre)
    active = (pre * sig).astype(BF16)
    delta_act = jnp.dot(upstream, weight_out.T, preferred_element_type=F32)
    delta_pre = (delta_act * slope).astype(BF16)
    delta_norm = jnp.dot(delta_pre, weight_in.T, preferred_element_type=F32) * gain
    inner = jnp.mean(delta_norm * normed, axis=-1, keepdims=True)
    result = (upstream.astype(F32) + scale * (delta_norm - normed * inner)).astype(BF16)
    term_in = jnp.dot(hidden.T, delta_pre, preferred_element_type=F32)
    term_out = jnp.dot(active.T, upstream, preferred_element_type=F32)
    return (result, term_in, term_out)


def relay_on_device(saved, top_grad, gains, adapter_in, adapter_out):
    sections = lax.axis_size("section")
    place = lax.axis_index("section")
    width = top_grad.shape[2]
    rank = adapter_in.shape[3]
    zero_in = jnp.zeros((width, rank), F32)
    zero_out = jnp.zeros((rank, width), F32)

    def step(turn, flows, sums):
        leaving, added = [], []
        for replica in (0, 1):
            serves = place == (sections - 1 - turn if replica == 0 else turn)
            result, term_in, term_out = lax.cond(
                serves,
                partial(
                    section_back,
                    saved[0, replica],
                    gains[0, replica],
                    adapter_in[0, replica],
                    adapter_out[0, replica],
                ),
                lambda flow: (flow, zero_in, zero_out),
                flows[replica],
            )
            leaving.append(result)
            added += [sums[2 * replica] + term_in, sums[2 * replica + 1] + term_out]
        return leaving, added

    down = [(i, i - 1) for i in range(1, sections)]
    up = [(i, i + 1) for i in range(sections - 1)]

    def turn_and_pass(turn, carry):
        leaving, sums = step(turn, carry[0], carry[1])
        return (
            [lax.ppermute(leaving[0], "section", down), lax.ppermute(leaving[1], "section", up)],
            sums,
        )

    start = ([top_grad[0], top_grad[1]], [zero_in, zero_out, zero_in, zero_out])
    flows, sums = lax.fori_loop(0, sections - 1, turn_and_pass, start)
    _, sums = step(sections - 1, flows, sums)
    shares = [
        lax.psum_scatter(term, "dp", scatter_dimension=i % 2, tiled=True)
        for i, term in enumerate(sums)
    ]
    mirror = [(i, sections - 1 - i) for i in range(sections)]
    total_in = shares[0] + lax.ppermute(shares[2], "section", mirror)
    total_out = shares[1] + lax.ppermute(shares[3], "section", mirror)
    return (total_in[None], total_out[None])


def solution(mesh):
    in_specs = (
        P("section", None, "dp", None),
        P(None, "dp", None),
        P("section", None, None),
        P("section", None, None, None),
        P("section", None, None, None),
    )
    out_specs = (P("section", "dp", None), P("section", None, "dp"))

    def run(saved, *others):
        share = saved.shape[3] // mesh.shape["dp"]
        count = mesh.shape["dp"]
        pair = mesh.shape["section"] == 2 and share % 128 == 0
        pair = pair and count >= 4 and count & (count - 1) == 0
        on_device = pair_on_device if pair else relay_on_device
        return jax.shard_map(
            on_device, mesh=mesh, in_specs=in_specs, out_specs=out_specs, check_vma=False
        )(saved, *others)

    return run
```

```python
from functools import partial

import jax
import jax.numpy as jnp
from jax import lax
from jax.experimental import pallas as pl
from jax.experimental.pallas import tpu as pltpu
from jax.sharding import PartitionSpec as P

EPS = 1e-05
VMEM_BYTES = 24 * 1024 * 1024
F32 = jnp.float32
BF16 = jnp.bfloat16


def nn(a, b):
    return lax.dot_general(a, b, (((1,), (0,)), ((), ())), preferred_element_type=F32)


def nt(a, b):
    return lax.dot_general(a, b, (((1,), (1,)), ((), ())), preferred_element_type=F32)


def tn(a, b):
    return lax.dot_general(a, b, (((0,), (0,)), ((), ())), preferred_element_type=F32)


def as_row(column):
    count = column.shape[0]
    return jnp.transpose(jnp.broadcast_to(column, (count, count)))[0:1, :]


def silu_slope(pre):
    sig = jax.nn.sigmoid(pre)
    return sig, sig * (1.0 + pre * (1.0 - sig))


def project(x_ref, gain_ref, w_ref, xg_ref, step):
    tokens, width = x_ref.shape
    squares = jnp.zeros((tokens, 128), F32)
    pre = jnp.zeros((w_ref.shape[0], tokens), F32)
    for c in range(0, width, step):
        x = x_ref[:, c : c + step].astype(F32)
        for k in range(0, step, 128):
            part = x[:, k : k + 128]
            squares += part * part
        xg = (x * gain_ref[:, c : c + step]).astype(BF16)
        xg_ref[:, c : c + step] = xg
        pre += nt(w_ref[:, c : c + step], xg)
    mean = jnp.sum(squares, axis=1, keepdims=True) * (1.0 / width)
    scale = lax.rsqrt(mean + EPS)
    return scale, pre


def split_terms(share, index, das, xg_ref, act, flow_ref, keep_ref, send_ref):
    rank = das.shape[0]
    core = index % 2
    for i in range(keep_ref.shape[0]):
        for to_ref, number in ((keep_ref, core), (send_ref, 1 - core)):
            cols = pl.ds(pl.multiple_of((2 * i + number) * share, share), share)
            to_ref[i, 0:rank] = nn(das, xg_ref[:, cols]).astype(BF16)
            to_ref[i, rank : 2 * rank] = nn(act, flow_ref[:, cols]).astype(BF16)


def upper_kernel(
    share, place_ref, index_ref, saved, top, gains, w_in, w_out,
    keep_ref, send_ref, flow_ref, xg0_ref, act0_ref, low_ref,
    x1, x0, g, gain1, gain0, wi1, wi0, wo1, xg1, sems,
):
    place = place_ref[0]
    upper, lower = 1 - place, place
    copies = [
        (gains.at[0, pl.ds(upper, 1)], gain1),
        (w_in.at[0, upper], wi1),
        (saved.at[0, upper], x1),
        (w_out.at[0, upper], wo1),
        (top.at[upper], g),
        (gains.at[0, pl.ds(lower, 1)], gain0),
        (w_in.at[0, lower], wi0),
        (saved.at[0, lower], x0),
    ]
    copies = [pltpu.make_async_copy(a, b, sems.at[i]) for i, (a, b) in enumerate(copies)]
    for copy in copies:
        copy.start()
    width = x1.shape[1]
    rank = wi1.shape[0]
    step = share
    for copy in copies[0:3]:
        copy.wait()
    scale1, raw1 = project(x1, gain1, wi1, xg1, step)
    for copy in copies[3:5]:
        copy.wait()
    delta = jnp.zeros(raw1.shape, F32)
    for c in range(0, width, step):
        delta += nt(wo1[:, c : c + step], g[:, c : c + step])
    row1 = as_row(scale1)
    pre1 = raw1 * row1
    sig, slope = silu_slope(pre1)
    act1 = (pre1 * sig).astype(BF16)
    da1 = (delta * slope).astype(BF16)
    da1f = da1.astype(F32)
    inner = jnp.sum(da1f * pre1, axis=0, keepdims=True) * (1.0 / width)
    das1 = (da1f * row1).astype(BF16)
    pull = jnp.transpose(jnp.broadcast_to(inner * row1 * row1, (x1.shape[0],) * 2))[:, 0:1]
    for copy in copies[5:8]:
        copy.wait()
    scale0, raw0 = project(x0, gain0, wi0, xg0_ref, step)
    row0 = as_row(scale0)
    pre0 = raw0 * row0
    sig0, slope0 = silu_slope(pre0)
    act0_ref[...] = (pre0 * sig0).astype(BF16)
    low_ref[0] = slope0
    low_ref[1] = jnp.broadcast_to(row0, raw0.shape)
    for c in range(0, width, step):
        cols = slice(c, c + step)
        dn = tn(da1, wi1[:, cols]) * gain1[:, cols]
        flow = g[:, cols].astype(F32) + scale1 * dn - pull * x1[:, cols].astype(F32)
        flow_ref[:, cols] = flow.astype(BF16)
    split_terms(share, index_ref[0], das1, xg1, act1, g, keep_ref, send_ref)


def pick_kernel(place_ref, index_ref, w_out, out_ref, sems):
    half = out_ref.shape[1]
    cols = pl.ds(pl.multiple_of((index_ref[0] % 2) * half, half), half)
    copy = pltpu.make_async_copy(w_out.at[0, place_ref[0], :, cols], out_ref, sems.at[0])
    copy.start()
    copy.wait()


def flow_kernel(share, index_ref, flow_ref, own_ref, other_ref, act0_ref, send_ref):
    half = own_ref.shape[1]
    core = index_ref[0] % 2
    delta = jnp.zeros(act0_ref.shape, F32)
    for w_ref, number in ((own_ref, core), (other_ref, 1 - core)):
        for c in range(0, half, share):
            cols = pl.ds(pl.multiple_of(number * half + c, share), share)
            delta += nt(w_ref[:, c : c + share], flow_ref[:, cols])
    send_ref[0] = act0_ref[...]
    send_ref[1] = delta.astype(BF16)


def lower_kernel(share, index_ref, flow_ref, xg0_ref, low_ref, got_ref, keep_ref, send_ref):
    da0 = (got_ref[1].astype(F32) * low_ref[0]).astype(BF16)
    das0 = (da0.astype(F32) * low_ref[1]).astype(BF16)
    split_terms(share, index_ref[0], das0, xg0_ref, got_ref[0], flow_ref, keep_ref, send_ref)


def plane_kernel(
    place_ref, index_ref, keep1, got1, keep0, got0, own_ref, first_ref, second_ref, across
):
    row = (index_ref[0] // 2) % 2

    def order(near, far, along_x, along_y):
        for i in range(own_ref.shape[0]):
            for to_ref, (keep, got), number in (
                (across, far, 1 - row),
                (along_x, far, row),
                (along_y, near, 1 - row),
                (own_ref, near, row),
            ):
                block = 2 * i + number
                to_ref[i] = (keep[block].astype(F32) + got[block].astype(F32)).astype(BF16)

    for place, near, far in (
        (1, (keep1, got1), (keep0, got0)),
        (0, (keep0, got0), (keep1, got1)),
    ):
        for core, ways in ((0, (second_ref, first_ref)), (1, (first_ref, second_ref))):
            pl.when((place_ref[0] == place) & (index_ref[0] % 2 == core))(
                partial(order, near, far, *ways)
            )


def layer_kernel(index_ref, own, got_a, got_b, got_c, *out_refs):
    layer = index_ref[0] // 4
    for k, out_ref in enumerate(out_refs):
        block = layer ^ k
        total = own[block].astype(F32) + got_a[block].astype(F32)
        total += got_b[block].astype(F32) + got_c[block].astype(F32)
        out_ref[...] = total.astype(BF16)


def total_kernel(*refs):
    *got, in_ref, out_ref = refs
    rank = in_ref.shape[1]
    total = got[0][...].astype(F32)
    for ref in got[1:]:
        total += ref[...].astype(F32)
    in_ref[0] = total[0:rank]
    out_ref[0] = total[rank : 2 * rank]


def params():
    return pltpu.CompilerParams(vmem_limit_bytes=VMEM_BYTES)


def whole():
    return pl.BlockSpec(memory_space=pltpu.VMEM)


def pair_on_device(saved, top_grad, gains, adapter_in, adapter_out):
    place = lax.axis_index("section")
    count = lax.axis_size("dp")
    tokens, width = saved.shape[2:]
    rank = adapter_in.shape[3]
    share = width // count
    adapter_in = jnp.swapaxes(adapter_in, 2, 3)
    saved, top_grad, gains, adapter_in, adapter_out = [
        pltpu.with_memory_space_constraint(a, pltpu.HBM)
        for a in (saved, top_grad, gains, adapter_in, adapter_out)
    ]
    place_ref = place.astype(jnp.int32)[None]
    index_ref = lax.axis_index("dp").astype(jnp.int32)[None]
    scalar = pl.BlockSpec(memory_space=pltpu.SMEM)
    chips, layers = count // 2, count // 4
    blocks = jax.ShapeDtypeStruct((chips, 2 * rank, share), BF16)
    fourth = jax.ShapeDtypeStruct((layers, 2 * rank, share), BF16)
    block = jax.ShapeDtypeStruct((2 * rank, share), BF16)
    wide = jax.ShapeDtypeStruct((tokens, width), BF16)

    def swapped(array, *ways):
        pairs = []
        for s in range(2):
            for d in range(count):
                over_section, bits = ways[d % len(ways)]
                pairs.append((s * count + d, (s ^ over_section) * count + (d ^ bits)))
        return lax.ppermute(array, ("section", "dp"), pairs)

    mine = pl.pallas_call(
        pick_kernel,
        in_specs=[scalar] * 2 + [pl.BlockSpec(memory_space=pltpu.HBM)],
        out_specs=whole(),
        out_shape=jax.ShapeDtypeStruct((rank, width // 2), BF16),
        scratch_shapes=[pltpu.SemaphoreType.DMA((1,))],
        compiler_params=params(),
        name="pick",
    )(place_ref, index_ref, adapter_out)
    partner_half = swapped(mine, (1, 0))
    keep1, send1, flow, xg0, act0, low = pl.pallas_call(
        partial(upper_kernel, share),
        in_specs=[scalar] * 2 + [pl.BlockSpec(memory_space=pltpu.HBM)] * 5,
        out_specs=[whole()] * 6,
        out_shape=[
            blocks, blocks, wide, wide,
            jax.ShapeDtypeStruct((rank, tokens), BF16),
            jax.ShapeDtypeStruct((2, rank, tokens), F32),
        ],
        scratch_shapes=[pltpu.VMEM((tokens, width), BF16)] * 3
        + [pltpu.VMEM((1, width), F32)] * 2
        + [pltpu.VMEM((rank, width), BF16)] * 3
        + [pltpu.VMEM((tokens, width), BF16), pltpu.SemaphoreType.DMA((8,))],
        compiler_params=params(),
        cost_estimate=pl.CostEstimate(
            flops=12 * tokens * width * rank, bytes_accessed=12 * tokens * width, transcendentals=0
        ),
        name="upper",
    )(place_ref, index_ref, saved, top_grad, gains, adapter_in, adapter_out)
    partner_half, flow = lax.optimization_barrier((partner_half, flow))
    partner_other = swapped(partner_half, (0, 1))
    got1 = swapped(send1, (0, 1))
    send = pl.pallas_call(
        partial(flow_kernel, share),
        in_specs=[scalar] + [whole()] * 4,
        out_specs=whole(),
        out_shape=jax.ShapeDtypeStruct((2, rank, tokens), BF16),
        compiler_params=params(),
        name="flow",
    )(index_ref, flow, partner_half, partner_other, act0)
    got = swapped(send, (1, 0))
    keep0, send0 = pl.pallas_call(
        partial(lower_kernel, share),
        in_specs=[scalar] + [whole()] * 4,
        out_specs=[whole()] * 2,
        out_shape=[blocks] * 2,
        compiler_params=params(),
        name="lower",
    )(index_ref, flow, xg0, low, got)
    got0 = swapped(send0, (0, 1))
    own, first, second, across = pl.pallas_call(
        plane_kernel,
        in_specs=[scalar] * 2 + [whole()] * 4,
        out_specs=[whole()] * 4,
        out_shape=[fourth] * 4,
        compiler_params=params(),
        name="plane",
    )(place_ref, index_ref, keep1, got1, keep0, got0)
    first = swapped(first, (0, 2), (1, 0))
    second = swapped(second, (1, 0), (0, 2))
    across = swapped(across, (1, 2))
    mine, *others = pl.pallas_call(
        layer_kernel,
        in_specs=[scalar] + [whole()] * 4,
        out_specs=[whole()] * layers,
        out_shape=[block] * layers,
        compiler_params=params(),
        name="layer",
    )(index_ref, own, first, across, second)
    others = [swapped(other, (0, 4 * k)) for k, other in enumerate(others, 1)]
    others = others[1:] + others[:1]
    total_in, total_out = pl.pallas_call(
        total_kernel,
        in_specs=[whole()] * layers,
        out_specs=[whole()] * 2,
        out_shape=[jax.ShapeDtypeStruct((1, rank, share), F32)] * 2,
        compiler_params=params(),
        name="total",
    )(mine, *others)
    return (jnp.swapaxes(total_in, 1, 2), total_out)


def section_back(x, gain, weight_in, weight_out, upstream):
    xf = x.astype(F32)
    scale = lax.rsqrt(jnp.mean(xf * xf, axis=-1, keepdims=True) + EPS)
    normed = xf * scale
    hidden = (normed * gain).astype(BF16)
    pre = jnp.dot(hidden, weight_in, preferred_element_type=F32)
    sig, slope = silu_slope(pre)
    active = (pre * sig).astype(BF16)
    delta_act = jnp.dot(upstream, weight_out.T, preferred_element_type=F32)
    delta_pre = (delta_act * slope).astype(BF16)
    delta_norm = jnp.dot(delta_pre, weight_in.T, preferred_element_type=F32) * gain
    inner = jnp.mean(delta_norm * normed, axis=-1, keepdims=True)
    result = (upstream.astype(F32) + scale * (delta_norm - normed * inner)).astype(BF16)
    term_in = jnp.dot(hidden.T, delta_pre, preferred_element_type=F32)
    term_out = jnp.dot(active.T, upstream, preferred_element_type=F32)
    return (result, term_in, term_out)


def relay_on_device(saved, top_grad, gains, adapter_in, adapter_out):
    sections = lax.axis_size("section")
    place = lax.axis_index("section")
    width = top_grad.shape[2]
    rank = adapter_in.shape[3]
    zero_in = jnp.zeros((width, rank), F32)
    zero_out = jnp.zeros((rank, width), F32)

    def step(turn, flows, sums):
        leaving, added = [], []
        for replica in (0, 1):
            serves = place == (sections - 1 - turn if replica == 0 else turn)
            result, term_in, term_out = lax.cond(
                serves,
                partial(
                    section_back,
                    saved[0, replica],
                    gains[0, replica],
                    adapter_in[0, replica],
                    adapter_out[0, replica],
                ),
                lambda flow: (flow, zero_in, zero_out),
                flows[replica],
            )
            leaving.append(result)
            added += [sums[2 * replica] + term_in, sums[2 * replica + 1] + term_out]
        return leaving, added

    down = [(i, i - 1) for i in range(1, sections)]
    up = [(i, i + 1) for i in range(sections - 1)]

    def turn_and_pass(turn, carry):
        leaving, sums = step(turn, carry[0], carry[1])
        return (
            [lax.ppermute(leaving[0], "section", down), lax.ppermute(leaving[1], "section", up)],
            sums,
        )

    start = ([top_grad[0], top_grad[1]], [zero_in, zero_out, zero_in, zero_out])
    flows, sums = lax.fori_loop(0, sections - 1, turn_and_pass, start)
    _, sums = step(sections - 1, flows, sums)
    shares = [
        lax.psum_scatter(term, "dp", scatter_dimension=i % 2, tiled=True)
        for i, term in enumerate(sums)
    ]
    mirror = [(i, sections - 1 - i) for i in range(sections)]
    total_in = shares[0] + lax.ppermute(shares[2], "section", mirror)
    total_out = shares[1] + lax.ppermute(shares[3], "section", mirror)
    return (total_in[None], total_out[None])


def solution(mesh):
    in_specs = (
        P("section", None, "dp", None),
        P(None, "dp", None),
        P("section", None, None),
        P("section", None, None, None),
        P("section", None, None, None),
    )
    out_specs = (P("section", "dp", None), P("section", None, "dp"))

    def run(saved, *others):
        share = saved.shape[3] // mesh.shape["dp"]
        count = mesh.shape["dp"]
        pair = mesh.shape["section"] == 2 and share % 128 == 0
        pair = pair and count >= 4 and count & (count - 1) == 0
        on_device = pair_on_device if pair else relay_on_device
        return jax.shard_map(
            on_device, mesh=mesh, in_specs=in_specs, out_specs=out_specs, check_vma=False
        )(saved, *others)

    return run
```

```python
from functools import partial

import jax
import jax.numpy as jnp
from jax import lax
from jax.experimental import pallas as pl
from jax.experimental.pallas import tpu as pltpu
from jax.sharding import PartitionSpec as P

EPS = 1e-05
VMEM_BYTES = 24 * 1024 * 1024
F32 = jnp.float32
BF16 = jnp.bfloat16


LONG = pl.CostEstimate(flops=2 * 10**10, bytes_accessed=2**20, transcendentals=0)


def nn(a, b):
    return lax.dot_general(a, b, (((1,), (0,)), ((), ())), preferred_element_type=F32)


def nt(a, b):
    return lax.dot_general(a, b, (((1,), (1,)), ((), ())), preferred_element_type=F32)


def tn(a, b):
    return lax.dot_general(a, b, (((0,), (0,)), ((), ())), preferred_element_type=F32)


def as_row(column):
    count = column.shape[0]
    return jnp.transpose(jnp.broadcast_to(column, (count, count)))[0:1, :]


def silu_slope(pre):
    sig = jax.nn.sigmoid(pre)
    return sig, sig * (1.0 + pre * (1.0 - sig))


def project(x_ref, gain_ref, w_ref, xg_ref, step):
    tokens, width = x_ref.shape
    squares = jnp.zeros((tokens, 128), F32)
    pre = jnp.zeros((w_ref.shape[0], tokens), F32)
    for c in range(0, width, step):
        x = x_ref[:, c : c + step].astype(F32)
        for k in range(0, step, 128):
            part = x[:, k : k + 128]
            squares += part * part
        xg = (x * gain_ref[:, c : c + step]).astype(BF16)
        xg_ref[:, c : c + step] = xg
        pre += nt(w_ref[:, c : c + step], xg)
    mean = jnp.sum(squares, axis=1, keepdims=True) * (1.0 / width)
    scale = lax.rsqrt(mean + EPS)
    return scale, pre


def split_terms(share, index, das, xg_ref, act, flow_ref, keep_ref, send_ref):
    rank = das.shape[0]
    core = index % 2
    for i in range(keep_ref.shape[0]):
        for to_ref, number in ((keep_ref, core), (send_ref, 1 - core)):
            cols = pl.ds(pl.multiple_of((2 * i + number) * share, share), share)
            to_ref[i, 0:rank] = nn(das, xg_ref[:, cols]).astype(BF16)
            to_ref[i, rank : 2 * rank] = nn(act, flow_ref[:, cols]).astype(BF16)


def front_kernel(
    step, place_ref, saved, top, gains, w_in, w_out,
    act0_ref, low_ref, xg0_ref, x1, g, gain1, wi1, wo1,
    x0, gain0, wi0, sems,
):
    lower = place_ref[0]
    upper = 1 - lower
    copies = [
        (gains.at[0, pl.ds(lower, 1)], gain0),
        (w_in.at[0, lower], wi0),
        (saved.at[0, lower], x0),
        (gains.at[0, pl.ds(upper, 1)], gain1),
        (w_in.at[0, upper], wi1),
        (saved.at[0, upper], x1),
        (w_out.at[0, upper], wo1),
        (top.at[upper], g),
    ]
    copies = [pltpu.make_async_copy(a, b, sems.at[i]) for i, (a, b) in enumerate(copies)]
    for copy in copies:
        copy.start()
    for copy in copies[0:3]:
        copy.wait()
    scale, raw = project(x0, gain0, wi0, xg0_ref, step)
    row = as_row(scale)
    pre = raw * row
    sig, slope = silu_slope(pre)
    act0_ref[...] = (pre * sig).astype(BF16)
    low_ref[0] = slope
    low_ref[1] = jnp.broadcast_to(row, raw.shape)
    for copy in copies[3:8]:
        copy.wait()


def upper_kernel(step, x, g, gain, wi, wo, xg_ref, act_ref, das_ref, da_ref, columns_ref):
    width = x.shape[1]
    scale, raw = project(x, gain, wi, xg_ref, step)
    delta = jnp.zeros(raw.shape, F32)
    for c in range(0, width, step):
        delta += nt(wo[:, c : c + step], g[:, c : c + step])
    row = as_row(scale)
    pre = raw * row
    sig, slope = silu_slope(pre)
    da = (delta * slope).astype(BF16)
    daf = da.astype(F32)
    inner = jnp.sum(daf * pre, axis=0, keepdims=True) * (1.0 / width)
    act_ref[...] = (pre * sig).astype(BF16)
    das_ref[...] = (daf * row).astype(BF16)
    da_ref[...] = da
    square = columns_ref.shape[1:]
    columns_ref[0] = jnp.broadcast_to(scale, square)
    columns_ref[1] = jnp.transpose(jnp.broadcast_to(inner * row * row, square))


def outgoing_kernel(step, x, g, gain, wi, da_ref, columns_ref, flow_ref):
    da = da_ref[...]
    scale = columns_ref[0][:, 0:1]
    pull = columns_ref[1][:, 0:1]
    for c in range(0, x.shape[1], step):
        cols = slice(c, c + step)
        dn = tn(da, wi[:, cols]) * gain[:, cols]
        flow = g[:, cols].astype(F32) + scale * dn - pull * x[:, cols].astype(F32)
        flow_ref[:, cols] = flow.astype(BF16)


def terms_kernel(share, index_ref, g, xg_ref, act_ref, das_ref, _, keep_ref, send_ref):
    split_terms(
        share, index_ref[0], das_ref[...], xg_ref, act_ref[...], g, keep_ref, send_ref
    )


def pick_kernel(place_ref, index_ref, w_out, out_ref, sems):
    half = out_ref.shape[1]
    cols = pl.ds(pl.multiple_of((index_ref[0] % 2) * half, half), half)
    copy = pltpu.make_async_copy(w_out.at[0, place_ref[0], :, cols], out_ref, sems.at[0])
    copy.start()
    copy.wait()


def flow_kernel(share, index_ref, flow_ref, own_ref, other_ref, act0_ref, send_ref):
    half = own_ref.shape[1]
    core = index_ref[0] % 2
    delta = jnp.zeros(act0_ref.shape, F32)
    for w_ref, number in ((own_ref, core), (other_ref, 1 - core)):
        for c in range(0, half, share):
            cols = pl.ds(pl.multiple_of(number * half + c, share), share)
            delta += nt(w_ref[:, c : c + share], flow_ref[:, cols])
    send_ref[0] = act0_ref[...]
    send_ref[1] = delta.astype(BF16)


def lower_kernel(share, index_ref, flow_ref, xg0_ref, low_ref, got_ref, keep_ref, send_ref):
    da0 = (got_ref[1].astype(F32) * low_ref[0]).astype(BF16)
    das0 = (da0.astype(F32) * low_ref[1]).astype(BF16)
    split_terms(share, index_ref[0], das0, xg0_ref, got_ref[0], flow_ref, keep_ref, send_ref)


def plane_kernel(
    place_ref, index_ref, keep1, got1, keep0, got0, own_ref, first_ref, second_ref, across
):
    row = (index_ref[0] // 2) % 2

    def order(near, far, along_x, along_y):
        for i in range(own_ref.shape[0]):
            for to_ref, (keep, got), number in (
                (across, far, 1 - row),
                (along_x, far, row),
                (along_y, near, 1 - row),
                (own_ref, near, row),
            ):
                block = 2 * i + number
                to_ref[i] = (keep[block].astype(F32) + got[block].astype(F32)).astype(BF16)

    for place, near, far in (
        (1, (keep1, got1), (keep0, got0)),
        (0, (keep0, got0), (keep1, got1)),
    ):
        for core, ways in ((0, (second_ref, first_ref)), (1, (first_ref, second_ref))):
            pl.when((place_ref[0] == place) & (index_ref[0] % 2 == core))(
                partial(order, near, far, *ways)
            )


def layer_kernel(index_ref, own, got_a, got_b, got_c, *out_refs):
    layer = index_ref[0] // 4
    for k, out_ref in enumerate(out_refs):
        block = layer ^ k
        total = own[block].astype(F32) + got_a[block].astype(F32)
        total += got_b[block].astype(F32) + got_c[block].astype(F32)
        out_ref[...] = total.astype(BF16)


def total_kernel(*refs):
    *got, in_ref, out_ref = refs
    rank = in_ref.shape[1]
    total = got[0][...].astype(F32)
    for ref in got[1:]:
        total += ref[...].astype(F32)
    in_ref[0] = total[0:rank]
    out_ref[0] = total[rank : 2 * rank]


def local(kernel, name, out_shapes, *operands, scratch=(), cost=None):
    spaces = {"scalar": pltpu.SMEM, "far": pltpu.HBM, "near": pltpu.VMEM}
    out = pl.pallas_call(
        kernel,
        in_specs=[pl.BlockSpec(memory_space=spaces[kind]) for kind, _ in operands],
        out_specs=[pl.BlockSpec(memory_space=pltpu.VMEM)] * len(out_shapes),
        out_shape=[jax.ShapeDtypeStruct(shape, dtype) for shape, dtype in out_shapes],
        scratch_shapes=list(scratch),
        compiler_params=pltpu.CompilerParams(vmem_limit_bytes=VMEM_BYTES),
        cost_estimate=cost,
        name=name,
    )(*[array for _, array in operands])
    return out if len(out) > 1 else out[0]


def near(*arrays):
    return [("near", array) for array in arrays]


def pair_on_device(saved, top_grad, gains, adapter_in, adapter_out):
    count = lax.axis_size("dp")
    tokens, width = saved.shape[2:]
    rank = adapter_in.shape[3]
    share = width // count
    chips, layers = count // 2, count // 4
    place = ("scalar", lax.axis_index("section").astype(jnp.int32)[None])
    index = ("scalar", lax.axis_index("dp").astype(jnp.int32)[None])
    saved, top, gains, w_in, w_out = [
        ("far", pltpu.with_memory_space_constraint(a, pltpu.HBM))
        for a in (saved, top_grad, gains, jnp.swapaxes(adapter_in, 2, 3), adapter_out)
    ]

    def swapped(array, *ways):
        pairs = []
        for s in range(2):
            for d in range(count):
                over_section, bits = ways[d % len(ways)]
                pairs.append((s * count + d, (s ^ over_section) * count + (d ^ bits)))
        return lax.ppermute(array, ("section", "dp"), pairs)

    sems = pltpu.SemaphoreType.DMA
    wide = ((tokens, width), BF16)
    thin = ((rank, width), BF16)
    gain = ((1, width), F32)
    small = ((rank, tokens), BF16)
    blocks = ((chips, 2 * rank, share), BF16)
    quarter = ((layers, 2 * rank, share), BF16)
    along_x, other_core = (1, 0), (0, 1)

    mine = local(
        pick_kernel, "pick", [((rank, width // 2), BF16)], place, index, w_out, scratch=[sems((1,))]
    )
    own_half = swapped(mine, along_x)
    act0, low, xg0, x1, g, gain1, wi1, wo1 = local(
        partial(front_kernel, share), "front",
        [small, ((2, rank, tokens), F32), wide, wide, wide, gain, thin, thin],
        place, saved, top, gains, w_in, w_out,
        scratch=[pltpu.VMEM(*wide), pltpu.VMEM(*gain), pltpu.VMEM(*thin), sems((8,))],
    )
    xg1, act1, das1, da1, columns = local(
        partial(upper_kernel, share), "upper",
        [wide, small, small, small, ((2, tokens, tokens), F32)],
        *near(x1, g, gain1, wi1, wo1),
    )
    own_half, da1 = lax.optimization_barrier((own_half, da1))
    other_half = swapped(own_half, other_core)
    flow = local(
        partial(outgoing_kernel, share), "outgoing", [wide], *near(x1, g, gain1, wi1, da1, columns)
    )
    send = local(
        partial(flow_kernel, share), "flow", [((2, rank, tokens), BF16)],
        index, *near(flow, own_half, other_half, act0), cost=LONG,
    )
    got = swapped(send, along_x)
    keep1, send1 = local(
        partial(terms_kernel, share), "terms", [blocks, blocks],
        index, *near(g, xg1, act1, das1, send),
    )
    got1 = swapped(send1, other_core)
    keep0, send0 = local(
        partial(lower_kernel, share), "lower", [blocks, blocks],
        index, *near(flow, xg0, low, got), cost=LONG,
    )
    got0 = swapped(send0, other_core)
    own, first, second, across = local(
        plane_kernel, "plane", [quarter] * 4, place, index, *near(keep1, got1, keep0, got0)
    )
    first = swapped(first, (0, 2), (1, 0))
    second = swapped(second, (1, 0), (0, 2))
    across = swapped(across, (1, 2))
    mine, *others = local(
        layer_kernel, "layer", [((2 * rank, share), BF16)] * layers,
        index, *near(own, first, across, second),
    )
    others = [swapped(other, (0, 4 * k)) for k, other in enumerate(others, 1)]
    others = others[1:] + others[:1]
    block = ((1, rank, share), F32)
    total_in, total_out = local(total_kernel, "total", [block, block], *near(mine, *others))
    return (jnp.swapaxes(total_in, 1, 2), total_out)


def section_back(x, gain, weight_in, weight_out, upstream):
    xf = x.astype(F32)
    scale = lax.rsqrt(jnp.mean(xf * xf, axis=-1, keepdims=True) + EPS)
    normed = xf * scale
    hidden = (normed * gain).astype(BF16)
    pre = jnp.dot(hidden, weight_in, preferred_element_type=F32)
    sig, slope = silu_slope(pre)
    active = (pre * sig).astype(BF16)
    delta_act = jnp.dot(upstream, weight_out.T, preferred_element_type=F32)
    delta_pre = (delta_act * slope).astype(BF16)
    delta_norm = jnp.dot(delta_pre, weight_in.T, preferred_element_type=F32) * gain
    inner = jnp.mean(delta_norm * normed, axis=-1, keepdims=True)
    result = (upstream.astype(F32) + scale * (delta_norm - normed * inner)).astype(BF16)
    term_in = jnp.dot(hidden.T, delta_pre, preferred_element_type=F32)
    term_out = jnp.dot(active.T, upstream, preferred_element_type=F32)
    return (result, term_in, term_out)


def relay_on_device(saved, top_grad, gains, adapter_in, adapter_out):
    sections = lax.axis_size("section")
    place = lax.axis_index("section")
    width = top_grad.shape[2]
    rank = adapter_in.shape[3]
    zero_in = jnp.zeros((width, rank), F32)
    zero_out = jnp.zeros((rank, width), F32)

    def step(turn, flows, sums):
        leaving, added = [], []
        for replica in (0, 1):
            serves = place == (sections - 1 - turn if replica == 0 else turn)
            result, term_in, term_out = lax.cond(
                serves,
                partial(
                    section_back,
                    saved[0, replica],
                    gains[0, replica],
                    adapter_in[0, replica],
                    adapter_out[0, replica],
                ),
                lambda flow: (flow, zero_in, zero_out),
                flows[replica],
            )
            leaving.append(result)
            added += [sums[2 * replica] + term_in, sums[2 * replica + 1] + term_out]
        return leaving, added

    down = [(i, i - 1) for i in range(1, sections)]
    up = [(i, i + 1) for i in range(sections - 1)]

    def turn_and_pass(turn, carry):
        leaving, sums = step(turn, carry[0], carry[1])
        return (
            [lax.ppermute(leaving[0], "section", down), lax.ppermute(leaving[1], "section", up)],
            sums,
        )

    start = ([top_grad[0], top_grad[1]], [zero_in, zero_out, zero_in, zero_out])
    flows, sums = lax.fori_loop(0, sections - 1, turn_and_pass, start)
    _, sums = step(sections - 1, flows, sums)
    shares = [
        lax.psum_scatter(term, "dp", scatter_dimension=i % 2, tiled=True)
        for i, term in enumerate(sums)
    ]
    mirror = [(i, sections - 1 - i) for i in range(sections)]
    total_in = shares[0] + lax.ppermute(shares[2], "section", mirror)
    total_out = shares[1] + lax.ppermute(shares[3], "section", mirror)
    return (total_in[None], total_out[None])


def solution(mesh):
    in_specs = (
        P("section", None, "dp", None),
        P(None, "dp", None),
        P("section", None, None),
        P("section", None, None, None),
        P("section", None, None, None),
    )
    out_specs = (P("section", "dp", None), P("section", None, "dp"))

    def run(saved, *others):
        share = saved.shape[3] // mesh.shape["dp"]
        count = mesh.shape["dp"]
        pair = mesh.shape["section"] == 2 and share % 128 == 0
        pair = pair and count >= 4 and count & (count - 1) == 0
        on_device = pair_on_device if pair else relay_on_device
        return jax.shard_map(
            on_device, mesh=mesh, in_specs=in_specs, out_specs=out_specs, check_vma=False
        )(saved, *others)

    return run
```

```python
from functools import partial

import jax
import jax.numpy as jnp
from jax import lax
from jax.experimental import pallas as pl
from jax.experimental.pallas import tpu as pltpu
from jax.sharding import PartitionSpec as P

EPS = 1e-05
VMEM_BYTES = 24 * 1024 * 1024
F32 = jnp.float32
BF16 = jnp.bfloat16


LONG = pl.CostEstimate(flops=2 * 10**10, bytes_accessed=2**20, transcendentals=0)


def nn(a, b):
    return lax.dot_general(a, b, (((1,), (0,)), ((), ())), preferred_element_type=F32)


def nt(a, b):
    return lax.dot_general(a, b, (((1,), (1,)), ((), ())), preferred_element_type=F32)


def tn(a, b):
    return lax.dot_general(a, b, (((0,), (0,)), ((), ())), preferred_element_type=F32)


def as_row(column):
    count = column.shape[0]
    return jnp.transpose(jnp.broadcast_to(column, (count, count)))[0:1, :]


def silu_slope(pre):
    sig = jax.nn.sigmoid(pre)
    return sig, sig * (1.0 + pre * (1.0 - sig))


def project(x_ref, gain_ref, w_ref, xg_ref, step):
    tokens, width = x_ref.shape
    squares = jnp.zeros((tokens, 128), F32)
    pre = jnp.zeros((w_ref.shape[0], tokens), F32)
    for c in range(0, width, step):
        x = x_ref[:, c : c + step].astype(F32)
        for k in range(0, step, 128):
            part = x[:, k : k + 128]
            squares += part * part
        xg = (x * gain_ref[:, c : c + step]).astype(BF16)
        xg_ref[:, c : c + step] = xg
        pre += nt(w_ref[:, c : c + step], xg)
    mean = jnp.sum(squares, axis=1, keepdims=True) * (1.0 / width)
    scale = lax.rsqrt(mean + EPS)
    return scale, pre


def fill(index, matrix, wide_ref, keep_ref, send_ref):
    share = keep_ref.shape[2]
    core = index % 2
    for i in range(wide_ref.shape[1] // share // 2):
        for to_ref, number in ((keep_ref, core), (send_ref, 1 - core)):
            cols = pl.ds(pl.multiple_of((2 * i + number) * share, share), share)
            to_ref[i] = nn(matrix, wide_ref[:, cols]).astype(BF16)


def front_kernel(
    step, place_ref, saved, top, gains, w_in, w_out,
    act0_ref, low_ref, xg0_ref, x1, g, gain1, wi1, wo1,
    x0, gain0, wi0, sems,
):
    lower = place_ref[0]
    upper = 1 - lower
    copies = [
        (gains.at[0, pl.ds(lower, 1)], gain0),
        (w_in.at[0, lower], wi0),
        (saved.at[0, lower], x0),
        (gains.at[0, pl.ds(upper, 1)], gain1),
        (w_in.at[0, upper], wi1),
        (saved.at[0, upper], x1),
        (w_out.at[0, upper], wo1),
        (top.at[upper], g),
    ]
    copies = [pltpu.make_async_copy(a, b, sems.at[i]) for i, (a, b) in enumerate(copies)]
    for copy in copies:
        copy.start()
    for copy in copies[0:3]:
        copy.wait()
    scale, raw = project(x0, gain0, wi0, xg0_ref, step)
    row = as_row(scale)
    pre = raw * row
    sig, slope = silu_slope(pre)
    act0_ref[...] = (pre * sig).astype(BF16)
    low_ref[0] = slope
    low_ref[1] = jnp.broadcast_to(row, raw.shape)
    for copy in copies[3:8]:
        copy.wait()


def upper_kernel(step, x, g, gain, wi, wo, xg_ref, act_ref, das_ref, da_ref, columns_ref):
    width = x.shape[1]
    scale, raw = project(x, gain, wi, xg_ref, step)
    delta = jnp.zeros(raw.shape, F32)
    for c in range(0, width, step):
        delta += nt(wo[:, c : c + step], g[:, c : c + step])
    row = as_row(scale)
    pre = raw * row
    sig, slope = silu_slope(pre)
    da = (delta * slope).astype(BF16)
    daf = da.astype(F32)
    inner = jnp.sum(daf * pre, axis=0, keepdims=True) * (1.0 / width)
    act_ref[...] = (pre * sig).astype(BF16)
    das_ref[...] = (daf * row).astype(BF16)
    da_ref[...] = da
    square = columns_ref.shape[1:]
    columns_ref[0] = jnp.broadcast_to(scale, square)
    columns_ref[1] = jnp.transpose(jnp.broadcast_to(inner * row * row, square))


def outgoing_kernel(step, x, g, gain, wi, da_ref, columns_ref, flow_ref):
    da = da_ref[...]
    scale = columns_ref[0][:, 0:1]
    pull = columns_ref[1][:, 0:1]
    for c in range(0, x.shape[1], step):
        cols = slice(c, c + step)
        dn = tn(da, wi[:, cols]) * gain[:, cols]
        flow = g[:, cols].astype(F32) + scale * dn - pull * x[:, cols].astype(F32)
        flow_ref[:, cols] = flow.astype(BF16)


def terms1_kernel(index_ref, g, xg_ref, act_ref, das_ref, _, keep_out, send_out, keep_in, send_in):
    fill(index_ref[0], act_ref[...], g, keep_out, send_out)
    fill(index_ref[0], das_ref[...], xg_ref, keep_in, send_in)


def terms_kernel(
    index_ref, flow_ref, act0_ref, keep_out1, send_out1, keep_in1, send_in1, keep_ref, send_ref
):
    fill(index_ref[0], act0_ref[...], flow_ref, keep_ref, send_ref)
    chips = keep_in1.shape[0]
    keep_ref[chips : 2 * chips] = keep_out1[...]
    send_ref[chips : 2 * chips] = send_out1[...]
    keep_ref[2 * chips : 3 * chips] = keep_in1[...]
    send_ref[2 * chips : 3 * chips] = send_in1[...]


def pick_kernel(place_ref, index_ref, w_out, out_ref, sems):
    half = out_ref.shape[1]
    cols = pl.ds(pl.multiple_of((index_ref[0] % 2) * half, half), half)
    copy = pltpu.make_async_copy(w_out.at[0, place_ref[0], :, cols], out_ref, sems.at[0])
    copy.start()
    copy.wait()


def flow_kernel(share, index_ref, flow_ref, own_ref, other_ref, send_ref):
    half = own_ref.shape[1]
    core = index_ref[0] % 2
    delta = jnp.zeros(send_ref.shape, F32)
    for w_ref, number in ((own_ref, core), (other_ref, 1 - core)):
        for c in range(0, half, share):
            cols = pl.ds(pl.multiple_of(number * half + c, share), share)
            delta += nt(w_ref[:, c : c + share], flow_ref[:, cols])
    send_ref[...] = delta.astype(BF16)


def lower_kernel(index_ref, xg0_ref, low_ref, got_ref, keep_ref, send_ref):
    da = (got_ref[...].astype(F32) * low_ref[0]).astype(BF16)
    das = (da.astype(F32) * low_ref[1]).astype(BF16)
    fill(index_ref[0], das, xg0_ref, keep_ref, send_ref)


def chip_kernel(place_ref, index_ref, keep, got, _, sum_ref, across):
    for i in range(keep.shape[0]):
        sum_ref[i] = (keep[i].astype(F32) + got[i].astype(F32)).astype(BF16)
    row = (index_ref[0] // 2) % 2
    first = (1 - place_ref[0]) * (2 * across.shape[0]) + 1 - row
    for i in range(across.shape[0]):
        across[i] = sum_ref[first + 2 * i]


def plane_kernel(
    place_ref, index_ref, sums, keep0, got0, own_ref, first_ref, second_ref, across
):
    rank = keep0.shape[1]
    chips = keep0.shape[0]
    row = (index_ref[0] // 2) % 2

    def terms_in(section, block):
        if section == 0:
            return (keep0[block].astype(F32) + got0[block].astype(F32)).astype(BF16)
        return sums[2 * chips + block]

    def order(near, along_x, along_y):
        far = 1 - near
        for i in range(own_ref.shape[0]):
            across[i] = terms_in(far, 2 * i + 1 - row)
            for to_ref, section, number in (
                (along_x, far, row),
                (along_y, near, 1 - row),
                (own_ref, near, row),
            ):
                block = 2 * i + number
                to_ref[i, 0:rank] = terms_in(section, block)
                to_ref[i, rank : 2 * rank] = sums[section * chips + block]

    for place in range(2):
        for core, ways in ((0, (second_ref, first_ref)), (1, (first_ref, second_ref))):
            pl.when((place_ref[0] == place) & (index_ref[0] % 2 == core))(
                partial(order, place, *ways)
            )


def add_kernel(own, across_out, out_ref):
    rank = across_out.shape[1]
    out_ref[:, 0:rank] = own[:, 0:rank]
    for i in range(own.shape[0]):
        total = own[i, rank : 2 * rank].astype(F32) + across_out[i].astype(F32)
        out_ref[i, rank : 2 * rank] = total.astype(BF16)


def layer_kernel(index_ref, own, first, across_in, second, *out_refs):
    rank = across_in.shape[1]
    layer = index_ref[0] // 4
    for k, out_ref in enumerate(out_refs):
        block = layer ^ k
        total = sum(ref[block].astype(F32) for ref in (own, first, second))
        out_ref[0:rank] = (total[0:rank] + across_in[block].astype(F32)).astype(BF16)
        out_ref[rank : 2 * rank] = total[rank : 2 * rank].astype(BF16)


def total_kernel(*refs):
    *got, in_ref, out_ref = refs
    rank = in_ref.shape[1]
    total = got[0][...].astype(F32)
    for ref in got[1:]:
        total += ref[...].astype(F32)
    in_ref[0] = total[0:rank]
    out_ref[0] = total[rank : 2 * rank]


def local(kernel, name, out_shapes, *operands, scratch=(), cost=None):
    spaces = {"scalar": pltpu.SMEM, "far": pltpu.HBM, "near": pltpu.VMEM}
    out = pl.pallas_call(
        kernel,
        in_specs=[pl.BlockSpec(memory_space=spaces[kind]) for kind, _ in operands],
        out_specs=[pl.BlockSpec(memory_space=pltpu.VMEM)] * len(out_shapes),
        out_shape=[jax.ShapeDtypeStruct(shape, dtype) for shape, dtype in out_shapes],
        scratch_shapes=list(scratch),
        compiler_params=pltpu.CompilerParams(vmem_limit_bytes=VMEM_BYTES),
        cost_estimate=cost,
        name=name,
    )(*[array for _, array in operands])
    return out if len(out) > 1 else out[0]


def near(*arrays):
    return [("near", array) for array in arrays]


def pair_on_device(saved, top_grad, gains, adapter_in, adapter_out):
    count = lax.axis_size("dp")
    tokens, width = saved.shape[2:]
    rank = adapter_in.shape[3]
    share = width // count
    chips, layers = count // 2, count // 4
    place = ("scalar", lax.axis_index("section").astype(jnp.int32)[None])
    index = ("scalar", lax.axis_index("dp").astype(jnp.int32)[None])
    saved, top, gains, w_in, w_out = [
        ("far", pltpu.with_memory_space_constraint(a, pltpu.HBM))
        for a in (saved, top_grad, gains, jnp.swapaxes(adapter_in, 2, 3), adapter_out)
    ]

    def swapped(array, *ways):
        pairs = []
        for s in range(2):
            for d in range(count):
                over_section, bits = ways[d % len(ways)]
                pairs.append((s * count + d, (s ^ over_section) * count + (d ^ bits)))
        return lax.ppermute(array, ("section", "dp"), pairs)

    sems = pltpu.SemaphoreType.DMA
    wide = ((tokens, width), BF16)
    thin = ((rank, width), BF16)
    gain = ((1, width), F32)
    small = ((rank, tokens), BF16)
    one = ((chips, rank, share), BF16)
    three = ((3 * chips, rank, share), BF16)
    quarter = ((layers, rank, share), BF16)
    double = ((layers, 2 * rank, share), BF16)
    along_x, other_core = (1, 0), (0, 1)

    mine = local(
        pick_kernel, "pick", [((rank, width // 2), BF16)], place, index, w_out, scratch=[sems((1,))]
    )
    own_half = swapped(mine, along_x)
    act0, low, xg0, x1, g, gain1, wi1, wo1 = local(
        partial(front_kernel, share), "front",
        [small, ((2, rank, tokens), F32), wide, wide, wide, gain, thin, thin],
        place, saved, top, gains, w_in, w_out,
        scratch=[pltpu.VMEM(*wide), pltpu.VMEM(*gain), pltpu.VMEM(*thin), sems((8,))],
    )
    got_act0 = swapped(act0, along_x)
    xg1, act1, das1, da1, columns = local(
        partial(upper_kernel, share), "upper",
        [wide, small, small, small, ((2, tokens, tokens), F32)],
        *near(x1, g, gain1, wi1, wo1),
    )
    own_half, da1 = lax.optimization_barrier((own_half, da1))
    other_half = swapped(own_half, other_core)
    flow = local(
        partial(outgoing_kernel, share), "outgoing", [wide], *near(x1, g, gain1, wi1, da1, columns),
        cost=LONG,
    )
    delta = local(
        partial(flow_kernel, share), "flow", [small], index, *near(flow, own_half, other_half),
    )
    got_delta = swapped(delta, along_x)
    terms1 = local(
        terms1_kernel, "terms1", [one] * 4, index, *near(g, xg1, act1, das1, delta)
    )
    keep, send = local(
        terms_kernel, "terms", [three, three], index, *near(flow, got_act0, *terms1)
    )
    got = swapped(send, other_core)
    keep0, send0 = local(
        lower_kernel, "lower", [one, one], index, *near(xg0, low, got_delta), cost=LONG
    )
    got0 = swapped(send0, other_core)
    sums, across_out = local(
        chip_kernel, "chip", [three, quarter], place, index, *near(keep, got, keep0)
    )
    across_out = swapped(across_out, (1, 2))
    own, first, second, across_in = local(
        plane_kernel, "plane", [double, double, double, quarter],
        place, index, *near(sums, keep0, got0),
    )
    first = swapped(first, (0, 2), (1, 0))
    across_in = swapped(across_in, (1, 2))
    second = swapped(second, (1, 0), (0, 2))
    own = local(add_kernel, "add", [double], *near(own, across_out), cost=LONG)
    mine, *others = local(
        layer_kernel, "layer", [((2 * rank, share), BF16)] * layers,
        index, *near(own, first, across_in, second),
    )
    others = [swapped(other, (0, 4 * k)) for k, other in enumerate(others, 1)]
    others = others[1:] + others[:1]
    block = ((1, rank, share), F32)
    total_in, total_out = local(total_kernel, "total", [block, block], *near(mine, *others))
    return (jnp.swapaxes(total_in, 1, 2), total_out)


def section_back(x, gain, weight_in, weight_out, upstream):
    xf = x.astype(F32)
    scale = lax.rsqrt(jnp.mean(xf * xf, axis=-1, keepdims=True) + EPS)
    normed = xf * scale
    hidden = (normed * gain).astype(BF16)
    pre = jnp.dot(hidden, weight_in, preferred_element_type=F32)
    sig, slope = silu_slope(pre)
    active = (pre * sig).astype(BF16)
    delta_act = jnp.dot(upstream, weight_out.T, preferred_element_type=F32)
    delta_pre = (delta_act * slope).astype(BF16)
    delta_norm = jnp.dot(delta_pre, weight_in.T, preferred_element_type=F32) * gain
    inner = jnp.mean(delta_norm * normed, axis=-1, keepdims=True)
    result = (upstream.astype(F32) + scale * (delta_norm - normed * inner)).astype(BF16)
    term_in = jnp.dot(hidden.T, delta_pre, preferred_element_type=F32)
    term_out = jnp.dot(active.T, upstream, preferred_element_type=F32)
    return (result, term_in, term_out)


def relay_on_device(saved, top_grad, gains, adapter_in, adapter_out):
    sections = lax.axis_size("section")
    place = lax.axis_index("section")
    width = top_grad.shape[2]
    rank = adapter_in.shape[3]
    zero_in = jnp.zeros((width, rank), F32)
    zero_out = jnp.zeros((rank, width), F32)

    def step(turn, flows, sums):
        leaving, added = [], []
        for replica in (0, 1):
            serves = place == (sections - 1 - turn if replica == 0 else turn)
            result, term_in, term_out = lax.cond(
                serves,
                partial(
                    section_back,
                    saved[0, replica],
                    gains[0, replica],
                    adapter_in[0, replica],
                    adapter_out[0, replica],
                ),
                lambda flow: (flow, zero_in, zero_out),
                flows[replica],
            )
            leaving.append(result)
            added += [sums[2 * replica] + term_in, sums[2 * replica + 1] + term_out]
        return leaving, added

    down = [(i, i - 1) for i in range(1, sections)]
    up = [(i, i + 1) for i in range(sections - 1)]

    def turn_and_pass(turn, carry):
        leaving, sums = step(turn, carry[0], carry[1])
        return (
            [lax.ppermute(leaving[0], "section", down), lax.ppermute(leaving[1], "section", up)],
            sums,
        )

    start = ([top_grad[0], top_grad[1]], [zero_in, zero_out, zero_in, zero_out])
    flows, sums = lax.fori_loop(0, sections - 1, turn_and_pass, start)
    _, sums = step(sections - 1, flows, sums)
    shares = [
        lax.psum_scatter(term, "dp", scatter_dimension=i % 2, tiled=True)
        for i, term in enumerate(sums)
    ]
    mirror = [(i, sections - 1 - i) for i in range(sections)]
    total_in = shares[0] + lax.ppermute(shares[2], "section", mirror)
    total_out = shares[1] + lax.ppermute(shares[3], "section", mirror)
    return (total_in[None], total_out[None])


def solution(mesh):
    in_specs = (
        P("section", None, "dp", None),
        P(None, "dp", None),
        P("section", None, None),
        P("section", None, None, None),
        P("section", None, None, None),
    )
    out_specs = (P("section", "dp", None), P("section", None, "dp"))

    def run(saved, *others):
        share = saved.shape[3] // mesh.shape["dp"]
        count = mesh.shape["dp"]
        pair = mesh.shape["section"] == 2 and share % 128 == 0
        pair = pair and count >= 4 and count & (count - 1) == 0
        on_device = pair_on_device if pair else relay_on_device
        return jax.shard_map(
            on_device, mesh=mesh, in_specs=in_specs, out_specs=out_specs, check_vma=False
        )(saved, *others)

    return run
```

```python
from functools import partial

import jax
import jax.numpy as jnp
from jax import lax
from jax.experimental import pallas as pl
from jax.experimental.pallas import tpu as pltpu
from jax.sharding import PartitionSpec as P

EPS = 1e-05
VMEM_BYTES = 24 * 1024 * 1024
F32 = jnp.float32
BF16 = jnp.bfloat16


LONG = pl.CostEstimate(flops=2 * 10**10, bytes_accessed=2**20, transcendentals=0)


def nn(a, b):
    return lax.dot_general(a, b, (((1,), (0,)), ((), ())), preferred_element_type=F32)


def nt(a, b):
    return lax.dot_general(a, b, (((1,), (1,)), ((), ())), preferred_element_type=F32)


def tn(a, b):
    return lax.dot_general(a, b, (((0,), (0,)), ((), ())), preferred_element_type=F32)


def as_row(column):
    count = column.shape[0]
    return jnp.transpose(jnp.broadcast_to(column, (count, count)))[0:1, :]


def silu_slope(pre):
    sig = jax.nn.sigmoid(pre)
    return sig, sig * (1.0 + pre * (1.0 - sig))


def project(x_ref, gain_ref, w_ref, xg_ref, step):
    tokens, width = x_ref.shape
    squares = jnp.zeros((tokens, 128), F32)
    pre = jnp.zeros((w_ref.shape[0], tokens), F32)
    for c in range(0, width, step):
        x = x_ref[:, c : c + step].astype(F32)
        for k in range(0, step, 128):
            part = x[:, k : k + 128]
            squares += part * part
        xg = (x * gain_ref[:, c : c + step]).astype(BF16)
        xg_ref[:, c : c + step] = xg
        pre += nt(w_ref[:, c : c + step], xg)
    mean = jnp.sum(squares, axis=1, keepdims=True) * (1.0 / width)
    scale = lax.rsqrt(mean + EPS)
    return scale, pre


def fill(index, matrix, wide_ref, keep_ref, send_ref):
    share = keep_ref.shape[2]
    core = index % 2
    for i in range(wide_ref.shape[1] // share // 2):
        for to_ref, number in ((keep_ref, core), (send_ref, 1 - core)):
            cols = pl.ds(pl.multiple_of((2 * i + number) * share, share), share)
            to_ref[i] = nn(matrix, wide_ref[:, cols]).astype(BF16)


def front_kernel(
    step, place_ref, saved, top, gains, w_in, w_out,
    act0_ref, low_ref, xg0_ref, x1, g, gain1, wi1, wo1,
    x0, gain0, wi0, sems,
):
    lower = place_ref[0]
    upper = 1 - lower
    copies = [
        (gains.at[0, pl.ds(lower, 1)], gain0),
        (w_in.at[0, lower], wi0),
        (saved.at[0, lower], x0),
        (gains.at[0, pl.ds(upper, 1)], gain1),
        (w_in.at[0, upper], wi1),
        (saved.at[0, upper], x1),
        (w_out.at[0, upper], wo1),
        (top.at[upper], g),
    ]
    copies = [pltpu.make_async_copy(a, b, sems.at[i]) for i, (a, b) in enumerate(copies)]
    for copy in copies:
        copy.start()
    for copy in copies[0:3]:
        copy.wait()
    scale, raw = project(x0, gain0, wi0, xg0_ref, step)
    row = as_row(scale)
    pre = raw * row
    sig, slope = silu_slope(pre)
    act0_ref[...] = (pre * sig).astype(BF16)
    low_ref[0] = slope
    low_ref[1] = jnp.broadcast_to(row, raw.shape)
    for copy in copies[3:8]:
        copy.wait()


def upper_kernel(step, x, g, gain, wi, wo, xg_ref, act_ref, das_ref, da_ref, columns_ref):
    width = x.shape[1]
    scale, raw = project(x, gain, wi, xg_ref, step)
    delta = jnp.zeros(raw.shape, F32)
    for c in range(0, width, step):
        delta += nt(wo[:, c : c + step], g[:, c : c + step])
    row = as_row(scale)
    pre = raw * row
    sig, slope = silu_slope(pre)
    da = (delta * slope).astype(BF16)
    daf = da.astype(F32)
    inner = jnp.sum(daf * pre, axis=0, keepdims=True) * (1.0 / width)
    act_ref[...] = (pre * sig).astype(BF16)
    das_ref[...] = (daf * row).astype(BF16)
    da_ref[...] = da
    square = columns_ref.shape[1:]
    columns_ref[0] = jnp.broadcast_to(scale, square)
    columns_ref[1] = jnp.transpose(jnp.broadcast_to(inner * row * row, square))


def outgoing_kernel(step, x, g, gain, wi, da_ref, columns_ref, flow_ref):
    da = da_ref[...]
    scale = columns_ref[0][:, 0:1]
    pull = columns_ref[1][:, 0:1]
    for c in range(0, x.shape[1], step):
        cols = slice(c, c + step)
        dn = tn(da, wi[:, cols]) * gain[:, cols]
        flow = g[:, cols].astype(F32) + scale * dn - pull * x[:, cols].astype(F32)
        flow_ref[:, cols] = flow.astype(BF16)


def terms1_kernel(index_ref, g, xg_ref, act_ref, das_ref, _, keep_out, send_out, keep_in, send_in):
    fill(index_ref[0], act_ref[...], g, keep_out, send_out)
    fill(index_ref[0], das_ref[...], xg_ref, keep_in, send_in)


def terms_kernel(
    index_ref, flow_ref, act0_ref, keep_out1, send_out1, keep_in1, send_in1, keep_ref, send_ref
):
    fill(index_ref[0], act0_ref[...], flow_ref, keep_ref, send_ref)
    chips = keep_in1.shape[0]
    keep_ref[chips : 2 * chips] = keep_out1[...]
    send_ref[chips : 2 * chips] = send_out1[...]
    keep_ref[2 * chips : 3 * chips] = keep_in1[...]
    send_ref[2 * chips : 3 * chips] = send_in1[...]


def pick_kernel(place_ref, index_ref, w_out, out_ref, sems):
    half = out_ref.shape[1]
    cols = pl.ds(pl.multiple_of((index_ref[0] % 2) * half, half), half)
    copy = pltpu.make_async_copy(w_out.at[0, place_ref[0], :, cols], out_ref, sems.at[0])
    copy.start()
    copy.wait()


def product(step, number, w_ref, flow_ref):
    half = w_ref.shape[1]
    delta = jnp.zeros((w_ref.shape[0], flow_ref.shape[0]), F32)
    for c in range(0, half, step):
        cols = pl.ds(pl.multiple_of(number * half + c, step), step)
        delta += nt(w_ref[:, c : c + step], flow_ref[:, cols])
    return delta


def flow_kernel(step, index_ref, flow_ref, own_ref, part_ref):
    part_ref[...] = product(step, index_ref[0] % 2, own_ref, flow_ref)


def flow_rest_kernel(step, index_ref, flow_ref, other_ref, part_ref, send_ref):
    rest = product(step, 1 - index_ref[0] % 2, other_ref, flow_ref)
    send_ref[...] = (part_ref[...] + rest).astype(BF16)


def lower_kernel(index_ref, xg0_ref, low_ref, got_ref, keep_ref, send_ref):
    da = (got_ref[...].astype(F32) * low_ref[0]).astype(BF16)
    das = (da.astype(F32) * low_ref[1]).astype(BF16)
    fill(index_ref[0], das, xg0_ref, keep_ref, send_ref)


def chip_kernel(place_ref, index_ref, keep, got, _, sum_ref, across):
    for i in range(keep.shape[0]):
        sum_ref[i] = (keep[i].astype(F32) + got[i].astype(F32)).astype(BF16)
    row = (index_ref[0] // 2) % 2
    first = (1 - place_ref[0]) * (2 * across.shape[0]) + 1 - row
    for i in range(across.shape[0]):
        across[i] = sum_ref[first + 2 * i]


def plane_kernel(
    place_ref, index_ref, sums, keep0, got0, own_ref, first_ref, second_ref, across
):
    rank = keep0.shape[1]
    chips = keep0.shape[0]
    row = (index_ref[0] // 2) % 2

    def terms_in(section, block):
        if section == 0:
            return (keep0[block].astype(F32) + got0[block].astype(F32)).astype(BF16)
        return sums[2 * chips + block]

    def order(near, along_x, along_y):
        far = 1 - near
        for i in range(own_ref.shape[0]):
            across[i] = terms_in(far, 2 * i + 1 - row)
            for to_ref, section, number in (
                (along_x, far, row),
                (along_y, near, 1 - row),
                (own_ref, near, row),
            ):
                block = 2 * i + number
                to_ref[i, 0:rank] = terms_in(section, block)
                to_ref[i, rank : 2 * rank] = sums[section * chips + block]

    for place in range(2):
        for core, ways in ((0, (second_ref, first_ref)), (1, (first_ref, second_ref))):
            pl.when((place_ref[0] == place) & (index_ref[0] % 2 == core))(
                partial(order, place, *ways)
            )


def add_kernel(own, across_out, out_ref):
    rank = across_out.shape[1]
    out_ref[:, 0:rank] = own[:, 0:rank]
    for i in range(own.shape[0]):
        total = own[i, rank : 2 * rank].astype(F32) + across_out[i].astype(F32)
        out_ref[i, rank : 2 * rank] = total.astype(BF16)


def layer_kernel(index_ref, own, first, across_in, second, *out_refs):
    rank = across_in.shape[1]
    layer = index_ref[0] // 4
    for k, out_ref in enumerate(out_refs):
        block = layer ^ k
        total = sum(ref[block].astype(F32) for ref in (own, first, second))
        out_ref[0:rank] = (total[0:rank] + across_in[block].astype(F32)).astype(BF16)
        out_ref[rank : 2 * rank] = total[rank : 2 * rank].astype(BF16)


def total_kernel(*refs):
    *got, in_far, out_far, in_ref, out_ref, sems = refs
    rank = in_ref.shape[1]
    copies = []
    for i, (ref, far) in enumerate(((in_ref, in_far), (out_ref, out_far))):
        ref[0] = sum(part[i * rank : (i + 1) * rank].astype(F32) for part in got)
        copies.append(pltpu.make_async_copy(ref, far, sems.at[i]))
        copies[i].start()
    for copy in copies:
        copy.wait()


def local(kernel, name, out_shapes, *operands, scratch=(), cost=None, out="near"):
    spaces = {"scalar": pltpu.SMEM, "far": pltpu.HBM, "near": pltpu.VMEM}
    out = pl.pallas_call(
        kernel,
        in_specs=[pl.BlockSpec(memory_space=spaces[kind]) for kind, _ in operands],
        out_specs=[pl.BlockSpec(memory_space=spaces[out])] * len(out_shapes),
        out_shape=[jax.ShapeDtypeStruct(shape, dtype) for shape, dtype in out_shapes],
        scratch_shapes=list(scratch),
        compiler_params=pltpu.CompilerParams(vmem_limit_bytes=VMEM_BYTES),
        cost_estimate=cost,
        name=name,
    )(*[array for _, array in operands])
    return out if len(out) > 1 else out[0]


def near(*arrays):
    return [("near", array) for array in arrays]


def pair_on_device(saved, top_grad, gains, adapter_in, adapter_out):
    count = lax.axis_size("dp")
    tokens, width = saved.shape[2:]
    rank = adapter_in.shape[3]
    share = width // count
    chips, layers = count // 2, count // 4
    place = ("scalar", lax.axis_index("section").astype(jnp.int32)[None])
    index = ("scalar", lax.axis_index("dp").astype(jnp.int32)[None])
    saved, top, gains, w_in, w_out = [
        ("far", pltpu.with_memory_space_constraint(a, pltpu.HBM))
        for a in (saved, top_grad, gains, jnp.swapaxes(adapter_in, 2, 3), adapter_out)
    ]

    def swapped(array, *ways):
        pairs = []
        for s in range(2):
            for d in range(count):
                over_section, bits = ways[d % len(ways)]
                pairs.append((s * count + d, (s ^ over_section) * count + (d ^ bits)))
        return lax.ppermute(array, ("section", "dp"), pairs)

    sems = pltpu.SemaphoreType.DMA
    wide = ((tokens, width), BF16)
    thin = ((rank, width), BF16)
    gain = ((1, width), F32)
    small = ((rank, tokens), BF16)
    one = ((chips, rank, share), BF16)
    three = ((3 * chips, rank, share), BF16)
    quarter = ((layers, rank, share), BF16)
    double = ((layers, 2 * rank, share), BF16)
    along_x, other_core = (1, 0), (0, 1)

    mine = local(
        pick_kernel, "pick", [((rank, width // 2), BF16)], place, index, w_out, scratch=[sems((1,))]
    )
    own_half = swapped(mine, along_x)
    act0, low, xg0, x1, g, gain1, wi1, wo1 = local(
        partial(front_kernel, share), "front",
        [small, ((2, rank, tokens), F32), wide, wide, wide, gain, thin, thin],
        place, saved, top, gains, w_in, w_out,
        scratch=[pltpu.VMEM(*wide), pltpu.VMEM(*gain), pltpu.VMEM(*thin), sems((8,))],
    )
    got_act0 = swapped(act0, along_x)
    xg1, act1, das1, da1, columns = local(
        partial(upper_kernel, share), "upper",
        [wide, small, small, small, ((2, tokens, tokens), F32)],
        *near(x1, g, gain1, wi1, wo1),
    )
    own_half, da1 = lax.optimization_barrier((own_half, da1))
    other_half = swapped(own_half, other_core)
    flow = local(
        partial(outgoing_kernel, share), "outgoing", [wide], *near(x1, g, gain1, wi1, da1, columns),
        cost=LONG,
    )
    part = local(
        partial(flow_kernel, share), "flow", [((rank, tokens), F32)], index, *near(flow, own_half)
    )
    delta = local(
        partial(flow_rest_kernel, share), "flow_rest", [small],
        index, *near(flow, other_half, part),
    )
    got_delta = swapped(delta, along_x)
    terms1 = local(
        terms1_kernel, "terms1", [one] * 4, index, *near(g, xg1, act1, das1, delta)
    )
    keep, send = local(
        terms_kernel, "terms", [three, three], index, *near(flow, got_act0, *terms1)
    )
    got = swapped(send, other_core)
    keep0, send0 = local(
        lower_kernel, "lower", [one, one], index, *near(xg0, low, got_delta), cost=LONG
    )
    got0 = swapped(send0, other_core)
    sums, across_out = local(
        chip_kernel, "chip", [three, quarter], place, index, *near(keep, got, keep0)
    )
    across_out = swapped(across_out, (1, 2))
    own, first, second, across_in = local(
        plane_kernel, "plane", [double, double, double, quarter],
        place, index, *near(sums, keep0, got0),
    )
    first = swapped(first, (0, 2), (1, 0))
    across_in = swapped(across_in, (1, 2))
    second = swapped(second, (1, 0), (0, 2))
    own = local(add_kernel, "add", [double], *near(own, across_out), cost=LONG)
    mine, *others = local(
        layer_kernel, "layer", [((2 * rank, share), BF16)] * layers,
        index, *near(own, first, across_in, second),
    )
    others = [swapped(other, (0, 4 * k)) for k, other in enumerate(others, 1)]
    others = others[1:] + others[:1]
    block = ((1, rank, share), F32)
    total_in, total_out = local(
        total_kernel, "total", [block, block], *near(mine, *others),
        scratch=[pltpu.VMEM(*block), pltpu.VMEM(*block), sems((2,))], out="far",
    )
    return (jnp.swapaxes(total_in, 1, 2), total_out)


def section_back(x, gain, weight_in, weight_out, upstream):
    xf = x.astype(F32)
    scale = lax.rsqrt(jnp.mean(xf * xf, axis=-1, keepdims=True) + EPS)
    normed = xf * scale
    hidden = (normed * gain).astype(BF16)
    pre = jnp.dot(hidden, weight_in, preferred_element_type=F32)
    sig, slope = silu_slope(pre)
    active = (pre * sig).astype(BF16)
    delta_act = jnp.dot(upstream, weight_out.T, preferred_element_type=F32)
    delta_pre = (delta_act * slope).astype(BF16)
    delta_norm = jnp.dot(delta_pre, weight_in.T, preferred_element_type=F32) * gain
    inner = jnp.mean(delta_norm * normed, axis=-1, keepdims=True)
    result = (upstream.astype(F32) + scale * (delta_norm - normed * inner)).astype(BF16)
    term_in = jnp.dot(hidden.T, delta_pre, preferred_element_type=F32)
    term_out = jnp.dot(active.T, upstream, preferred_element_type=F32)
    return (result, term_in, term_out)


def relay_on_device(saved, top_grad, gains, adapter_in, adapter_out):
    sections = lax.axis_size("section")
    place = lax.axis_index("section")
    width = top_grad.shape[2]
    rank = adapter_in.shape[3]
    zero_in = jnp.zeros((width, rank), F32)
    zero_out = jnp.zeros((rank, width), F32)

    def step(turn, flows, sums):
        leaving, added = [], []
        for replica in (0, 1):
            serves = place == (sections - 1 - turn if replica == 0 else turn)
            result, term_in, term_out = lax.cond(
                serves,
                partial(
                    section_back,
                    saved[0, replica],
                    gains[0, replica],
                    adapter_in[0, replica],
                    adapter_out[0, replica],
                ),
                lambda flow: (flow, zero_in, zero_out),
                flows[replica],
            )
            leaving.append(result)
            added += [sums[2 * replica] + term_in, sums[2 * replica + 1] + term_out]
        return leaving, added

    down = [(i, i - 1) for i in range(1, sections)]
    up = [(i, i + 1) for i in range(sections - 1)]

    def turn_and_pass(turn, carry):
        leaving, sums = step(turn, carry[0], carry[1])
        return (
            [lax.ppermute(leaving[0], "section", down), lax.ppermute(leaving[1], "section", up)],
            sums,
        )

    start = ([top_grad[0], top_grad[1]], [zero_in, zero_out, zero_in, zero_out])
    flows, sums = lax.fori_loop(0, sections - 1, turn_and_pass, start)
    _, sums = step(sections - 1, flows, sums)
    shares = [
        lax.psum_scatter(term, "dp", scatter_dimension=i % 2, tiled=True)
        for i, term in enumerate(sums)
    ]
    mirror = [(i, sections - 1 - i) for i in range(sections)]
    total_in = shares[0] + lax.ppermute(shares[2], "section", mirror)
    total_out = shares[1] + lax.ppermute(shares[3], "section", mirror)
    return (total_in[None], total_out[None])


def solution(mesh):
    in_specs = (
        P("section", None, "dp", None),
        P(None, "dp", None),
        P("section", None, None),
        P("section", None, None, None),
        P("section", None, None, None),
    )
    out_specs = (P("section", "dp", None), P("section", None, "dp"))

    def run(saved, *others):
        share = saved.shape[3] // mesh.shape["dp"]
        count = mesh.shape["dp"]
        pair = mesh.shape["section"] == 2 and share % 128 == 0
        pair = pair and count >= 4 and count & (count - 1) == 0
        on_device = pair_on_device if pair else relay_on_device
        return jax.shard_map(
            on_device, mesh=mesh, in_specs=in_specs, out_specs=out_specs, check_vma=False
        )(saved, *others)

    return run
```

```python
from functools import partial

import jax
import jax.numpy as jnp
from jax import lax
from jax.experimental import pallas as pl
from jax.experimental.pallas import tpu as pltpu
from jax.sharding import PartitionSpec as P

EPS = 1e-05
VMEM_BYTES = 24 * 1024 * 1024
F32 = jnp.float32
BF16 = jnp.bfloat16


MEDIUM = pl.CostEstimate(flops=10**9, bytes_accessed=2**20, transcendentals=0)
LONG = pl.CostEstimate(flops=2 * 10**10, bytes_accessed=2**20, transcendentals=0)


def nn(a, b):
    return lax.dot_general(a, b, (((1,), (0,)), ((), ())), preferred_element_type=F32)


def nt(a, b):
    return lax.dot_general(a, b, (((1,), (1,)), ((), ())), preferred_element_type=F32)


def tn(a, b):
    return lax.dot_general(a, b, (((0,), (0,)), ((), ())), preferred_element_type=F32)


def as_row(column):
    count = column.shape[0]
    return jnp.transpose(jnp.broadcast_to(column, (count, count)))[0:1, :]


def silu_slope(pre):
    sig = jax.nn.sigmoid(pre)
    return sig, sig * (1.0 + pre * (1.0 - sig))


def project(x_ref, gain_ref, w_ref, xg_ref, step):
    tokens, width = x_ref.shape
    squares = jnp.zeros((tokens, 128), F32)
    pre = jnp.zeros((w_ref.shape[0], tokens), F32)
    for c in range(0, width, step):
        x = x_ref[:, c : c + step].astype(F32)
        for k in range(0, step, 128):
            part = x[:, k : k + 128]
            squares += part * part
        xg = (x * gain_ref[:, c : c + step]).astype(BF16)
        xg_ref[:, c : c + step] = xg
        pre += nt(w_ref[:, c : c + step], xg)
    mean = jnp.sum(squares, axis=1, keepdims=True) * (1.0 / width)
    scale = lax.rsqrt(mean + EPS)
    return scale, pre


def fill(index, matrix, wide_ref, keep_ref, send_ref):
    share = keep_ref.shape[2]
    core = index % 2
    for i in range(wide_ref.shape[1] // share // 2):
        for to_ref, number in ((keep_ref, core), (send_ref, 1 - core)):
            cols = pl.ds(pl.multiple_of((2 * i + number) * share, share), share)
            to_ref[i] = nn(matrix, wide_ref[:, cols]).astype(BF16)


def front_kernel(
    step, place_ref, saved, top, gains, w_in, w_out,
    act0_ref, low_ref, xg0_ref, x1, g, gain1, wi1, wo1,
    x0, gain0, wi0, sems,
):
    lower = place_ref[0]
    upper = 1 - lower
    copies = [
        (gains.at[0, pl.ds(lower, 1)], gain0),
        (w_in.at[0, lower], wi0),
        (saved.at[0, lower], x0),
        (gains.at[0, pl.ds(upper, 1)], gain1),
        (w_in.at[0, upper], wi1),
        (saved.at[0, upper], x1),
        (w_out.at[0, upper], wo1),
        (top.at[upper], g),
    ]
    copies = [pltpu.make_async_copy(a, b, sems.at[i]) for i, (a, b) in enumerate(copies)]
    for copy in copies:
        copy.start()
    for copy in copies[0:3]:
        copy.wait()
    scale, raw = project(x0, gain0, wi0, xg0_ref, step)
    row = as_row(scale)
    pre = raw * row
    sig, slope = silu_slope(pre)
    act0_ref[...] = (pre * sig).astype(BF16)
    low_ref[0] = slope
    low_ref[1] = jnp.broadcast_to(row, raw.shape)
    for copy in copies[3:8]:
        copy.wait()


def upper_kernel(step, x, g, gain, wi, wo, xg_ref, act_ref, das_ref, da_ref, columns_ref):
    width = x.shape[1]
    scale, raw = project(x, gain, wi, xg_ref, step)
    delta = jnp.zeros(raw.shape, F32)
    for c in range(0, width, step):
        delta += nt(wo[:, c : c + step], g[:, c : c + step])
    row = as_row(scale)
    pre = raw * row
    sig, slope = silu_slope(pre)
    da = (delta * slope).astype(BF16)
    daf = da.astype(F32)
    inner = jnp.sum(daf * pre, axis=0, keepdims=True) * (1.0 / width)
    act_ref[...] = (pre * sig).astype(BF16)
    das_ref[...] = (daf * row).astype(BF16)
    da_ref[...] = da
    square = columns_ref.shape[1:]
    columns_ref[0] = jnp.broadcast_to(scale, square)
    columns_ref[1] = jnp.transpose(jnp.broadcast_to(inner * row * row, square))


def outgoing_kernel(step, x, g, gain, wi, da_ref, columns_ref, flow_ref):
    da = da_ref[...]
    scale = columns_ref[0][:, 0:1]
    pull = columns_ref[1][:, 0:1]
    for c in range(0, x.shape[1], step):
        cols = slice(c, c + step)
        dn = tn(da, wi[:, cols]) * gain[:, cols]
        flow = g[:, cols].astype(F32) + scale * dn - pull * x[:, cols].astype(F32)
        flow_ref[:, cols] = flow.astype(BF16)


def terms1_kernel(index_ref, g, xg_ref, act_ref, das_ref, _, keep_out, send_out, keep_in, send_in):
    fill(index_ref[0], act_ref[...], g, keep_out, send_out)
    fill(index_ref[0], das_ref[...], xg_ref, keep_in, send_in)


def terms_kernel(
    index_ref, flow_ref, act0_ref, keep_out1, send_out1, keep_in1, send_in1, keep_ref, send_ref
):
    fill(index_ref[0], act0_ref[...], flow_ref, keep_ref, send_ref)
    chips = keep_in1.shape[0]
    keep_ref[chips : 2 * chips] = keep_out1[...]
    send_ref[chips : 2 * chips] = send_out1[...]
    keep_ref[2 * chips : 3 * chips] = keep_in1[...]
    send_ref[2 * chips : 3 * chips] = send_in1[...]


def pick_kernel(place_ref, index_ref, w_out, out_ref, sems):
    half = out_ref.shape[1]
    cols = pl.ds(pl.multiple_of((index_ref[0] % 2) * half, half), half)
    copy = pltpu.make_async_copy(w_out.at[0, place_ref[0], :, cols], out_ref, sems.at[0])
    copy.start()
    copy.wait()


def product(step, number, w_ref, flow_ref):
    half = w_ref.shape[1]
    delta = jnp.zeros((w_ref.shape[0], flow_ref.shape[0]), F32)
    for c in range(0, half, step):
        cols = pl.ds(pl.multiple_of(number * half + c, step), step)
        delta += nt(w_ref[:, c : c + step], flow_ref[:, cols])
    return delta


def flow_kernel(step, index_ref, flow_ref, own_ref, part_ref):
    part_ref[...] = product(step, index_ref[0] % 2, own_ref, flow_ref)


def flow_rest_kernel(step, index_ref, flow_ref, other_ref, part_ref, send_ref):
    rest = product(step, 1 - index_ref[0] % 2, other_ref, flow_ref)
    send_ref[...] = (part_ref[...] + rest).astype(BF16)


def lower_kernel(index_ref, xg0_ref, low_ref, got_ref, keep_ref, send_ref):
    da = (got_ref[...].astype(F32) * low_ref[0]).astype(BF16)
    das = (da.astype(F32) * low_ref[1]).astype(BF16)
    fill(index_ref[0], das, xg0_ref, keep_ref, send_ref)


def chip_kernel(place_ref, index_ref, keep, got, _, sum_ref, across):
    for i in range(keep.shape[0]):
        sum_ref[i] = (keep[i].astype(F32) + got[i].astype(F32)).astype(BF16)
    row = (index_ref[0] // 2) % 2
    first = (1 - place_ref[0]) * (2 * across.shape[0]) + 1 - row
    for i in range(across.shape[0]):
        across[i] = sum_ref[first + 2 * i]


def plane_kernel(
    place_ref, index_ref, sums, keep0, got0, own_ref, first_ref, second_ref, across
):
    rank = keep0.shape[1]
    chips = keep0.shape[0]
    row = (index_ref[0] // 2) % 2

    def terms_in(section, block):
        if section == 0:
            return (keep0[block].astype(F32) + got0[block].astype(F32)).astype(BF16)
        return sums[2 * chips + block]

    def order(near, along_x, along_y):
        far = 1 - near
        for i in range(own_ref.shape[0]):
            across[i] = terms_in(far, 2 * i + 1 - row)
            for to_ref, section, number in (
                (along_x, far, row),
                (along_y, near, 1 - row),
                (own_ref, near, row),
            ):
                block = 2 * i + number
                to_ref[i, 0:rank] = terms_in(section, block)
                to_ref[i, rank : 2 * rank] = sums[section * chips + block]

    for place in range(2):
        for core, ways in ((0, (second_ref, first_ref)), (1, (first_ref, second_ref))):
            pl.when((place_ref[0] == place) & (index_ref[0] % 2 == core))(
                partial(order, place, *ways)
            )


def add_kernel(own, across_out, out_ref):
    rank = across_out.shape[1]
    out_ref[:, 0:rank] = own[:, 0:rank]
    for i in range(own.shape[0]):
        total = own[i, rank : 2 * rank].astype(F32) + across_out[i].astype(F32)
        out_ref[i, rank : 2 * rank] = total.astype(BF16)


def layer_kernel(index_ref, own, first, across_in, second, *out_refs):
    rank = across_in.shape[1]
    layer = index_ref[0] // 4
    for k, out_ref in enumerate(out_refs):
        block = layer ^ k
        total = sum(ref[block].astype(F32) for ref in (own, first, second))
        out_ref[0:rank] = (total[0:rank] + across_in[block].astype(F32)).astype(BF16)
        out_ref[rank : 2 * rank] = total[rank : 2 * rank].astype(BF16)


def total_kernel(*refs):
    *got, in_far, out_far, in_ref, out_ref, sems = refs
    rank = in_ref.shape[1]
    copies = []
    for i, (ref, far) in enumerate(((in_ref, in_far), (out_ref, out_far))):
        ref[0] = sum(part[i * rank : (i + 1) * rank].astype(F32) for part in got)
        copies.append(pltpu.make_async_copy(ref, far, sems.at[i]))
        copies[i].start()
    for copy in copies:
        copy.wait()


def local(kernel, name, out_shapes, *operands, scratch=(), cost=None, out="near"):
    spaces = {"scalar": pltpu.SMEM, "far": pltpu.HBM, "near": pltpu.VMEM}
    out = pl.pallas_call(
        kernel,
        in_specs=[pl.BlockSpec(memory_space=spaces[kind]) for kind, _ in operands],
        out_specs=[pl.BlockSpec(memory_space=spaces[out])] * len(out_shapes),
        out_shape=[jax.ShapeDtypeStruct(shape, dtype) for shape, dtype in out_shapes],
        scratch_shapes=list(scratch),
        compiler_params=pltpu.CompilerParams(vmem_limit_bytes=VMEM_BYTES),
        cost_estimate=cost,
        name=name,
    )(*[array for _, array in operands])
    return out if len(out) > 1 else out[0]


def near(*arrays):
    return [("near", array) for array in arrays]


def pair_on_device(saved, top_grad, gains, adapter_in, adapter_out):
    count = lax.axis_size("dp")
    tokens, width = saved.shape[2:]
    rank = adapter_in.shape[3]
    share = width // count
    chips, layers = count // 2, count // 4
    place = ("scalar", lax.axis_index("section").astype(jnp.int32)[None])
    index = ("scalar", lax.axis_index("dp").astype(jnp.int32)[None])
    saved, top, gains, w_in, w_out = [
        ("far", pltpu.with_memory_space_constraint(a, pltpu.HBM))
        for a in (saved, top_grad, gains, jnp.swapaxes(adapter_in, 2, 3), adapter_out)
    ]

    def swapped(array, *ways):
        pairs = []
        for s in range(2):
            for d in range(count):
                over_section, bits = ways[d % len(ways)]
                pairs.append((s * count + d, (s ^ over_section) * count + (d ^ bits)))
        return lax.ppermute(array, ("section", "dp"), pairs)

    sems = pltpu.SemaphoreType.DMA
    wide = ((tokens, width), BF16)
    thin = ((rank, width), BF16)
    gain = ((1, width), F32)
    small = ((rank, tokens), BF16)
    one = ((chips, rank, share), BF16)
    three = ((3 * chips, rank, share), BF16)
    quarter = ((layers, rank, share), BF16)
    double = ((layers, 2 * rank, share), BF16)
    along_x, other_core = (1, 0), (0, 1)

    mine = local(
        pick_kernel, "pick", [((rank, width // 2), BF16)], place, index, w_out, scratch=[sems((1,))]
    )
    own_half = swapped(mine, along_x)
    act0, low, xg0, x1, g, gain1, wi1, wo1 = local(
        partial(front_kernel, share), "front",
        [small, ((2, rank, tokens), F32), wide, wide, wide, gain, thin, thin],
        place, saved, top, gains, w_in, w_out,
        scratch=[pltpu.VMEM(*wide), pltpu.VMEM(*gain), pltpu.VMEM(*thin), sems((8,))],
    )
    got_act0 = swapped(act0, along_x)
    xg1, act1, das1, da1, columns = local(
        partial(upper_kernel, share), "upper",
        [wide, small, small, small, ((2, tokens, tokens), F32)],
        *near(x1, g, gain1, wi1, wo1),
    )
    own_half, da1 = lax.optimization_barrier((own_half, da1))
    other_half = swapped(own_half, other_core)
    flow = local(
        partial(outgoing_kernel, share), "outgoing", [wide], *near(x1, g, gain1, wi1, da1, columns),
        cost=LONG,
    )
    part = local(
        partial(flow_kernel, share), "flow", [((rank, tokens), F32)], index, *near(flow, own_half)
    )
    delta = local(
        partial(flow_rest_kernel, share), "flow_rest", [small],
        index, *near(flow, other_half, part),
    )
    got_delta = swapped(delta, along_x)
    terms1 = local(
        terms1_kernel, "terms1", [one] * 4, index, *near(g, xg1, act1, das1, delta)
    )
    keep, send = local(
        terms_kernel, "terms", [three, three], index, *near(flow, got_act0, *terms1)
    )
    got = swapped(send, other_core)
    keep0, send0 = local(
        lower_kernel, "lower", [one, one], index, *near(xg0, low, got_delta), cost=LONG
    )
    got0 = swapped(send0, other_core)
    sums, across_out = local(
        chip_kernel, "chip", [three, quarter], place, index, *near(keep, got, keep0)
    )
    across_out = swapped(across_out, (1, 2))
    own, first, second, across_in = local(
        plane_kernel, "plane", [double, double, double, quarter],
        place, index, *near(sums, keep0, got0),
    )
    first = swapped(first, (0, 2), (1, 0))
    across_in = swapped(across_in, (1, 2))
    second = swapped(second, (1, 0), (0, 2))
    own = local(add_kernel, "add", [double], *near(own, across_out), cost=MEDIUM)
    mine, *others = local(
        layer_kernel, "layer", [((2 * rank, share), BF16)] * layers,
        index, *near(own, first, across_in, second),
    )
    others = [swapped(other, (0, 4 * k)) for k, other in enumerate(others, 1)]
    others = others[1:] + others[:1]
    block = ((1, rank, share), F32)
    total_in, total_out = local(
        total_kernel, "total", [block, block], *near(mine, *others),
        scratch=[pltpu.VMEM(*block), pltpu.VMEM(*block), sems((2,))], out="far",
    )
    return (jnp.swapaxes(total_in, 1, 2), total_out)


def section_back(x, gain, weight_in, weight_out, upstream):
    xf = x.astype(F32)
    scale = lax.rsqrt(jnp.mean(xf * xf, axis=-1, keepdims=True) + EPS)
    normed = xf * scale
    hidden = (normed * gain).astype(BF16)
    pre = jnp.dot(hidden, weight_in, preferred_element_type=F32)
    sig, slope = silu_slope(pre)
    active = (pre * sig).astype(BF16)
    delta_act = jnp.dot(upstream, weight_out.T, preferred_element_type=F32)
    delta_pre = (delta_act * slope).astype(BF16)
    delta_norm = jnp.dot(delta_pre, weight_in.T, preferred_element_type=F32) * gain
    inner = jnp.mean(delta_norm * normed, axis=-1, keepdims=True)
    result = (upstream.astype(F32) + scale * (delta_norm - normed * inner)).astype(BF16)
    term_in = jnp.dot(hidden.T, delta_pre, preferred_element_type=F32)
    term_out = jnp.dot(active.T, upstream, preferred_element_type=F32)
    return (result, term_in, term_out)


def relay_on_device(saved, top_grad, gains, adapter_in, adapter_out):
    sections = lax.axis_size("section")
    place = lax.axis_index("section")
    width = top_grad.shape[2]
    rank = adapter_in.shape[3]
    zero_in = jnp.zeros((width, rank), F32)
    zero_out = jnp.zeros((rank, width), F32)

    def step(turn, flows, sums):
        leaving, added = [], []
        for replica in (0, 1):
            serves = place == (sections - 1 - turn if replica == 0 else turn)
            result, term_in, term_out = lax.cond(
                serves,
                partial(
                    section_back,
                    saved[0, replica],
                    gains[0, replica],
                    adapter_in[0, replica],
                    adapter_out[0, replica],
                ),
                lambda flow: (flow, zero_in, zero_out),
                flows[replica],
            )
            leaving.append(result)
            added += [sums[2 * replica] + term_in, sums[2 * replica + 1] + term_out]
        return leaving, added

    down = [(i, i - 1) for i in range(1, sections)]
    up = [(i, i + 1) for i in range(sections - 1)]

    def turn_and_pass(turn, carry):
        leaving, sums = step(turn, carry[0], carry[1])
        return (
            [lax.ppermute(leaving[0], "section", down), lax.ppermute(leaving[1], "section", up)],
            sums,
        )

    start = ([top_grad[0], top_grad[1]], [zero_in, zero_out, zero_in, zero_out])
    flows, sums = lax.fori_loop(0, sections - 1, turn_and_pass, start)
    _, sums = step(sections - 1, flows, sums)
    shares = [
        lax.psum_scatter(term, "dp", scatter_dimension=i % 2, tiled=True)
        for i, term in enumerate(sums)
    ]
    mirror = [(i, sections - 1 - i) for i in range(sections)]
    total_in = shares[0] + lax.ppermute(shares[2], "section", mirror)
    total_out = shares[1] + lax.ppermute(shares[3], "section", mirror)
    return (total_in[None], total_out[None])


def solution(mesh):
    in_specs = (
        P("section", None, "dp", None),
        P(None, "dp", None),
        P("section", None, None),
        P("section", None, None, None),
        P("section", None, None, None),
    )
    out_specs = (P("section", "dp", None), P("section", None, "dp"))

    def run(saved, *others):
        share = saved.shape[3] // mesh.shape["dp"]
        count = mesh.shape["dp"]
        pair = mesh.shape["section"] == 2 and share % 128 == 0
        pair = pair and count >= 4 and count & (count - 1) == 0
        on_device = pair_on_device if pair else relay_on_device
        return jax.shard_map(
            on_device, mesh=mesh, in_specs=in_specs, out_specs=out_specs, check_vma=False
        )(saved, *others)

    return run
```

```python
from functools import partial

import jax
import jax.numpy as jnp
from jax import lax
from jax.experimental import pallas as pl
from jax.experimental.pallas import tpu as pltpu
from jax.sharding import PartitionSpec as P

EPS = 1e-05
VMEM_BYTES = 24 * 1024 * 1024
F32 = jnp.float32
BF16 = jnp.bfloat16


MEDIUM = pl.CostEstimate(flops=10**9, bytes_accessed=2**20, transcendentals=0)
LONG = pl.CostEstimate(flops=2 * 10**10, bytes_accessed=2**20, transcendentals=0)


def nn(a, b):
    return lax.dot_general(a, b, (((1,), (0,)), ((), ())), preferred_element_type=F32)


def nt(a, b):
    return lax.dot_general(a, b, (((1,), (1,)), ((), ())), preferred_element_type=F32)


def tn(a, b):
    return lax.dot_general(a, b, (((0,), (0,)), ((), ())), preferred_element_type=F32)


def as_row(column):
    count = column.shape[0]
    return jnp.transpose(jnp.broadcast_to(column, (count, count)))[0:1, :]


def silu_slope(pre):
    sig = jax.nn.sigmoid(pre)
    return sig, sig * (1.0 + pre * (1.0 - sig))


PIECES = 4


def pieces(source, target, sems, first):
    step = target.shape[-1] // PIECES
    copies = []
    for i in range(PIECES):
        cols = pl.ds(i * step, step)
        copies.append(
            pltpu.make_async_copy(source.at[:, cols], target.at[:, cols], sems.at[first + i])
        )
    return copies


def project(x_ref, gain_ref, w_ref, xg_ref, step, copies=()):
    tokens, width = x_ref.shape
    squares = jnp.zeros((tokens, 128), F32)
    pre = jnp.zeros((w_ref.shape[0], tokens), F32)
    for c in range(0, width, step):
        if copies and c % (width // len(copies)) == 0:
            copies[c * len(copies) // width].wait()
        x = x_ref[:, c : c + step].astype(F32)
        for k in range(0, step, 128):
            part = x[:, k : k + 128]
            squares += part * part
        xg = (x * gain_ref[:, c : c + step]).astype(BF16)
        xg_ref[:, c : c + step] = xg
        pre += nt(w_ref[:, c : c + step], xg)
    mean = jnp.sum(squares, axis=1, keepdims=True) * (1.0 / width)
    scale = lax.rsqrt(mean + EPS)
    return scale, pre


def fill(index, matrix, wide_ref, keep_ref, send_ref):
    share = keep_ref.shape[2]
    core = index % 2
    for i in range(wide_ref.shape[1] // share // 2):
        for to_ref, number in ((keep_ref, core), (send_ref, 1 - core)):
            cols = pl.ds(pl.multiple_of((2 * i + number) * share, share), share)
            to_ref[i] = nn(matrix, wide_ref[:, cols]).astype(BF16)


def front_kernel(
    step, place_ref, saved, top, gains, w_in, w_out,
    act0_ref, low_ref, xg0_ref, x1, g, gain1, wi1, wo1,
    x0, gain0, wi0, sems,
):
    lower = place_ref[0]
    upper = 1 - lower
    copies = [
        (gains.at[0, pl.ds(lower, 1)], gain0),
        (w_in.at[0, lower], wi0),
        (gains.at[0, pl.ds(upper, 1)], gain1),
        (w_in.at[0, upper], wi1),
        (w_out.at[0, upper], wo1),
    ]
    copies = [pltpu.make_async_copy(a, b, sems.at[i]) for i, (a, b) in enumerate(copies)]
    first = len(copies)
    copies_x0 = pieces(saved.at[0, lower], x0, sems, first)
    others = pieces(saved.at[0, upper], x1, sems, first + PIECES)
    others += pieces(top.at[upper], g, sems, first + 2 * PIECES)
    for copy in copies[0:2] + copies_x0 + copies[2:5] + others:
        copy.start()
    for copy in copies[0:2]:
        copy.wait()
    scale, raw = project(x0, gain0, wi0, xg0_ref, step, copies_x0)
    row = as_row(scale)
    pre = raw * row
    sig, slope = silu_slope(pre)
    act0_ref[...] = (pre * sig).astype(BF16)
    low_ref[0] = slope
    low_ref[1] = jnp.broadcast_to(row, raw.shape)
    for copy in copies[2:5] + others:
        copy.wait()


def upper_kernel(step, x, g, gain, wi, wo, xg_ref, act_ref, das_ref, da_ref, columns_ref):
    width = x.shape[1]
    scale, raw = project(x, gain, wi, xg_ref, step)
    delta = jnp.zeros(raw.shape, F32)
    for c in range(0, width, step):
        delta += nt(wo[:, c : c + step], g[:, c : c + step])
    row = as_row(scale)
    pre = raw * row
    sig, slope = silu_slope(pre)
    da = (delta * slope).astype(BF16)
    daf = da.astype(F32)
    inner = jnp.sum(daf * pre, axis=0, keepdims=True) * (1.0 / width)
    act_ref[...] = (pre * sig).astype(BF16)
    das_ref[...] = (daf * row).astype(BF16)
    da_ref[...] = da
    square = columns_ref.shape[1:]
    columns_ref[0] = jnp.broadcast_to(scale, square)
    columns_ref[1] = jnp.transpose(jnp.broadcast_to(inner * row * row, square))


def outgoing_kernel(step, x, g, gain, wi, da_ref, columns_ref, flow_ref):
    da = da_ref[...]
    scale = columns_ref[0][:, 0:1]
    pull = columns_ref[1][:, 0:1]
    for c in range(0, x.shape[1], step):
        cols = slice(c, c + step)
        dn = tn(da, wi[:, cols]) * gain[:, cols]
        flow = g[:, cols].astype(F32) + scale * dn - pull * x[:, cols].astype(F32)
        flow_ref[:, cols] = flow.astype(BF16)


def terms1_kernel(index_ref, g, xg_ref, act_ref, das_ref, _, keep_out, send_out, keep_in, send_in):
    fill(index_ref[0], act_ref[...], g, keep_out, send_out)
    fill(index_ref[0], das_ref[...], xg_ref, keep_in, send_in)


def terms_kernel(
    index_ref, flow_ref, act0_ref, keep_out1, send_out1, keep_in1, send_in1, keep_ref, send_ref
):
    fill(index_ref[0], act0_ref[...], flow_ref, keep_ref, send_ref)
    chips = keep_in1.shape[0]
    keep_ref[chips : 2 * chips] = keep_out1[...]
    send_ref[chips : 2 * chips] = send_out1[...]
    keep_ref[2 * chips : 3 * chips] = keep_in1[...]
    send_ref[2 * chips : 3 * chips] = send_in1[...]


def pick_kernel(place_ref, index_ref, w_out, out_ref, sems):
    half = out_ref.shape[1]
    cols = pl.ds(pl.multiple_of((index_ref[0] % 2) * half, half), half)
    copies = pieces(w_out.at[0, place_ref[0], :, cols], out_ref, sems, 0)
    for copy in copies:
        copy.start()
    for copy in copies:
        copy.wait()


def product(step, number, w_ref, flow_ref):
    half = w_ref.shape[1]
    delta = jnp.zeros((w_ref.shape[0], flow_ref.shape[0]), F32)
    for c in range(0, half, step):
        cols = pl.ds(pl.multiple_of(number * half + c, step), step)
        delta += nt(w_ref[:, c : c + step], flow_ref[:, cols])
    return delta


def flow_kernel(step, index_ref, flow_ref, own_ref, part_ref):
    part_ref[...] = product(step, index_ref[0] % 2, own_ref, flow_ref)


def flow_rest_kernel(step, index_ref, flow_ref, other_ref, part_ref, send_ref):
    rest = product(step, 1 - index_ref[0] % 2, other_ref, flow_ref)
    send_ref[...] = (part_ref[...] + rest).astype(BF16)


def lower_kernel(index_ref, xg0_ref, low_ref, got_ref, keep_ref, send_ref):
    da = (got_ref[...].astype(F32) * low_ref[0]).astype(BF16)
    das = (da.astype(F32) * low_ref[1]).astype(BF16)
    fill(index_ref[0], das, xg0_ref, keep_ref, send_ref)


def chip_kernel(place_ref, index_ref, keep, got, _, sum_ref, across):
    for i in range(keep.shape[0]):
        sum_ref[i] = (keep[i].astype(F32) + got[i].astype(F32)).astype(BF16)
    row = (index_ref[0] // 2) % 2
    first = (1 - place_ref[0]) * (2 * across.shape[0]) + 1 - row
    for i in range(across.shape[0]):
        across[i] = sum_ref[first + 2 * i]


def plane_kernel(
    place_ref, index_ref, sums, keep0, got0, own_ref, first_ref, second_ref, across
):
    rank = keep0.shape[1]
    chips = keep0.shape[0]
    row = (index_ref[0] // 2) % 2

    def terms_in(section, block):
        if section == 0:
            return (keep0[block].astype(F32) + got0[block].astype(F32)).astype(BF16)
        return sums[2 * chips + block]

    def order(near, along_x, along_y):
        far = 1 - near
        for i in range(own_ref.shape[0]):
            across[i] = terms_in(far, 2 * i + 1 - row)
            for to_ref, section, number in (
                (along_x, far, row),
                (along_y, near, 1 - row),
                (own_ref, near, row),
            ):
                block = 2 * i + number
                to_ref[i, 0:rank] = terms_in(section, block)
                to_ref[i, rank : 2 * rank] = sums[section * chips + block]

    for place in range(2):
        for core, ways in ((0, (second_ref, first_ref)), (1, (first_ref, second_ref))):
            pl.when((place_ref[0] == place) & (index_ref[0] % 2 == core))(
                partial(order, place, *ways)
            )


def add_kernel(own, across_out, out_ref):
    rank = across_out.shape[1]
    out_ref[:, 0:rank] = own[:, 0:rank]
    for i in range(own.shape[0]):
        total = own[i, rank : 2 * rank].astype(F32) + across_out[i].astype(F32)
        out_ref[i, rank : 2 * rank] = total.astype(BF16)


def layer_kernel(index_ref, own, first, across_in, second, *out_refs):
    rank = across_in.shape[1]
    layer = index_ref[0] // 4
    for k, out_ref in enumerate(out_refs):
        block = layer ^ k
        total = sum(ref[block].astype(F32) for ref in (own, first, second))
        out_ref[0:rank] = (total[0:rank] + across_in[block].astype(F32)).astype(BF16)
        out_ref[rank : 2 * rank] = total[rank : 2 * rank].astype(BF16)


def total_kernel(*refs):
    *got, in_far, out_far, in_ref, out_ref, sems = refs
    rank = in_ref.shape[1]
    copies = []
    for i, (ref, far) in enumerate(((in_ref, in_far), (out_ref, out_far))):
        ref[0] = sum(part[i * rank : (i + 1) * rank].astype(F32) for part in got)
        copies.append(pltpu.make_async_copy(ref, far, sems.at[i]))
        copies[i].start()
    for copy in copies:
        copy.wait()


def local(kernel, name, out_shapes, *operands, scratch=(), cost=None, out="near"):
    spaces = {"scalar": pltpu.SMEM, "far": pltpu.HBM, "near": pltpu.VMEM}
    out = pl.pallas_call(
        kernel,
        in_specs=[pl.BlockSpec(memory_space=spaces[kind]) for kind, _ in operands],
        out_specs=[pl.BlockSpec(memory_space=spaces[out])] * len(out_shapes),
        out_shape=[jax.ShapeDtypeStruct(shape, dtype) for shape, dtype in out_shapes],
        scratch_shapes=list(scratch),
        compiler_params=pltpu.CompilerParams(vmem_limit_bytes=VMEM_BYTES),
        cost_estimate=cost,
        name=name,
    )(*[array for _, array in operands])
    return out if len(out) > 1 else out[0]


def near(*arrays):
    return [("near", array) for array in arrays]


def pair_on_device(saved, top_grad, gains, adapter_in, adapter_out):
    count = lax.axis_size("dp")
    tokens, width = saved.shape[2:]
    rank = adapter_in.shape[3]
    share = width // count
    chips, layers = count // 2, count // 4
    place = ("scalar", lax.axis_index("section").astype(jnp.int32)[None])
    index = ("scalar", lax.axis_index("dp").astype(jnp.int32)[None])
    saved, top, gains, w_in, w_out = [
        ("far", pltpu.with_memory_space_constraint(a, pltpu.HBM))
        for a in (saved, top_grad, gains, jnp.swapaxes(adapter_in, 2, 3), adapter_out)
    ]

    def swapped(array, *ways):
        pairs = []
        for s in range(2):
            for d in range(count):
                over_section, bits = ways[d % len(ways)]
                pairs.append((s * count + d, (s ^ over_section) * count + (d ^ bits)))
        return lax.ppermute(array, ("section", "dp"), pairs)

    sems = pltpu.SemaphoreType.DMA
    wide = ((tokens, width), BF16)
    thin = ((rank, width), BF16)
    gain = ((1, width), F32)
    small = ((rank, tokens), BF16)
    one = ((chips, rank, share), BF16)
    three = ((3 * chips, rank, share), BF16)
    quarter = ((layers, rank, share), BF16)
    double = ((layers, 2 * rank, share), BF16)
    along_x, other_core = (1, 0), (0, 1)

    mine = local(
        pick_kernel, "pick", [((rank, width // 2), BF16)], place, index, w_out, scratch=[sems((PIECES,))]
    )
    own_half = swapped(mine, along_x)
    act0, low, xg0, x1, g, gain1, wi1, wo1 = local(
        partial(front_kernel, share), "front",
        [small, ((2, rank, tokens), F32), wide, wide, wide, gain, thin, thin],
        place, saved, top, gains, w_in, w_out,
        scratch=[pltpu.VMEM(*wide), pltpu.VMEM(*gain), pltpu.VMEM(*thin), sems((5 + 3 * PIECES,))],
    )
    got_act0 = swapped(act0, along_x)
    xg1, act1, das1, da1, columns = local(
        partial(upper_kernel, share), "upper",
        [wide, small, small, small, ((2, tokens, tokens), F32)],
        *near(x1, g, gain1, wi1, wo1),
    )
    own_half, da1 = lax.optimization_barrier((own_half, da1))
    other_half = swapped(own_half, other_core)
    flow = local(
        partial(outgoing_kernel, share), "outgoing", [wide], *near(x1, g, gain1, wi1, da1, columns),
        cost=LONG,
    )
    part = local(
        partial(flow_kernel, share), "flow", [((rank, tokens), F32)], index, *near(flow, own_half)
    )
    delta = local(
        partial(flow_rest_kernel, share), "flow_rest", [small],
        index, *near(flow, other_half, part),
    )
    got_delta = swapped(delta, along_x)
    terms1 = local(
        terms1_kernel, "terms1", [one] * 4, index, *near(g, xg1, act1, das1, delta)
    )
    keep, send = local(
        terms_kernel, "terms", [three, three], index, *near(flow, got_act0, *terms1)
    )
    got = swapped(send, other_core)
    keep0, send0 = local(
        lower_kernel, "lower", [one, one], index, *near(xg0, low, got_delta), cost=LONG
    )
    got0 = swapped(send0, other_core)
    sums, across_out = local(
        chip_kernel, "chip", [three, quarter], place, index, *near(keep, got, keep0)
    )
    across_out = swapped(across_out, (1, 2))
    own, first, second, across_in = local(
        plane_kernel, "plane", [double, double, double, quarter],
        place, index, *near(sums, keep0, got0),
    )
    first = swapped(first, (0, 2), (1, 0))
    across_in = swapped(across_in, (1, 2))
    second = swapped(second, (1, 0), (0, 2))
    own = local(add_kernel, "add", [double], *near(own, across_out), cost=MEDIUM)
    mine, *others = local(
        layer_kernel, "layer", [((2 * rank, share), BF16)] * layers,
        index, *near(own, first, across_in, second),
    )
    others = [swapped(other, (0, 4 * k)) for k, other in enumerate(others, 1)]
    others = others[1:] + others[:1]
    block = ((1, rank, share), F32)
    total_in, total_out = local(
        total_kernel, "total", [block, block], *near(mine, *others),
        scratch=[pltpu.VMEM(*block), pltpu.VMEM(*block), sems((2,))], out="far",
    )
    return (jnp.swapaxes(total_in, 1, 2), total_out)


def section_back(x, gain, weight_in, weight_out, upstream):
    xf = x.astype(F32)
    scale = lax.rsqrt(jnp.mean(xf * xf, axis=-1, keepdims=True) + EPS)
    normed = xf * scale
    hidden = (normed * gain).astype(BF16)
    pre = jnp.dot(hidden, weight_in, preferred_element_type=F32)
    sig, slope = silu_slope(pre)
    active = (pre * sig).astype(BF16)
    delta_act = jnp.dot(upstream, weight_out.T, preferred_element_type=F32)
    delta_pre = (delta_act * slope).astype(BF16)
    delta_norm = jnp.dot(delta_pre, weight_in.T, preferred_element_type=F32) * gain
    inner = jnp.mean(delta_norm * normed, axis=-1, keepdims=True)
    result = (upstream.astype(F32) + scale * (delta_norm - normed * inner)).astype(BF16)
    term_in = jnp.dot(hidden.T, delta_pre, preferred_element_type=F32)
    term_out = jnp.dot(active.T, upstream, preferred_element_type=F32)
    return (result, term_in, term_out)


def relay_on_device(saved, top_grad, gains, adapter_in, adapter_out):
    sections = lax.axis_size("section")
    place = lax.axis_index("section")
    width = top_grad.shape[2]
    rank = adapter_in.shape[3]
    zero_in = jnp.zeros((width, rank), F32)
    zero_out = jnp.zeros((rank, width), F32)

    def step(turn, flows, sums):
        leaving, added = [], []
        for replica in (0, 1):
            serves = place == (sections - 1 - turn if replica == 0 else turn)
            result, term_in, term_out = lax.cond(
                serves,
                partial(
                    section_back,
                    saved[0, replica],
                    gains[0, replica],
                    adapter_in[0, replica],
                    adapter_out[0, replica],
                ),
                lambda flow: (flow, zero_in, zero_out),
                flows[replica],
            )
            leaving.append(result)
            added += [sums[2 * replica] + term_in, sums[2 * replica + 1] + term_out]
        return leaving, added

    down = [(i, i - 1) for i in range(1, sections)]
    up = [(i, i + 1) for i in range(sections - 1)]

    def turn_and_pass(turn, carry):
        leaving, sums = step(turn, carry[0], carry[1])
        return (
            [lax.ppermute(leaving[0], "section", down), lax.ppermute(leaving[1], "section", up)],
            sums,
        )

    start = ([top_grad[0], top_grad[1]], [zero_in, zero_out, zero_in, zero_out])
    flows, sums = lax.fori_loop(0, sections - 1, turn_and_pass, start)
    _, sums = step(sections - 1, flows, sums)
    shares = [
        lax.psum_scatter(term, "dp", scatter_dimension=i % 2, tiled=True)
        for i, term in enumerate(sums)
    ]
    mirror = [(i, sections - 1 - i) for i in range(sections)]
    total_in = shares[0] + lax.ppermute(shares[2], "section", mirror)
    total_out = shares[1] + lax.ppermute(shares[3], "section", mirror)
    return (total_in[None], total_out[None])


def solution(mesh):
    in_specs = (
        P("section", None, "dp", None),
        P(None, "dp", None),
        P("section", None, None),
        P("section", None, None, None),
        P("section", None, None, None),
    )
    out_specs = (P("section", "dp", None), P("section", None, "dp"))

    def run(saved, *others):
        share = saved.shape[3] // mesh.shape["dp"]
        count = mesh.shape["dp"]
        pair = mesh.shape["section"] == 2 and share % 128 == 0
        pair = pair and count >= 4 and count & (count - 1) == 0
        on_device = pair_on_device if pair else relay_on_device
        return jax.shard_map(
            on_device, mesh=mesh, in_specs=in_specs, out_specs=out_specs, check_vma=False
        )(saved, *others)

    return run
```

```python
from functools import partial

import jax
import jax.numpy as jnp
from jax import lax
from jax.experimental import pallas as pl
from jax.experimental.pallas import tpu as pltpu
from jax.sharding import PartitionSpec as P

EPS = 1e-05
VMEM_BYTES = 24 * 1024 * 1024
F32 = jnp.float32
BF16 = jnp.bfloat16


MEDIUM = pl.CostEstimate(flops=10**9, bytes_accessed=2**20, transcendentals=0)
LONG = pl.CostEstimate(flops=2 * 10**10, bytes_accessed=2**20, transcendentals=0)


def nn(a, b):
    return lax.dot_general(a, b, (((1,), (0,)), ((), ())), preferred_element_type=F32)


def nt(a, b):
    return lax.dot_general(a, b, (((1,), (1,)), ((), ())), preferred_element_type=F32)


def tn(a, b):
    return lax.dot_general(a, b, (((0,), (0,)), ((), ())), preferred_element_type=F32)


def as_row(column):
    count = column.shape[0]
    return jnp.transpose(jnp.broadcast_to(column, (count, count)))[0:1, :]


def silu_slope(pre):
    sig = jax.nn.sigmoid(pre)
    return sig, sig * (1.0 + pre * (1.0 - sig))


PIECES = 4


def pieces(source, target, sems, first):
    step = target.shape[-1] // PIECES
    copies = []
    for i in range(PIECES):
        cols = pl.ds(i * step, step)
        copies.append(
            pltpu.make_async_copy(source.at[:, cols], target.at[:, cols], sems.at[first + i])
        )
    return copies


def project(x_ref, gain_ref, w_ref, xg_ref, step, copies=()):
    tokens, width = x_ref.shape
    squares = jnp.zeros((tokens, 128), F32)
    pre = jnp.zeros((w_ref.shape[0], tokens), F32)
    for c in range(0, width, step):
        if copies and c % (width // len(copies)) == 0:
            copies[c * len(copies) // width].wait()
        x = x_ref[:, c : c + step].astype(F32)
        for k in range(0, step, 128):
            part = x[:, k : k + 128]
            squares += part * part
        xg = (x * gain_ref[:, c : c + step]).astype(BF16)
        xg_ref[:, c : c + step] = xg
        pre += nt(w_ref[:, c : c + step], xg)
    mean = jnp.sum(squares, axis=1, keepdims=True) * (1.0 / width)
    scale = lax.rsqrt(mean + EPS)
    return scale, pre


def fill(index, matrix, wide_ref, keep_ref, send_ref):
    share = keep_ref.shape[2]
    core = index % 2
    for i in range(wide_ref.shape[1] // share // 2):
        for to_ref, number in ((keep_ref, core), (send_ref, 1 - core)):
            cols = pl.ds(pl.multiple_of((2 * i + number) * share, share), share)
            to_ref[i] = nn(matrix, wide_ref[:, cols]).astype(BF16)


def front_kernel(
    step, place_ref, saved, gains, w_in,
    act0_ref, low_ref, xg0_ref, x1, gain1, wi1,
    x0, gain0, wi0, sems,
):
    lower = place_ref[0]
    upper = 1 - lower
    copies = [
        (gains.at[0, pl.ds(lower, 1)], gain0),
        (w_in.at[0, lower], wi0),
        (gains.at[0, pl.ds(upper, 1)], gain1),
        (w_in.at[0, upper], wi1),
    ]
    copies = [pltpu.make_async_copy(a, b, sems.at[i]) for i, (a, b) in enumerate(copies)]
    first = len(copies)
    copies_x0 = pieces(saved.at[0, lower], x0, sems, first)
    others = pieces(saved.at[0, upper], x1, sems, first + PIECES)
    for copy in copies[0:2] + copies_x0 + copies[2:4] + others:
        copy.start()
    for copy in copies[0:2]:
        copy.wait()
    scale, raw = project(x0, gain0, wi0, xg0_ref, step, copies_x0)
    row = as_row(scale)
    pre = raw * row
    sig, slope = silu_slope(pre)
    act0_ref[...] = (pre * sig).astype(BF16)
    low_ref[0] = slope
    low_ref[1] = jnp.broadcast_to(row, raw.shape)
    for copy in copies[2:4] + others:
        copy.wait()


def upper_kernel(
    step, place_ref, x, gain, wi, top, w_out,
    xg_ref, act_ref, das_ref, da_ref, columns_ref, g,
    wo, sems,
):
    width = x.shape[1]
    upper = 1 - place_ref[0]
    copies = pieces(w_out.at[0, upper], wo, sems, 0)
    copies_g = pieces(top.at[upper], g, sems, PIECES)
    for copy in copies + copies_g:
        copy.start()
    scale, raw = project(x, gain, wi, xg_ref, step)
    delta = jnp.zeros(raw.shape, F32)
    for copy in copies:
        copy.wait()
    for c in range(0, width, step):
        if c % (width // PIECES) == 0:
            copies_g[c * PIECES // width].wait()
        delta += nt(wo[:, c : c + step], g[:, c : c + step])
    row = as_row(scale)
    pre = raw * row
    sig, slope = silu_slope(pre)
    da = (delta * slope).astype(BF16)
    daf = da.astype(F32)
    inner = jnp.sum(daf * pre, axis=0, keepdims=True) * (1.0 / width)
    act_ref[...] = (pre * sig).astype(BF16)
    das_ref[...] = (daf * row).astype(BF16)
    da_ref[...] = da
    square = columns_ref.shape[1:]
    columns_ref[0] = jnp.broadcast_to(scale, square)
    columns_ref[1] = jnp.transpose(jnp.broadcast_to(inner * row * row, square))


def outgoing_kernel(step, x, g, gain, wi, da_ref, columns_ref, flow_ref):
    da = da_ref[...]
    scale = columns_ref[0][:, 0:1]
    pull = columns_ref[1][:, 0:1]
    for c in range(0, x.shape[1], step):
        cols = slice(c, c + step)
        dn = tn(da, wi[:, cols]) * gain[:, cols]
        flow = g[:, cols].astype(F32) + scale * dn - pull * x[:, cols].astype(F32)
        flow_ref[:, cols] = flow.astype(BF16)


def terms1_kernel(index_ref, g, xg_ref, act_ref, das_ref, _, keep_out, send_out, keep_in, send_in):
    fill(index_ref[0], act_ref[...], g, keep_out, send_out)
    fill(index_ref[0], das_ref[...], xg_ref, keep_in, send_in)


def terms_kernel(
    index_ref, flow_ref, act0_ref, keep_out1, send_out1, keep_in1, send_in1, keep_ref, send_ref
):
    fill(index_ref[0], act0_ref[...], flow_ref, keep_ref, send_ref)
    chips = keep_in1.shape[0]
    keep_ref[chips : 2 * chips] = keep_out1[...]
    send_ref[chips : 2 * chips] = send_out1[...]
    keep_ref[2 * chips : 3 * chips] = keep_in1[...]
    send_ref[2 * chips : 3 * chips] = send_in1[...]


def pick_kernel(place_ref, index_ref, w_out, out_ref, sems):
    half = out_ref.shape[1]
    cols = pl.ds(pl.multiple_of((index_ref[0] % 2) * half, half), half)
    copies = pieces(w_out.at[0, place_ref[0], :, cols], out_ref, sems, 0)
    for copy in copies:
        copy.start()
    for copy in copies:
        copy.wait()


def product(step, number, w_ref, flow_ref):
    half = w_ref.shape[1]
    delta = jnp.zeros((w_ref.shape[0], flow_ref.shape[0]), F32)
    for c in range(0, half, step):
        cols = pl.ds(pl.multiple_of(number * half + c, step), step)
        delta += nt(w_ref[:, c : c + step], flow_ref[:, cols])
    return delta


def flow_kernel(step, index_ref, flow_ref, own_ref, part_ref):
    part_ref[...] = product(step, index_ref[0] % 2, own_ref, flow_ref)


def flow_rest_kernel(step, index_ref, flow_ref, other_ref, part_ref, send_ref):
    rest = product(step, 1 - index_ref[0] % 2, other_ref, flow_ref)
    send_ref[...] = (part_ref[...] + rest).astype(BF16)


def lower_kernel(index_ref, xg0_ref, low_ref, got_ref, keep_ref, send_ref):
    da = (got_ref[...].astype(F32) * low_ref[0]).astype(BF16)
    das = (da.astype(F32) * low_ref[1]).astype(BF16)
    fill(index_ref[0], das, xg0_ref, keep_ref, send_ref)


def chip_kernel(place_ref, index_ref, keep, got, _, sum_ref, across):
    for i in range(keep.shape[0]):
        sum_ref[i] = (keep[i].astype(F32) + got[i].astype(F32)).astype(BF16)
    row = (index_ref[0] // 2) % 2
    first = (1 - place_ref[0]) * (2 * across.shape[0]) + 1 - row
    for i in range(across.shape[0]):
        across[i] = sum_ref[first + 2 * i]


def plane_kernel(
    place_ref, index_ref, sums, keep0, got0, own_ref, first_ref, second_ref, across
):
    rank = keep0.shape[1]
    chips = keep0.shape[0]
    row = (index_ref[0] // 2) % 2

    def terms_in(section, block):
        if section == 0:
            return (keep0[block].astype(F32) + got0[block].astype(F32)).astype(BF16)
        return sums[2 * chips + block]

    def order(near, along_x, along_y):
        far = 1 - near
        for i in range(own_ref.shape[0]):
            across[i] = terms_in(far, 2 * i + 1 - row)
            for to_ref, section, number in (
                (along_x, far, row),
                (along_y, near, 1 - row),
                (own_ref, near, row),
            ):
                block = 2 * i + number
                to_ref[i, 0:rank] = terms_in(section, block)
                to_ref[i, rank : 2 * rank] = sums[section * chips + block]

    for place in range(2):
        for core, ways in ((0, (second_ref, first_ref)), (1, (first_ref, second_ref))):
            pl.when((place_ref[0] == place) & (index_ref[0] % 2 == core))(
                partial(order, place, *ways)
            )


def add_kernel(own, across_out, out_ref):
    rank = across_out.shape[1]
    out_ref[:, 0:rank] = own[:, 0:rank]
    for i in range(own.shape[0]):
        total = own[i, rank : 2 * rank].astype(F32) + across_out[i].astype(F32)
        out_ref[i, rank : 2 * rank] = total.astype(BF16)


def layer_kernel(index_ref, own, first, across_in, second, *out_refs):
    rank = across_in.shape[1]
    layer = index_ref[0] // 4
    for k, out_ref in enumerate(out_refs):
        block = layer ^ k
        total = sum(ref[block].astype(F32) for ref in (own, first, second))
        out_ref[0:rank] = (total[0:rank] + across_in[block].astype(F32)).astype(BF16)
        out_ref[rank : 2 * rank] = total[rank : 2 * rank].astype(BF16)


def total_kernel(*refs):
    *got, in_far, out_far, in_ref, out_ref, sems = refs
    rank = in_ref.shape[1]
    copies = []
    for i, (ref, far) in enumerate(((in_ref, in_far), (out_ref, out_far))):
        ref[0] = sum(part[i * rank : (i + 1) * rank].astype(F32) for part in got)
        copies.append(pltpu.make_async_copy(ref, far, sems.at[i]))
        copies[i].start()
    for copy in copies:
        copy.wait()


def local(kernel, name, out_shapes, *operands, scratch=(), cost=None, out="near"):
    spaces = {"scalar": pltpu.SMEM, "far": pltpu.HBM, "near": pltpu.VMEM}
    out = pl.pallas_call(
        kernel,
        in_specs=[pl.BlockSpec(memory_space=spaces[kind]) for kind, _ in operands],
        out_specs=[pl.BlockSpec(memory_space=spaces[out])] * len(out_shapes),
        out_shape=[jax.ShapeDtypeStruct(shape, dtype) for shape, dtype in out_shapes],
        scratch_shapes=list(scratch),
        compiler_params=pltpu.CompilerParams(vmem_limit_bytes=VMEM_BYTES),
        cost_estimate=cost,
        name=name,
    )(*[array for _, array in operands])
    return out if len(out) > 1 else out[0]


def near(*arrays):
    return [("near", array) for array in arrays]


def pair_on_device(saved, top_grad, gains, adapter_in, adapter_out):
    count = lax.axis_size("dp")
    tokens, width = saved.shape[2:]
    rank = adapter_in.shape[3]
    share = width // count
    chips, layers = count // 2, count // 4
    place = ("scalar", lax.axis_index("section").astype(jnp.int32)[None])
    index = ("scalar", lax.axis_index("dp").astype(jnp.int32)[None])
    saved, top, gains, w_in, w_out = [
        ("far", pltpu.with_memory_space_constraint(a, pltpu.HBM))
        for a in (saved, top_grad, gains, jnp.swapaxes(adapter_in, 2, 3), adapter_out)
    ]

    def swapped(array, *ways):
        pairs = []
        for s in range(2):
            for d in range(count):
                over_section, bits = ways[d % len(ways)]
                pairs.append((s * count + d, (s ^ over_section) * count + (d ^ bits)))
        return lax.ppermute(array, ("section", "dp"), pairs)

    sems = pltpu.SemaphoreType.DMA
    wide = ((tokens, width), BF16)
    thin = ((rank, width), BF16)
    gain = ((1, width), F32)
    small = ((rank, tokens), BF16)
    one = ((chips, rank, share), BF16)
    three = ((3 * chips, rank, share), BF16)
    quarter = ((layers, rank, share), BF16)
    double = ((layers, 2 * rank, share), BF16)
    along_x, other_core = (1, 0), (0, 1)

    mine = local(
        pick_kernel, "pick", [((rank, width // 2), BF16)], place, index, w_out, scratch=[sems((PIECES,))]
    )
    own_half = swapped(mine, along_x)
    act0, low, xg0, x1, gain1, wi1 = local(
        partial(front_kernel, share), "front",
        [small, ((2, rank, tokens), F32), wide, wide, gain, thin],
        place, saved, gains, w_in,
        scratch=[pltpu.VMEM(*wide), pltpu.VMEM(*gain), pltpu.VMEM(*thin), sems((4 + 2 * PIECES,))],
    )
    got_act0 = swapped(act0, along_x)
    xg1, act1, das1, da1, columns, g = local(
        partial(upper_kernel, share), "upper",
        [wide, small, small, small, ((2, tokens, tokens), F32), wide],
        place, *near(x1, gain1, wi1), top, w_out,
        scratch=[pltpu.VMEM(*thin), sems((2 * PIECES,))],
    )
    own_half, da1 = lax.optimization_barrier((own_half, da1))
    other_half = swapped(own_half, other_core)
    flow = local(
        partial(outgoing_kernel, share), "outgoing", [wide], *near(x1, g, gain1, wi1, da1, columns),
        cost=LONG,
    )
    part = local(
        partial(flow_kernel, share), "flow", [((rank, tokens), F32)], index, *near(flow, own_half)
    )
    delta = local(
        partial(flow_rest_kernel, share), "flow_rest", [small],
        index, *near(flow, other_half, part),
    )
    got_delta = swapped(delta, along_x)
    terms1 = local(
        terms1_kernel, "terms1", [one] * 4, index, *near(g, xg1, act1, das1, delta)
    )
    keep, send = local(
        terms_kernel, "terms", [three, three], index, *near(flow, got_act0, *terms1)
    )
    got = swapped(send, other_core)
    keep0, send0 = local(
        lower_kernel, "lower", [one, one], index, *near(xg0, low, got_delta), cost=LONG
    )
    got0 = swapped(send0, other_core)
    sums, across_out = local(
        chip_kernel, "chip", [three, quarter], place, index, *near(keep, got, keep0)
    )
    across_out = swapped(across_out, (1, 2))
    own, first, second, across_in = local(
        plane_kernel, "plane", [double, double, double, quarter],
        place, index, *near(sums, keep0, got0),
    )
    first = swapped(first, (0, 2), (1, 0))
    across_in = swapped(across_in, (1, 2))
    second = swapped(second, (1, 0), (0, 2))
    own = local(add_kernel, "add", [double], *near(own, across_out), cost=MEDIUM)
    mine, *others = local(
        layer_kernel, "layer", [((2 * rank, share), BF16)] * layers,
        index, *near(own, first, across_in, second),
    )
    others = [swapped(other, (0, 4 * k)) for k, other in enumerate(others, 1)]
    others = others[1:] + others[:1]
    block = ((1, rank, share), F32)
    total_in, total_out = local(
        total_kernel, "total", [block, block], *near(mine, *others),
        scratch=[pltpu.VMEM(*block), pltpu.VMEM(*block), sems((2,))], out="far",
    )
    return (jnp.swapaxes(total_in, 1, 2), total_out)


def section_back(x, gain, weight_in, weight_out, upstream):
    xf = x.astype(F32)
    scale = lax.rsqrt(jnp.mean(xf * xf, axis=-1, keepdims=True) + EPS)
    normed = xf * scale
    hidden = (normed * gain).astype(BF16)
    pre = jnp.dot(hidden, weight_in, preferred_element_type=F32)
    sig, slope = silu_slope(pre)
    active = (pre * sig).astype(BF16)
    delta_act = jnp.dot(upstream, weight_out.T, preferred_element_type=F32)
    delta_pre = (delta_act * slope).astype(BF16)
    delta_norm = jnp.dot(delta_pre, weight_in.T, preferred_element_type=F32) * gain
    inner = jnp.mean(delta_norm * normed, axis=-1, keepdims=True)
    result = (upstream.astype(F32) + scale * (delta_norm - normed * inner)).astype(BF16)
    term_in = jnp.dot(hidden.T, delta_pre, preferred_element_type=F32)
    term_out = jnp.dot(active.T, upstream, preferred_element_type=F32)
    return (result, term_in, term_out)


def relay_on_device(saved, top_grad, gains, adapter_in, adapter_out):
    sections = lax.axis_size("section")
    place = lax.axis_index("section")
    width = top_grad.shape[2]
    rank = adapter_in.shape[3]
    zero_in = jnp.zeros((width, rank), F32)
    zero_out = jnp.zeros((rank, width), F32)

    def step(turn, flows, sums):
        leaving, added = [], []
        for replica in (0, 1):
            serves = place == (sections - 1 - turn if replica == 0 else turn)
            result, term_in, term_out = lax.cond(
                serves,
                partial(
                    section_back,
                    saved[0, replica],
                    gains[0, replica],
                    adapter_in[0, replica],
                    adapter_out[0, replica],
                ),
                lambda flow: (flow, zero_in, zero_out),
                flows[replica],
            )
            leaving.append(result)
            added += [sums[2 * replica] + term_in, sums[2 * replica + 1] + term_out]
        return leaving, added

    down = [(i, i - 1) for i in range(1, sections)]
    up = [(i, i + 1) for i in range(sections - 1)]

    def turn_and_pass(turn, carry):
        leaving, sums = step(turn, carry[0], carry[1])
        return (
            [lax.ppermute(leaving[0], "section", down), lax.ppermute(leaving[1], "section", up)],
            sums,
        )

    start = ([top_grad[0], top_grad[1]], [zero_in, zero_out, zero_in, zero_out])
    flows, sums = lax.fori_loop(0, sections - 1, turn_and_pass, start)
    _, sums = step(sections - 1, flows, sums)
    shares = [
        lax.psum_scatter(term, "dp", scatter_dimension=i % 2, tiled=True)
        for i, term in enumerate(sums)
    ]
    mirror = [(i, sections - 1 - i) for i in range(sections)]
    total_in = shares[0] + lax.ppermute(shares[2], "section", mirror)
    total_out = shares[1] + lax.ppermute(shares[3], "section", mirror)
    return (total_in[None], total_out[None])


def solution(mesh):
    in_specs = (
        P("section", None, "dp", None),
        P(None, "dp", None),
        P("section", None, None),
        P("section", None, None, None),
        P("section", None, None, None),
    )
    out_specs = (P("section", "dp", None), P("section", None, "dp"))

    def run(saved, *others):
        share = saved.shape[3] // mesh.shape["dp"]
        count = mesh.shape["dp"]
        pair = mesh.shape["section"] == 2 and share % 128 == 0
        pair = pair and count >= 4 and count & (count - 1) == 0
        on_device = pair_on_device if pair else relay_on_device
        return jax.shard_map(
            on_device, mesh=mesh, in_specs=in_specs, out_specs=out_specs, check_vma=False
        )(saved, *others)

    return run
```

```python
from functools import partial

import jax
import jax.numpy as jnp
from jax import lax
from jax.experimental import pallas as pl
from jax.experimental.pallas import tpu as pltpu
from jax.sharding import PartitionSpec as P

EPS = 1e-05
VMEM_BYTES = 24 * 1024 * 1024
F32 = jnp.float32
BF16 = jnp.bfloat16


MEDIUM = pl.CostEstimate(flops=10**9, bytes_accessed=2**20, transcendentals=0)
LONG = pl.CostEstimate(flops=2 * 10**10, bytes_accessed=2**20, transcendentals=0)


def nn(a, b):
    return lax.dot_general(a, b, (((1,), (0,)), ((), ())), preferred_element_type=F32)


def nt(a, b):
    return lax.dot_general(a, b, (((1,), (1,)), ((), ())), preferred_element_type=F32)


def tn(a, b):
    return lax.dot_general(a, b, (((0,), (0,)), ((), ())), preferred_element_type=F32)


def as_row(column):
    count = column.shape[0]
    return jnp.transpose(jnp.broadcast_to(column, (count, count)))[0:1, :]


def silu_slope(pre):
    sig = jax.nn.sigmoid(pre)
    return sig, sig * (1.0 + pre * (1.0 - sig))


PIECES = 4


def pieces(source, target, sems, first):
    step = target.shape[-1] // PIECES
    copies = []
    for i in range(PIECES):
        cols = pl.ds(i * step, step)
        copies.append(
            pltpu.make_async_copy(source.at[:, cols], target.at[:, cols], sems.at[first + i])
        )
    return copies


def project(x_ref, gain_ref, w_ref, xg_ref, step, copies=()):
    tokens, width = x_ref.shape
    squares = jnp.zeros((tokens, 128), F32)
    pre = jnp.zeros((w_ref.shape[0], tokens), F32)
    for c in range(0, width, step):
        if copies and c % (width // len(copies)) == 0:
            copies[c * len(copies) // width].wait()
        x = x_ref[:, c : c + step].astype(F32)
        for k in range(0, step, 128):
            part = x[:, k : k + 128]
            squares += part * part
        xg = (x * gain_ref[:, c : c + step]).astype(BF16)
        xg_ref[:, c : c + step] = xg
        pre += nt(w_ref[:, c : c + step], xg)
    mean = jnp.sum(squares, axis=1, keepdims=True) * (1.0 / width)
    scale = lax.rsqrt(mean + EPS)
    return scale, pre


def fill(index, matrix, wide_ref, keep_ref, send_ref):
    share = keep_ref.shape[2]
    core = index % 2
    for i in range(wide_ref.shape[1] // share // 2):
        for to_ref, number in ((keep_ref, core), (send_ref, 1 - core)):
            cols = pl.ds(pl.multiple_of((2 * i + number) * share, share), share)
            to_ref[i] = nn(matrix, wide_ref[:, cols]).astype(BF16)


def front_kernel(
    step, place_ref, saved, top, gains, w_in, w_out,
    act0_ref, low_ref, xg0_ref, x1, g, gain1, wi1, wo1,
    x0, gain0, wi0, sems,
):
    lower = place_ref[0]
    upper = 1 - lower
    copies = [
        (gains.at[0, pl.ds(lower, 1)], gain0),
        (w_in.at[0, lower], wi0),
        (gains.at[0, pl.ds(upper, 1)], gain1),
        (w_in.at[0, upper], wi1),
        (w_out.at[0, upper], wo1),
    ]
    copies = [pltpu.make_async_copy(a, b, sems.at[i]) for i, (a, b) in enumerate(copies)]
    first = len(copies)
    copies_x0 = pieces(saved.at[0, lower], x0, sems, first)
    others = pieces(saved.at[0, upper], x1, sems, first + PIECES)
    others += pieces(top.at[upper], g, sems, first + 2 * PIECES)
    for copy in copies[0:2] + copies_x0 + copies[2:5] + others:
        copy.start()
    for copy in copies[0:2]:
        copy.wait()
    scale, raw = project(x0, gain0, wi0, xg0_ref, step, copies_x0)
    row = as_row(scale)
    pre = raw * row
    sig, slope = silu_slope(pre)
    act0_ref[...] = (pre * sig).astype(BF16)
    low_ref[0] = slope
    low_ref[1] = jnp.broadcast_to(row, raw.shape)
    for copy in copies[2:5] + others:
        copy.wait()


def upper_kernel(step, x, g, gain, wi, wo, xg_ref, act_ref, das_ref, da_ref, columns_ref):
    width = x.shape[1]
    scale, raw = project(x, gain, wi, xg_ref, step)
    delta = jnp.zeros(raw.shape, F32)
    for c in range(0, width, step):
        delta += nt(wo[:, c : c + step], g[:, c : c + step])
    row = as_row(scale)
    pre = raw * row
    sig, slope = silu_slope(pre)
    da = (delta * slope).astype(BF16)
    daf = da.astype(F32)
    inner = jnp.sum(daf * pre, axis=0, keepdims=True) * (1.0 / width)
    act_ref[...] = (pre * sig).astype(BF16)
    das_ref[...] = (daf * row).astype(BF16)
    da_ref[...] = da
    square = columns_ref.shape[1:]
    columns_ref[0] = jnp.broadcast_to(scale, square)
    columns_ref[1] = jnp.transpose(jnp.broadcast_to(inner * row * row, square))


def outgoing_kernel(step, x, g, gain, wi, da_ref, columns_ref, flow_ref):
    da = da_ref[...]
    scale = columns_ref[0][:, 0:1]
    pull = columns_ref[1][:, 0:1]
    for c in range(0, x.shape[1], step):
        cols = slice(c, c + step)
        dn = tn(da, wi[:, cols]) * gain[:, cols]
        flow = g[:, cols].astype(F32) + scale * dn - pull * x[:, cols].astype(F32)
        flow_ref[:, cols] = flow.astype(BF16)


def terms1_kernel(index_ref, g, xg_ref, act_ref, das_ref, _, keep_out, send_out, keep_in, send_in):
    fill(index_ref[0], act_ref[...], g, keep_out, send_out)
    fill(index_ref[0], das_ref[...], xg_ref, keep_in, send_in)


def terms_kernel(
    index_ref, flow_ref, act0_ref, keep_out1, send_out1, keep_in1, send_in1, keep_ref, send_ref
):
    fill(index_ref[0], act0_ref[...], flow_ref, keep_ref, send_ref)
    chips = keep_in1.shape[0]
    keep_ref[chips : 2 * chips] = keep_out1[...]
    send_ref[chips : 2 * chips] = send_out1[...]
    keep_ref[2 * chips : 3 * chips] = keep_in1[...]
    send_ref[2 * chips : 3 * chips] = send_in1[...]


def pick_kernel(place_ref, index_ref, w_out, out_ref, sems):
    half = out_ref.shape[1]
    cols = pl.ds(pl.multiple_of((index_ref[0] % 2) * half, half), half)
    copies = pieces(w_out.at[0, place_ref[0], :, cols], out_ref, sems, 0)
    for copy in copies:
        copy.start()
    for copy in copies:
        copy.wait()


def product(step, number, w_ref, flow_ref):
    half = w_ref.shape[1]
    delta = jnp.zeros((w_ref.shape[0], flow_ref.shape[0]), F32)
    for c in range(0, half, step):
        cols = pl.ds(pl.multiple_of(number * half + c, step), step)
        delta += nt(w_ref[:, c : c + step], flow_ref[:, cols])
    return delta


def flow_kernel(step, index_ref, flow_ref, own_ref, part_ref):
    part_ref[...] = product(step, index_ref[0] % 2, own_ref, flow_ref)


def flow_rest_kernel(step, index_ref, flow_ref, other_ref, part_ref, send_ref):
    rest = product(step, 1 - index_ref[0] % 2, other_ref, flow_ref)
    send_ref[...] = (part_ref[...] + rest).astype(BF16)


def lower_kernel(index_ref, xg0_ref, low_ref, got_ref, keep_ref, send_ref):
    da = (got_ref[...].astype(F32) * low_ref[0]).astype(BF16)
    das = (da.astype(F32) * low_ref[1]).astype(BF16)
    fill(index_ref[0], das, xg0_ref, keep_ref, send_ref)


def chip_kernel(place_ref, index_ref, keep, got, _, sum_ref, across):
    for i in range(keep.shape[0]):
        sum_ref[i] = (keep[i].astype(F32) + got[i].astype(F32)).astype(BF16)
    row = (index_ref[0] // 2) % 2
    first = (1 - place_ref[0]) * (2 * across.shape[0]) + 1 - row
    for i in range(across.shape[0]):
        across[i] = sum_ref[first + 2 * i]


def plane_kernel(
    place_ref, index_ref, sums, keep0, got0, own_ref, first_ref, second_ref, across
):
    rank = keep0.shape[1]
    chips = keep0.shape[0]
    row = (index_ref[0] // 2) % 2

    def terms_in(section, block):
        if section == 0:
            return (keep0[block].astype(F32) + got0[block].astype(F32)).astype(BF16)
        return sums[2 * chips + block]

    def order(near, along_x, along_y):
        far = 1 - near
        for i in range(own_ref.shape[0]):
            across[i] = terms_in(far, 2 * i + 1 - row)
            for to_ref, section, number in (
                (along_x, far, row),
                (along_y, near, 1 - row),
                (own_ref, near, row),
            ):
                block = 2 * i + number
                to_ref[i, 0:rank] = terms_in(section, block)
                to_ref[i, rank : 2 * rank] = sums[section * chips + block]

    for place in range(2):
        for core, ways in ((0, (second_ref, first_ref)), (1, (first_ref, second_ref))):
            pl.when((place_ref[0] == place) & (index_ref[0] % 2 == core))(
                partial(order, place, *ways)
            )


def add_kernel(own, across_out, out_ref):
    rank = across_out.shape[1]
    out_ref[:, 0:rank] = own[:, 0:rank]
    for i in range(own.shape[0]):
        total = own[i, rank : 2 * rank].astype(F32) + across_out[i].astype(F32)
        out_ref[i, rank : 2 * rank] = total.astype(BF16)


def layer_routes(layers):
    if layers == 4:
        return [[1, 3, 0, 2], [3, 2, 1, 0], [2, 0, 3, 1]]
    return [[i ^ k for i in range(layers)] for k in range(1, layers)]


def layer_kernel(routes, index_ref, own, first, across_in, second, *out_refs):
    rank = across_in.shape[1]
    layer = index_ref[0] // 4
    for route, out_ref in zip([range(len(out_refs)), *routes], out_refs):
        block = sum(jnp.where(layer == i, target, 0) for i, target in enumerate(route))
        total = sum(ref[block].astype(F32) for ref in (own, first, second))
        out_ref[0:rank] = (total[0:rank] + across_in[block].astype(F32)).astype(BF16)
        out_ref[rank : 2 * rank] = total[rank : 2 * rank].astype(BF16)


def total_kernel(*refs):
    *got, in_far, out_far, in_ref, out_ref, sems = refs
    rank = in_ref.shape[1]
    copies = []
    for i, (ref, far) in enumerate(((in_ref, in_far), (out_ref, out_far))):
        ref[0] = sum(part[i * rank : (i + 1) * rank].astype(F32) for part in got)
        copies.append(pltpu.make_async_copy(ref, far, sems.at[i]))
        copies[i].start()
    for copy in copies:
        copy.wait()


def local(kernel, name, out_shapes, *operands, scratch=(), cost=None, out="near"):
    spaces = {"scalar": pltpu.SMEM, "far": pltpu.HBM, "near": pltpu.VMEM}
    out = pl.pallas_call(
        kernel,
        in_specs=[pl.BlockSpec(memory_space=spaces[kind]) for kind, _ in operands],
        out_specs=[pl.BlockSpec(memory_space=spaces[out])] * len(out_shapes),
        out_shape=[jax.ShapeDtypeStruct(shape, dtype) for shape, dtype in out_shapes],
        scratch_shapes=list(scratch),
        compiler_params=pltpu.CompilerParams(vmem_limit_bytes=VMEM_BYTES),
        cost_estimate=cost,
        name=name,
    )(*[array for _, array in operands])
    return out if len(out) > 1 else out[0]


def near(*arrays):
    return [("near", array) for array in arrays]


def pair_on_device(saved, top_grad, gains, adapter_in, adapter_out):
    count = lax.axis_size("dp")
    tokens, width = saved.shape[2:]
    rank = adapter_in.shape[3]
    share = width // count
    chips, layers = count // 2, count // 4
    place = ("scalar", lax.axis_index("section").astype(jnp.int32)[None])
    index = ("scalar", lax.axis_index("dp").astype(jnp.int32)[None])
    saved, top, gains, w_in, w_out = [
        ("far", pltpu.with_memory_space_constraint(a, pltpu.HBM))
        for a in (saved, top_grad, gains, jnp.swapaxes(adapter_in, 2, 3), adapter_out)
    ]

    def swapped(array, *ways):
        pairs = []
        for s in range(2):
            for d in range(count):
                over_section, bits = ways[d % len(ways)]
                pairs.append((s * count + d, (s ^ over_section) * count + (d ^ bits)))
        return lax.ppermute(array, ("section", "dp"), pairs)

    sems = pltpu.SemaphoreType.DMA
    wide = ((tokens, width), BF16)
    thin = ((rank, width), BF16)
    gain = ((1, width), F32)
    small = ((rank, tokens), BF16)
    one = ((chips, rank, share), BF16)
    three = ((3 * chips, rank, share), BF16)
    quarter = ((layers, rank, share), BF16)
    double = ((layers, 2 * rank, share), BF16)
    along_x, other_core = (1, 0), (0, 1)

    mine = local(
        pick_kernel, "pick", [((rank, width // 2), BF16)], place, index, w_out, scratch=[sems((PIECES,))]
    )
    own_half = swapped(mine, along_x)
    act0, low, xg0, x1, g, gain1, wi1, wo1 = local(
        partial(front_kernel, share), "front",
        [small, ((2, rank, tokens), F32), wide, wide, wide, gain, thin, thin],
        place, saved, top, gains, w_in, w_out,
        scratch=[pltpu.VMEM(*wide), pltpu.VMEM(*gain), pltpu.VMEM(*thin), sems((5 + 3 * PIECES,))],
    )
    got_act0 = swapped(act0, along_x)
    xg1, act1, das1, da1, columns = local(
        partial(upper_kernel, share), "upper",
        [wide, small, small, small, ((2, tokens, tokens), F32)],
        *near(x1, g, gain1, wi1, wo1),
    )
    own_half, da1 = lax.optimization_barrier((own_half, da1))
    other_half = swapped(own_half, other_core)
    flow = local(
        partial(outgoing_kernel, share), "outgoing", [wide], *near(x1, g, gain1, wi1, da1, columns),
        cost=LONG,
    )
    part = local(
        partial(flow_kernel, share), "flow", [((rank, tokens), F32)], index, *near(flow, own_half)
    )
    delta = local(
        partial(flow_rest_kernel, share), "flow_rest", [small],
        index, *near(flow, other_half, part),
    )
    got_delta = swapped(delta, along_x)
    terms1 = local(
        terms1_kernel, "terms1", [one] * 4, index, *near(g, xg1, act1, das1, delta)
    )
    keep, send = local(
        terms_kernel, "terms", [three, three], index, *near(flow, got_act0, *terms1)
    )
    got = swapped(send, other_core)
    keep0, send0 = local(
        lower_kernel, "lower", [one, one], index, *near(xg0, low, got_delta), cost=LONG
    )
    got0 = swapped(send0, other_core)
    sums, across_out = local(
        chip_kernel, "chip", [three, quarter], place, index, *near(keep, got, keep0)
    )
    across_out = swapped(across_out, (1, 2))
    own, first, second, across_in = local(
        plane_kernel, "plane", [double, double, double, quarter],
        place, index, *near(sums, keep0, got0),
    )
    first = swapped(first, (0, 2), (1, 0))
    across_in = swapped(across_in, (1, 2))
    second = swapped(second, (1, 0), (0, 2))
    own = local(add_kernel, "add", [double], *near(own, across_out), cost=MEDIUM)
    routes = layer_routes(layers)
    mine, *others = local(
        partial(layer_kernel, routes), "layer", [((2 * rank, share), BF16)] * layers,
        index, *near(own, first, across_in, second),
    )
    others = [
        lax.ppermute(
            other,
            ("section", "dp"),
            [
                (s * count + d, s * count + 4 * route[d // 4] + d % 4)
                for s in range(2)
                for d in range(count)
            ],
        )
        for route, other in zip(routes, others)
    ]
    block = ((1, rank, share), F32)
    total_in, total_out = local(
        total_kernel, "total", [block, block], *near(mine, *others),
        scratch=[pltpu.VMEM(*block), pltpu.VMEM(*block), sems((2,))], out="far",
    )
    return (jnp.swapaxes(total_in, 1, 2), total_out)


def section_back(x, gain, weight_in, weight_out, upstream):
    xf = x.astype(F32)
    scale = lax.rsqrt(jnp.mean(xf * xf, axis=-1, keepdims=True) + EPS)
    normed = xf * scale
    hidden = (normed * gain).astype(BF16)
    pre = jnp.dot(hidden, weight_in, preferred_element_type=F32)
    sig, slope = silu_slope(pre)
    active = (pre * sig).astype(BF16)
    delta_act = jnp.dot(upstream, weight_out.T, preferred_element_type=F32)
    delta_pre = (delta_act * slope).astype(BF16)
    delta_norm = jnp.dot(delta_pre, weight_in.T, preferred_element_type=F32) * gain
    inner = jnp.mean(delta_norm * normed, axis=-1, keepdims=True)
    result = (upstream.astype(F32) + scale * (delta_norm - normed * inner)).astype(BF16)
    term_in = jnp.dot(hidden.T, delta_pre, preferred_element_type=F32)
    term_out = jnp.dot(active.T, upstream, preferred_element_type=F32)
    return (result, term_in, term_out)


def relay_on_device(saved, top_grad, gains, adapter_in, adapter_out):
    sections = lax.axis_size("section")
    place = lax.axis_index("section")
    width = top_grad.shape[2]
    rank = adapter_in.shape[3]
    zero_in = jnp.zeros((width, rank), F32)
    zero_out = jnp.zeros((rank, width), F32)

    def step(turn, flows, sums):
        leaving, added = [], []
        for replica in (0, 1):
            serves = place == (sections - 1 - turn if replica == 0 else turn)
            result, term_in, term_out = lax.cond(
                serves,
                partial(
                    section_back,
                    saved[0, replica],
                    gains[0, replica],
                    adapter_in[0, replica],
                    adapter_out[0, replica],
                ),
                lambda flow: (flow, zero_in, zero_out),
                flows[replica],
            )
            leaving.append(result)
            added += [sums[2 * replica] + term_in, sums[2 * replica + 1] + term_out]
        return leaving, added

    down = [(i, i - 1) for i in range(1, sections)]
    up = [(i, i + 1) for i in range(sections - 1)]

    def turn_and_pass(turn, carry):
        leaving, sums = step(turn, carry[0], carry[1])
        return (
            [lax.ppermute(leaving[0], "section", down), lax.ppermute(leaving[1], "section", up)],
            sums,
        )

    start = ([top_grad[0], top_grad[1]], [zero_in, zero_out, zero_in, zero_out])
    flows, sums = lax.fori_loop(0, sections - 1, turn_and_pass, start)
    _, sums = step(sections - 1, flows, sums)
    shares = [
        lax.psum_scatter(term, "dp", scatter_dimension=i % 2, tiled=True)
        for i, term in enumerate(sums)
    ]
    mirror = [(i, sections - 1 - i) for i in range(sections)]
    total_in = shares[0] + lax.ppermute(shares[2], "section", mirror)
    total_out = shares[1] + lax.ppermute(shares[3], "section", mirror)
    return (total_in[None], total_out[None])


def solution(mesh):
    in_specs = (
        P("section", None, "dp", None),
        P(None, "dp", None),
        P("section", None, None),
        P("section", None, None, None),
        P("section", None, None, None),
    )
    out_specs = (P("section", "dp", None), P("section", None, "dp"))

    def run(saved, *others):
        share = saved.shape[3] // mesh.shape["dp"]
        count = mesh.shape["dp"]
        pair = mesh.shape["section"] == 2 and share % 128 == 0
        pair = pair and count >= 4 and count & (count - 1) == 0
        on_device = pair_on_device if pair else relay_on_device
        return jax.shard_map(
            on_device, mesh=mesh, in_specs=in_specs, out_specs=out_specs, check_vma=False
        )(saved, *others)

    return run
```

```python
from functools import partial

import jax
import jax.numpy as jnp
from jax import lax
from jax.experimental import pallas as pl
from jax.experimental.pallas import tpu as pltpu
from jax.sharding import PartitionSpec as P

EPS = 1e-05
VMEM_BYTES = 24 * 1024 * 1024
F32 = jnp.float32
BF16 = jnp.bfloat16


MEDIUM = pl.CostEstimate(flops=10**9, bytes_accessed=2**20, transcendentals=0)
LONG = pl.CostEstimate(flops=2 * 10**10, bytes_accessed=2**20, transcendentals=0)


def nn(a, b):
    return lax.dot_general(a, b, (((1,), (0,)), ((), ())), preferred_element_type=F32)


def nt(a, b):
    return lax.dot_general(a, b, (((1,), (1,)), ((), ())), preferred_element_type=F32)


def tn(a, b):
    return lax.dot_general(a, b, (((0,), (0,)), ((), ())), preferred_element_type=F32)


def as_row(column):
    count = column.shape[0]
    return jnp.transpose(jnp.broadcast_to(column, (count, count)))[0:1, :]


def silu_slope(pre):
    sig = jax.nn.sigmoid(pre)
    return sig, sig * (1.0 + pre * (1.0 - sig))


PIECES = 4


def pieces(source, target, sems, first):
    step = target.shape[-1] // PIECES
    copies = []
    for i in range(PIECES):
        cols = pl.ds(i * step, step)
        copies.append(
            pltpu.make_async_copy(source.at[:, cols], target.at[:, cols], sems.at[first + i])
        )
    return copies


def project(x_ref, gain_ref, w_ref, xg_ref, step, copies=()):
    tokens, width = x_ref.shape
    squares = jnp.zeros((tokens, 128), F32)
    pre = jnp.zeros((w_ref.shape[0], tokens), F32)
    for c in range(0, width, step):
        if copies and c % (width // len(copies)) == 0:
            copies[c * len(copies) // width].wait()
        x = x_ref[:, c : c + step].astype(F32)
        for k in range(0, step, 128):
            part = x[:, k : k + 128]
            squares += part * part
        xg = (x * gain_ref[:, c : c + step]).astype(BF16)
        xg_ref[:, c : c + step] = xg
        pre += nt(w_ref[:, c : c + step], xg)
    mean = jnp.sum(squares, axis=1, keepdims=True) * (1.0 / width)
    scale = lax.rsqrt(mean + EPS)
    return scale, pre


def fill(index, matrix, wide_ref, keep_ref, send_ref):
    share = keep_ref.shape[2]
    core = index % 2
    for i in range(wide_ref.shape[1] // share // 2):
        for to_ref, number in ((keep_ref, core), (send_ref, 1 - core)):
            cols = pl.ds(pl.multiple_of((2 * i + number) * share, share), share)
            to_ref[i] = nn(matrix, wide_ref[:, cols]).astype(BF16)


def front_kernel(
    step, place_ref, saved, top, gains, w_in, w_out,
    act0_ref, low_ref, xg0_ref, x1, g, gain1, wi1, wo1,
    x0, gain0, wi0, sems,
):
    lower = place_ref[0]
    upper = 1 - lower
    copies = [
        (gains.at[0, pl.ds(lower, 1)], gain0),
        (w_in.at[0, lower], wi0),
        (gains.at[0, pl.ds(upper, 1)], gain1),
        (w_in.at[0, upper], wi1),
        (w_out.at[0, upper], wo1),
    ]
    copies = [pltpu.make_async_copy(a, b, sems.at[i]) for i, (a, b) in enumerate(copies)]
    first = len(copies)
    copies_x0 = pieces(saved.at[0, lower], x0, sems, first)
    others = pieces(saved.at[0, upper], x1, sems, first + PIECES)
    others += pieces(top.at[upper], g, sems, first + 2 * PIECES)
    for copy in copies[0:2] + copies_x0 + copies[2:5] + others:
        copy.start()
    for copy in copies[0:2]:
        copy.wait()
    scale, raw = project(x0, gain0, wi0, xg0_ref, step, copies_x0)
    row = as_row(scale)
    pre = raw * row
    sig, slope = silu_slope(pre)
    act0_ref[...] = (pre * sig).astype(BF16)
    low_ref[0] = slope
    low_ref[1] = jnp.broadcast_to(row, raw.shape)
    for copy in copies[2:5] + others:
        copy.wait()


def upper_kernel(step, x, g, gain, wi, wo, xg_ref, act_ref, das_ref, da_ref, columns_ref):
    width = x.shape[1]
    scale, raw = project(x, gain, wi, xg_ref, step)
    delta = jnp.zeros(raw.shape, F32)
    for c in range(0, width, step):
        delta += nt(wo[:, c : c + step], g[:, c : c + step])
    row = as_row(scale)
    pre = raw * row
    sig, slope = silu_slope(pre)
    da = (delta * slope).astype(BF16)
    daf = da.astype(F32)
    inner = jnp.sum(daf * pre, axis=0, keepdims=True) * (1.0 / width)
    act_ref[...] = (pre * sig).astype(BF16)
    das_ref[...] = (daf * row).astype(BF16)
    da_ref[...] = da
    square = columns_ref.shape[1:]
    columns_ref[0] = jnp.broadcast_to(scale, square)
    columns_ref[1] = jnp.transpose(jnp.broadcast_to(inner * row * row, square))


def outgoing_kernel(step, x, g, gain, wi, da_ref, columns_ref, flow_ref):
    da = da_ref[...]
    scale = columns_ref[0][:, 0:1]
    pull = columns_ref[1][:, 0:1]
    for c in range(0, x.shape[1], step):
        cols = slice(c, c + step)
        dn = tn(da, wi[:, cols]) * gain[:, cols]
        flow = g[:, cols].astype(F32) + scale * dn - pull * x[:, cols].astype(F32)
        flow_ref[:, cols] = flow.astype(BF16)


def terms1_kernel(index_ref, g, xg_ref, act_ref, das_ref, _, keep_out, send_out, keep_in, send_in):
    fill(index_ref[0], act_ref[...], g, keep_out, send_out)
    fill(index_ref[0], das_ref[...], xg_ref, keep_in, send_in)


def terms_kernel(
    index_ref, flow_ref, act0_ref, keep_out1, send_out1, keep_in1, send_in1, keep_ref, send_ref
):
    fill(index_ref[0], act0_ref[...], flow_ref, keep_ref, send_ref)
    chips = keep_in1.shape[0]
    keep_ref[chips : 2 * chips] = keep_out1[...]
    send_ref[chips : 2 * chips] = send_out1[...]
    keep_ref[2 * chips : 3 * chips] = keep_in1[...]
    send_ref[2 * chips : 3 * chips] = send_in1[...]


def pick_kernel(place_ref, index_ref, w_out, out_ref, sems):
    half = out_ref.shape[1]
    cols = pl.ds(pl.multiple_of((index_ref[0] % 2) * half, half), half)
    copies = pieces(w_out.at[0, place_ref[0], :, cols], out_ref, sems, 0)
    for copy in copies:
        copy.start()
    for copy in copies:
        copy.wait()


def product(step, number, w_ref, flow_ref):
    half = w_ref.shape[1]
    delta = jnp.zeros((w_ref.shape[0], flow_ref.shape[0]), F32)
    for c in range(0, half, step):
        cols = pl.ds(pl.multiple_of(number * half + c, step), step)
        delta += nt(w_ref[:, c : c + step], flow_ref[:, cols])
    return delta


def flow_kernel(step, index_ref, flow_ref, own_ref, part_ref):
    part_ref[...] = product(step, index_ref[0] % 2, own_ref, flow_ref)


def flow_rest_kernel(step, index_ref, flow_ref, other_ref, part_ref, send_ref):
    rest = product(step, 1 - index_ref[0] % 2, other_ref, flow_ref)
    send_ref[...] = (part_ref[...] + rest).astype(BF16)


def lower_kernel(index_ref, xg0_ref, low_ref, got_ref, keep_ref, send_ref):
    da = (got_ref[...].astype(F32) * low_ref[0]).astype(BF16)
    das = (da.astype(F32) * low_ref[1]).astype(BF16)
    fill(index_ref[0], das, xg0_ref, keep_ref, send_ref)


def chip_kernel(place_ref, index_ref, keep, got, _, sum_ref, across):
    for i in range(keep.shape[0]):
        sum_ref[i] = (keep[i].astype(F32) + got[i].astype(F32)).astype(BF16)
    row = (index_ref[0] // 2) % 2
    first = (1 - place_ref[0]) * (2 * across.shape[0]) + 1 - row
    for i in range(across.shape[0]):
        across[i] = sum_ref[first + 2 * i]


def x_first(section, index):
    return (index % 2 == 0) | (section == (index // 2) % 2)


def plane_kernel(
    place_ref, index_ref, sums, keep0, got0, own_ref, first_ref, second_ref, across
):
    rank = keep0.shape[1]
    chips = keep0.shape[0]
    row = (index_ref[0] // 2) % 2

    def terms_in(section, block):
        if section == 0:
            return (keep0[block].astype(F32) + got0[block].astype(F32)).astype(BF16)
        return sums[2 * chips + block]

    def order(near, along_x, along_y):
        far = 1 - near
        for i in range(own_ref.shape[0]):
            across[i] = terms_in(far, 2 * i + 1 - row)
            for to_ref, section, number in (
                (along_x, far, row),
                (along_y, near, 1 - row),
                (own_ref, near, row),
            ):
                block = 2 * i + number
                to_ref[i, 0:rank] = terms_in(section, block)
                to_ref[i, rank : 2 * rank] = sums[section * chips + block]

    along_x = x_first(place_ref[0], index_ref[0])
    for place in range(2):
        for x_is_first, ways in ((True, (first_ref, second_ref)), (False, (second_ref, first_ref))):
            pl.when((place_ref[0] == place) & (along_x == x_is_first))(
                partial(order, place, *ways)
            )


def add_kernel(own, across_out, out_ref):
    rank = across_out.shape[1]
    out_ref[:, 0:rank] = own[:, 0:rank]
    for i in range(own.shape[0]):
        total = own[i, rank : 2 * rank].astype(F32) + across_out[i].astype(F32)
        out_ref[i, rank : 2 * rank] = total.astype(BF16)


def layer_routes(layers):
    if layers == 4:
        return [[1, 3, 0, 2], [3, 2, 1, 0], [2, 0, 3, 1]]
    return [[i ^ k for i in range(layers)] for k in range(1, layers)]


def layer_kernel(routes, index_ref, own, first, across_in, second, *out_refs):
    rank = across_in.shape[1]
    layer = index_ref[0] // 4
    for route, out_ref in zip([range(len(out_refs)), *routes], out_refs):
        block = sum(jnp.where(layer == i, target, 0) for i, target in enumerate(route))
        total = sum(ref[block].astype(F32) for ref in (own, first, second))
        out_ref[0:rank] = (total[0:rank] + across_in[block].astype(F32)).astype(BF16)
        out_ref[rank : 2 * rank] = total[rank : 2 * rank].astype(BF16)


def total_kernel(*refs):
    *got, in_far, out_far, in_ref, out_ref, sems = refs
    rank = in_ref.shape[1]
    copies = []
    for i, (ref, far) in enumerate(((in_ref, in_far), (out_ref, out_far))):
        ref[0] = sum(part[i * rank : (i + 1) * rank].astype(F32) for part in got)
        copies.append(pltpu.make_async_copy(ref, far, sems.at[i]))
        copies[i].start()
    for copy in copies:
        copy.wait()


def local(kernel, name, out_shapes, *operands, scratch=(), cost=None, out="near"):
    spaces = {"scalar": pltpu.SMEM, "far": pltpu.HBM, "near": pltpu.VMEM}
    out = pl.pallas_call(
        kernel,
        in_specs=[pl.BlockSpec(memory_space=spaces[kind]) for kind, _ in operands],
        out_specs=[pl.BlockSpec(memory_space=spaces[out])] * len(out_shapes),
        out_shape=[jax.ShapeDtypeStruct(shape, dtype) for shape, dtype in out_shapes],
        scratch_shapes=list(scratch),
        compiler_params=pltpu.CompilerParams(vmem_limit_bytes=VMEM_BYTES),
        cost_estimate=cost,
        name=name,
    )(*[array for _, array in operands])
    return out if len(out) > 1 else out[0]


def near(*arrays):
    return [("near", array) for array in arrays]


def pair_on_device(saved, top_grad, gains, adapter_in, adapter_out):
    count = lax.axis_size("dp")
    tokens, width = saved.shape[2:]
    rank = adapter_in.shape[3]
    share = width // count
    chips, layers = count // 2, count // 4
    place = ("scalar", lax.axis_index("section").astype(jnp.int32)[None])
    index = ("scalar", lax.axis_index("dp").astype(jnp.int32)[None])
    saved, top, gains, w_in, w_out = [
        ("far", pltpu.with_memory_space_constraint(a, pltpu.HBM))
        for a in (saved, top_grad, gains, jnp.swapaxes(adapter_in, 2, 3), adapter_out)
    ]

    def swapped(array, way):
        pairs = []
        for s in range(2):
            for d in range(count):
                over_section, bits = way(s, d) if callable(way) else way
                pairs.append((s * count + d, (s ^ over_section) * count + (d ^ bits)))
        return lax.ppermute(array, ("section", "dp"), pairs)

    def first_way(s, d):
        return (1, 0) if x_first(s, d) else (0, 2)

    def second_way(s, d):
        return (0, 2) if x_first(s, d) else (1, 0)

    sems = pltpu.SemaphoreType.DMA
    wide = ((tokens, width), BF16)
    thin = ((rank, width), BF16)
    gain = ((1, width), F32)
    small = ((rank, tokens), BF16)
    one = ((chips, rank, share), BF16)
    three = ((3 * chips, rank, share), BF16)
    quarter = ((layers, rank, share), BF16)
    double = ((layers, 2 * rank, share), BF16)
    along_x, other_core = (1, 0), (0, 1)

    mine = local(
        pick_kernel, "pick", [((rank, width // 2), BF16)], place, index, w_out, scratch=[sems((PIECES,))]
    )
    own_half = swapped(mine, along_x)
    act0, low, xg0, x1, g, gain1, wi1, wo1 = local(
        partial(front_kernel, share), "front",
        [small, ((2, rank, tokens), F32), wide, wide, wide, gain, thin, thin],
        place, saved, top, gains, w_in, w_out,
        scratch=[pltpu.VMEM(*wide), pltpu.VMEM(*gain), pltpu.VMEM(*thin), sems((5 + 3 * PIECES,))],
    )
    got_act0 = swapped(act0, along_x)
    xg1, act1, das1, da1, columns = local(
        partial(upper_kernel, share), "upper",
        [wide, small, small, small, ((2, tokens, tokens), F32)],
        *near(x1, g, gain1, wi1, wo1),
    )
    own_half, da1 = lax.optimization_barrier((own_half, da1))
    other_half = swapped(own_half, other_core)
    flow = local(
        partial(outgoing_kernel, share), "outgoing", [wide], *near(x1, g, gain1, wi1, da1, columns),
        cost=LONG,
    )
    part = local(
        partial(flow_kernel, share), "flow", [((rank, tokens), F32)], index, *near(flow, own_half)
    )
    delta = local(
        partial(flow_rest_kernel, share), "flow_rest", [small],
        index, *near(flow, other_half, part),
    )
    got_delta = swapped(delta, along_x)
    terms1 = local(
        terms1_kernel, "terms1", [one] * 4, index, *near(g, xg1, act1, das1, delta)
    )
    keep, send = local(
        terms_kernel, "terms", [three, three], index, *near(flow, got_act0, *terms1)
    )
    got = swapped(send, other_core)
    keep0, send0 = local(
        lower_kernel, "lower", [one, one], index, *near(xg0, low, got_delta), cost=LONG
    )
    got0 = swapped(send0, other_core)
    sums, across_out = local(
        chip_kernel, "chip", [three, quarter], place, index, *near(keep, got, keep0)
    )
    across_out = swapped(across_out, (1, 2))
    own, first, second, across_in = local(
        plane_kernel, "plane", [double, double, double, quarter],
        place, index, *near(sums, keep0, got0),
    )
    first = swapped(first, first_way)
    across_in = swapped(across_in, (1, 2))
    second = swapped(second, second_way)
    own = local(add_kernel, "add", [double], *near(own, across_out), cost=MEDIUM)
    routes = layer_routes(layers)
    mine, *others = local(
        partial(layer_kernel, routes), "layer", [((2 * rank, share), BF16)] * layers,
        index, *near(own, first, across_in, second),
    )
    others = [
        lax.ppermute(
            other,
            ("section", "dp"),
            [
                (s * count + d, s * count + 4 * route[d // 4] + d % 4)
                for s in range(2)
                for d in range(count)
            ],
        )
        for route, other in zip(routes, others)
    ]
    block = ((1, rank, share), F32)
    total_in, total_out = local(
        total_kernel, "total", [block, block], *near(mine, *others),
        scratch=[pltpu.VMEM(*block), pltpu.VMEM(*block), sems((2,))], out="far",
    )
    return (jnp.swapaxes(total_in, 1, 2), total_out)


def section_back(x, gain, weight_in, weight_out, upstream):
    xf = x.astype(F32)
    scale = lax.rsqrt(jnp.mean(xf * xf, axis=-1, keepdims=True) + EPS)
    normed = xf * scale
    hidden = (normed * gain).astype(BF16)
    pre = jnp.dot(hidden, weight_in, preferred_element_type=F32)
    sig, slope = silu_slope(pre)
    active = (pre * sig).astype(BF16)
    delta_act = jnp.dot(upstream, weight_out.T, preferred_element_type=F32)
    delta_pre = (delta_act * slope).astype(BF16)
    delta_norm = jnp.dot(delta_pre, weight_in.T, preferred_element_type=F32) * gain
    inner = jnp.mean(delta_norm * normed, axis=-1, keepdims=True)
    result = (upstream.astype(F32) + scale * (delta_norm - normed * inner)).astype(BF16)
    term_in = jnp.dot(hidden.T, delta_pre, preferred_element_type=F32)
    term_out = jnp.dot(active.T, upstream, preferred_element_type=F32)
    return (result, term_in, term_out)


def relay_on_device(saved, top_grad, gains, adapter_in, adapter_out):
    sections = lax.axis_size("section")
    place = lax.axis_index("section")
    width = top_grad.shape[2]
    rank = adapter_in.shape[3]
    zero_in = jnp.zeros((width, rank), F32)
    zero_out = jnp.zeros((rank, width), F32)

    def step(turn, flows, sums):
        leaving, added = [], []
        for replica in (0, 1):
            serves = place == (sections - 1 - turn if replica == 0 else turn)
            result, term_in, term_out = lax.cond(
                serves,
                partial(
                    section_back,
                    saved[0, replica],
                    gains[0, replica],
                    adapter_in[0, replica],
                    adapter_out[0, replica],
                ),
                lambda flow: (flow, zero_in, zero_out),
                flows[replica],
            )
            leaving.append(result)
            added += [sums[2 * replica] + term_in, sums[2 * replica + 1] + term_out]
        return leaving, added

    down = [(i, i - 1) for i in range(1, sections)]
    up = [(i, i + 1) for i in range(sections - 1)]

    def turn_and_pass(turn, carry):
        leaving, sums = step(turn, carry[0], carry[1])
        return (
            [lax.ppermute(leaving[0], "section", down), lax.ppermute(leaving[1], "section", up)],
            sums,
        )

    start = ([top_grad[0], top_grad[1]], [zero_in, zero_out, zero_in, zero_out])
    flows, sums = lax.fori_loop(0, sections - 1, turn_and_pass, start)
    _, sums = step(sections - 1, flows, sums)
    shares = [
        lax.psum_scatter(term, "dp", scatter_dimension=i % 2, tiled=True)
        for i, term in enumerate(sums)
    ]
    mirror = [(i, sections - 1 - i) for i in range(sections)]
    total_in = shares[0] + lax.ppermute(shares[2], "section", mirror)
    total_out = shares[1] + lax.ppermute(shares[3], "section", mirror)
    return (total_in[None], total_out[None])


def solution(mesh):
    in_specs = (
        P("section", None, "dp", None),
        P(None, "dp", None),
        P("section", None, None),
        P("section", None, None, None),
        P("section", None, None, None),
    )
    out_specs = (P("section", "dp", None), P("section", None, "dp"))

    def run(saved, *others):
        share = saved.shape[3] // mesh.shape["dp"]
        count = mesh.shape["dp"]
        pair = mesh.shape["section"] == 2 and share % 128 == 0
        pair = pair and count >= 4 and count & (count - 1) == 0
        on_device = pair_on_device if pair else relay_on_device
        return jax.shard_map(
            on_device, mesh=mesh, in_specs=in_specs, out_specs=out_specs, check_vma=False
        )(saved, *others)

    return run
```

```python
from functools import partial

import jax
import jax.numpy as jnp
from jax import lax
from jax.experimental import pallas as pl
from jax.experimental.pallas import tpu as pltpu
from jax.sharding import PartitionSpec as P

EPS = 1e-05
VMEM_BYTES = 24 * 1024 * 1024
F32 = jnp.float32
BF16 = jnp.bfloat16


MEDIUM = pl.CostEstimate(flops=10**9, bytes_accessed=2**20, transcendentals=0)
LONG = pl.CostEstimate(flops=2 * 10**10, bytes_accessed=2**20, transcendentals=0)


def nn(a, b):
    return lax.dot_general(a, b, (((1,), (0,)), ((), ())), preferred_element_type=F32)


def nt(a, b):
    return lax.dot_general(a, b, (((1,), (1,)), ((), ())), preferred_element_type=F32)


def tn(a, b):
    return lax.dot_general(a, b, (((0,), (0,)), ((), ())), preferred_element_type=F32)


def as_row(column):
    count = column.shape[0]
    return jnp.transpose(jnp.broadcast_to(column, (count, count)))[0:1, :]


def silu_slope(pre):
    sig = jax.nn.sigmoid(pre)
    return sig, sig * (1.0 + pre * (1.0 - sig))


PIECES = 4


def pieces(source, target, sems, first):
    step = target.shape[-1] // PIECES
    copies = []
    for i in range(PIECES):
        cols = pl.ds(i * step, step)
        copies.append(
            pltpu.make_async_copy(source.at[:, cols], target.at[:, cols], sems.at[first + i])
        )
    return copies


def project(x_ref, gain_ref, w_ref, xg_ref, step, copies=()):
    tokens, width = x_ref.shape
    squares = jnp.zeros((tokens, 128), F32)
    pre = jnp.zeros((w_ref.shape[0], tokens), F32)
    for c in range(0, width, step):
        if copies and c % (width // len(copies)) == 0:
            copies[c * len(copies) // width].wait()
        x = x_ref[:, c : c + step].astype(F32)
        for k in range(0, step, 128):
            part = x[:, k : k + 128]
            squares += part * part
        xg = (x * gain_ref[:, c : c + step]).astype(BF16)
        xg_ref[:, c : c + step] = xg
        pre += nt(w_ref[:, c : c + step], xg)
    mean = jnp.sum(squares, axis=1, keepdims=True) * (1.0 / width)
    scale = lax.rsqrt(mean + EPS)
    return scale, pre


def fill(index, matrix, wide_ref, keep_ref, send_ref):
    share = keep_ref.shape[2]
    core = index % 2
    for i in range(wide_ref.shape[1] // share // 2):
        for to_ref, number in ((keep_ref, core), (send_ref, 1 - core)):
            cols = pl.ds(pl.multiple_of((2 * i + number) * share, share), share)
            to_ref[i] = nn(matrix, wide_ref[:, cols]).astype(BF16)


def front_kernel(
    step, place_ref, saved, top, gains, w_in, w_out,
    act0_ref, low_ref, xg0_ref, x1, g, gain1, wi1, wo1,
    x0, gain0, wi0, sems,
):
    lower = place_ref[0]
    upper = 1 - lower
    copies = [
        (gains.at[0, pl.ds(lower, 1)], gain0),
        (w_in.at[0, lower], wi0),
        (gains.at[0, pl.ds(upper, 1)], gain1),
        (w_in.at[0, upper], wi1),
        (w_out.at[0, upper], wo1),
    ]
    copies = [pltpu.make_async_copy(a, b, sems.at[i]) for i, (a, b) in enumerate(copies)]
    first = len(copies)
    copies_x0 = pieces(saved.at[0, lower], x0, sems, first)
    others = pieces(saved.at[0, upper], x1, sems, first + PIECES)
    others += pieces(top.at[upper], g, sems, first + 2 * PIECES)
    for copy in copies[0:2] + copies_x0 + copies[2:5] + others:
        copy.start()
    for copy in copies[0:2]:
        copy.wait()
    scale, raw = project(x0, gain0, wi0, xg0_ref, step, copies_x0)
    row = as_row(scale)
    pre = raw * row
    sig, slope = silu_slope(pre)
    act0_ref[...] = (pre * sig).astype(BF16)
    low_ref[0] = slope
    low_ref[1] = jnp.broadcast_to(row, raw.shape)
    for copy in copies[2:5] + others:
        copy.wait()


def upper_kernel(step, x, g, gain, wi, wo, xg_ref, act_ref, das_ref, da_ref, columns_ref):
    width = x.shape[1]
    scale, raw = project(x, gain, wi, xg_ref, step)
    delta = jnp.zeros(raw.shape, F32)
    for c in range(0, width, step):
        delta += nt(wo[:, c : c + step], g[:, c : c + step])
    row = as_row(scale)
    pre = raw * row
    sig, slope = silu_slope(pre)
    da = (delta * slope).astype(BF16)
    daf = da.astype(F32)
    inner = jnp.sum(daf * pre, axis=0, keepdims=True) * (1.0 / width)
    act_ref[...] = (pre * sig).astype(BF16)
    das_ref[...] = (daf * row).astype(BF16)
    da_ref[...] = da
    square = columns_ref.shape[1:]
    columns_ref[0] = jnp.broadcast_to(scale, square)
    columns_ref[1] = jnp.transpose(jnp.broadcast_to(inner * row * row, square))


def outgoing_kernel(step, x, g, gain, wi, da_ref, columns_ref, flow_ref):
    da = da_ref[...]
    scale = columns_ref[0][:, 0:1]
    pull = columns_ref[1][:, 0:1]
    for c in range(0, x.shape[1], step):
        cols = slice(c, c + step)
        dn = tn(da, wi[:, cols]) * gain[:, cols]
        flow = g[:, cols].astype(F32) + scale * dn - pull * x[:, cols].astype(F32)
        flow_ref[:, cols] = flow.astype(BF16)


def terms1_kernel(index_ref, g, xg_ref, act_ref, das_ref, _, keep_out, send_out, keep_in, send_in):
    fill(index_ref[0], act_ref[...], g, keep_out, send_out)
    fill(index_ref[0], das_ref[...], xg_ref, keep_in, send_in)


def terms_kernel(
    index_ref, flow_ref, act0_ref, keep_out1, send_out1, keep_in1, send_in1, keep_ref, send_ref
):
    fill(index_ref[0], act0_ref[...], flow_ref, keep_ref, send_ref)
    chips = keep_in1.shape[0]
    keep_ref[chips : 2 * chips] = keep_out1[...]
    send_ref[chips : 2 * chips] = send_out1[...]
    keep_ref[2 * chips : 3 * chips] = keep_in1[...]
    send_ref[2 * chips : 3 * chips] = send_in1[...]


def pick_kernel(place_ref, index_ref, w_out, out_ref, sems):
    half = out_ref.shape[1]
    cols = pl.ds(pl.multiple_of((index_ref[0] % 2) * half, half), half)
    copies = pieces(w_out.at[0, place_ref[0], :, cols], out_ref, sems, 0)
    for copy in copies:
        copy.start()
    for copy in copies:
        copy.wait()


def product(step, number, w_ref, flow_ref):
    half = w_ref.shape[1]
    delta = jnp.zeros((w_ref.shape[0], flow_ref.shape[0]), F32)
    for c in range(0, half, step):
        cols = pl.ds(pl.multiple_of(number * half + c, step), step)
        delta += nt(w_ref[:, c : c + step], flow_ref[:, cols])
    return delta


def flow_kernel(step, index_ref, flow_ref, own_ref, part_ref):
    part_ref[...] = product(step, index_ref[0] % 2, own_ref, flow_ref)


def flow_rest_kernel(step, index_ref, flow_ref, other_ref, part_ref, send_ref):
    rest = product(step, 1 - index_ref[0] % 2, other_ref, flow_ref)
    send_ref[...] = (part_ref[...] + rest).astype(BF16)


def lower_kernel(index_ref, xg0_ref, low_ref, got_ref, keep_ref, send_ref):
    da = (got_ref[...].astype(F32) * low_ref[0]).astype(BF16)
    das = (da.astype(F32) * low_ref[1]).astype(BF16)
    fill(index_ref[0], das, xg0_ref, keep_ref, send_ref)


def chip_kernel(place_ref, index_ref, keep, got, _, sum_ref, across):
    for i in range(keep.shape[0]):
        sum_ref[i] = (keep[i].astype(F32) + got[i].astype(F32)).astype(BF16)
    row = (index_ref[0] // 2) % 2
    first = (1 - place_ref[0]) * (2 * across.shape[0]) + 1 - row
    for i in range(across.shape[0]):
        across[i] = sum_ref[first + 2 * i]


def x_first(section, index):
    return (index % 2 == 0) | (section == (index // 2) % 2)


def plane_kernel(
    place_ref, index_ref, sums, keep0, got0, own_ref, first_ref, second_ref, across
):
    rank = keep0.shape[1]
    chips = keep0.shape[0]
    row = (index_ref[0] // 2) % 2

    def terms_in(section, block):
        if section == 0:
            return (keep0[block].astype(F32) + got0[block].astype(F32)).astype(BF16)
        return sums[2 * chips + block]

    def order(near, along_x, along_y):
        far = 1 - near
        for i in range(own_ref.shape[0]):
            across[i] = terms_in(far, 2 * i + 1 - row)
            for to_ref, section, number in (
                (along_x, far, row),
                (along_y, near, 1 - row),
                (own_ref, near, row),
            ):
                block = 2 * i + number
                to_ref[i, 0:rank] = terms_in(section, block)
                to_ref[i, rank : 2 * rank] = sums[section * chips + block]

    along_x = x_first(place_ref[0], index_ref[0])
    for place in range(2):
        for x_is_first, ways in ((True, (first_ref, second_ref)), (False, (second_ref, first_ref))):
            pl.when((place_ref[0] == place) & (along_x == x_is_first))(
                partial(order, place, *ways)
            )


def add_kernel(own, across_out, out_ref):
    rank = across_out.shape[1]
    out_ref[:, 0:rank] = own[:, 0:rank]
    for i in range(own.shape[0]):
        total = own[i, rank : 2 * rank].astype(F32) + across_out[i].astype(F32)
        out_ref[i, rank : 2 * rank] = total.astype(BF16)


def layer_routes(layers):
    if layers == 4:
        return [[2, 3, 1, 0], [3, 2, 0, 1], [1, 0, 3, 2]]
    return [[i ^ k for i in range(layers)] for k in range(1, layers)]


def layer_kernel(routes, index_ref, own, first, across_in, second, *out_refs):
    rank = across_in.shape[1]
    layer = index_ref[0] // 4
    for route, out_ref in zip([range(len(out_refs)), *routes], out_refs):
        block = sum(jnp.where(layer == i, target, 0) for i, target in enumerate(route))
        total = sum(ref[block].astype(F32) for ref in (own, first, second))
        out_ref[0:rank] = (total[0:rank] + across_in[block].astype(F32)).astype(BF16)
        out_ref[rank : 2 * rank] = total[rank : 2 * rank].astype(BF16)


def total_kernel(*refs):
    *got, in_far, out_far, in_ref, out_ref, sems = refs
    rank = in_ref.shape[1]
    copies = []
    for i, (ref, far) in enumerate(((in_ref, in_far), (out_ref, out_far))):
        ref[0] = sum(part[i * rank : (i + 1) * rank].astype(F32) for part in got)
        copies.append(pltpu.make_async_copy(ref, far, sems.at[i]))
        copies[i].start()
    for copy in copies:
        copy.wait()


def local(kernel, name, out_shapes, *operands, scratch=(), cost=None, out="near"):
    spaces = {"scalar": pltpu.SMEM, "far": pltpu.HBM, "near": pltpu.VMEM}
    out = pl.pallas_call(
        kernel,
        in_specs=[pl.BlockSpec(memory_space=spaces[kind]) for kind, _ in operands],
        out_specs=[pl.BlockSpec(memory_space=spaces[out])] * len(out_shapes),
        out_shape=[jax.ShapeDtypeStruct(shape, dtype) for shape, dtype in out_shapes],
        scratch_shapes=list(scratch),
        compiler_params=pltpu.CompilerParams(vmem_limit_bytes=VMEM_BYTES),
        cost_estimate=cost,
        name=name,
    )(*[array for _, array in operands])
    return out if len(out) > 1 else out[0]


def near(*arrays):
    return [("near", array) for array in arrays]


def pair_on_device(saved, top_grad, gains, adapter_in, adapter_out):
    count = lax.axis_size("dp")
    tokens, width = saved.shape[2:]
    rank = adapter_in.shape[3]
    share = width // count
    chips, layers = count // 2, count // 4
    place = ("scalar", lax.axis_index("section").astype(jnp.int32)[None])
    index = ("scalar", lax.axis_index("dp").astype(jnp.int32)[None])
    saved, top, gains, w_in, w_out = [
        ("far", pltpu.with_memory_space_constraint(a, pltpu.HBM))
        for a in (saved, top_grad, gains, jnp.swapaxes(adapter_in, 2, 3), adapter_out)
    ]

    def swapped(array, way):
        pairs = []
        for s in range(2):
            for d in range(count):
                over_section, bits = way(s, d) if callable(way) else way
                pairs.append((s * count + d, (s ^ over_section) * count + (d ^ bits)))
        return lax.ppermute(array, ("section", "dp"), pairs)

    def first_way(s, d):
        return (1, 0) if x_first(s, d) else (0, 2)

    def second_way(s, d):
        return (0, 2) if x_first(s, d) else (1, 0)

    sems = pltpu.SemaphoreType.DMA
    wide = ((tokens, width), BF16)
    thin = ((rank, width), BF16)
    gain = ((1, width), F32)
    small = ((rank, tokens), BF16)
    one = ((chips, rank, share), BF16)
    three = ((3 * chips, rank, share), BF16)
    quarter = ((layers, rank, share), BF16)
    double = ((layers, 2 * rank, share), BF16)
    along_x, other_core = (1, 0), (0, 1)

    mine = local(
        pick_kernel, "pick", [((rank, width // 2), BF16)], place, index, w_out, scratch=[sems((PIECES,))]
    )
    own_half = swapped(mine, along_x)
    act0, low, xg0, x1, g, gain1, wi1, wo1 = local(
        partial(front_kernel, share), "front",
        [small, ((2, rank, tokens), F32), wide, wide, wide, gain, thin, thin],
        place, saved, top, gains, w_in, w_out,
        scratch=[pltpu.VMEM(*wide), pltpu.VMEM(*gain), pltpu.VMEM(*thin), sems((5 + 3 * PIECES,))],
    )
    got_act0 = swapped(act0, along_x)
    xg1, act1, das1, da1, columns = local(
        partial(upper_kernel, share), "upper",
        [wide, small, small, small, ((2, tokens, tokens), F32)],
        *near(x1, g, gain1, wi1, wo1),
    )
    own_half, da1 = lax.optimization_barrier((own_half, da1))
    other_half = swapped(own_half, other_core)
    flow = local(
        partial(outgoing_kernel, share), "outgoing", [wide], *near(x1, g, gain1, wi1, da1, columns),
        cost=LONG,
    )
    part = local(
        partial(flow_kernel, share), "flow", [((rank, tokens), F32)], index, *near(flow, own_half)
    )
    delta = local(
        partial(flow_rest_kernel, share), "flow_rest", [small],
        index, *near(flow, other_half, part),
    )
    got_delta = swapped(delta, along_x)
    terms1 = local(
        terms1_kernel, "terms1", [one] * 4, index, *near(g, xg1, act1, das1, delta)
    )
    keep, send = local(
        terms_kernel, "terms", [three, three], index, *near(flow, got_act0, *terms1)
    )
    got = swapped(send, other_core)
    keep0, send0 = local(
        lower_kernel, "lower", [one, one], index, *near(xg0, low, got_delta), cost=LONG
    )
    got0 = swapped(send0, other_core)
    sums, across_out = local(
        chip_kernel, "chip", [three, quarter], place, index, *near(keep, got, keep0)
    )
    across_out = swapped(across_out, (1, 2))
    own, first, second, across_in = local(
        plane_kernel, "plane", [double, double, double, quarter],
        place, index, *near(sums, keep0, got0),
    )
    first = swapped(first, first_way)
    across_in = swapped(across_in, (1, 2))
    second = swapped(second, second_way)
    own = local(add_kernel, "add", [double], *near(own, across_out), cost=MEDIUM)
    routes = layer_routes(layers)
    mine, *others = local(
        partial(layer_kernel, routes), "layer", [((2 * rank, share), BF16)] * layers,
        index, *near(own, first, across_in, second),
    )
    others = [
        lax.ppermute(
            other,
            ("section", "dp"),
            [
                (s * count + d, s * count + 4 * route[d // 4] + d % 4)
                for s in range(2)
                for d in range(count)
            ],
        )
        for route, other in zip(routes, others)
    ]
    block = ((1, rank, share), F32)
    total_in, total_out = local(
        total_kernel, "total", [block, block], *near(mine, *others),
        scratch=[pltpu.VMEM(*block), pltpu.VMEM(*block), sems((2,))], out="far",
    )
    return (jnp.swapaxes(total_in, 1, 2), total_out)


def section_back(x, gain, weight_in, weight_out, upstream):
    xf = x.astype(F32)
    scale = lax.rsqrt(jnp.mean(xf * xf, axis=-1, keepdims=True) + EPS)
    normed = xf * scale
    hidden = (normed * gain).astype(BF16)
    pre = jnp.dot(hidden, weight_in, preferred_element_type=F32)
    sig, slope = silu_slope(pre)
    active = (pre * sig).astype(BF16)
    delta_act = jnp.dot(upstream, weight_out.T, preferred_element_type=F32)
    delta_pre = (delta_act * slope).astype(BF16)
    delta_norm = jnp.dot(delta_pre, weight_in.T, preferred_element_type=F32) * gain
    inner = jnp.mean(delta_norm * normed, axis=-1, keepdims=True)
    result = (upstream.astype(F32) + scale * (delta_norm - normed * inner)).astype(BF16)
    term_in = jnp.dot(hidden.T, delta_pre, preferred_element_type=F32)
    term_out = jnp.dot(active.T, upstream, preferred_element_type=F32)
    return (result, term_in, term_out)


def relay_on_device(saved, top_grad, gains, adapter_in, adapter_out):
    sections = lax.axis_size("section")
    place = lax.axis_index("section")
    width = top_grad.shape[2]
    rank = adapter_in.shape[3]
    zero_in = jnp.zeros((width, rank), F32)
    zero_out = jnp.zeros((rank, width), F32)

    def step(turn, flows, sums):
        leaving, added = [], []
        for replica in (0, 1):
            serves = place == (sections - 1 - turn if replica == 0 else turn)
            result, term_in, term_out = lax.cond(
                serves,
                partial(
                    section_back,
                    saved[0, replica],
                    gains[0, replica],
                    adapter_in[0, replica],
                    adapter_out[0, replica],
                ),
                lambda flow: (flow, zero_in, zero_out),
                flows[replica],
            )
            leaving.append(result)
            added += [sums[2 * replica] + term_in, sums[2 * replica + 1] + term_out]
        return leaving, added

    down = [(i, i - 1) for i in range(1, sections)]
    up = [(i, i + 1) for i in range(sections - 1)]

    def turn_and_pass(turn, carry):
        leaving, sums = step(turn, carry[0], carry[1])
        return (
            [lax.ppermute(leaving[0], "section", down), lax.ppermute(leaving[1], "section", up)],
            sums,
        )

    start = ([top_grad[0], top_grad[1]], [zero_in, zero_out, zero_in, zero_out])
    flows, sums = lax.fori_loop(0, sections - 1, turn_and_pass, start)
    _, sums = step(sections - 1, flows, sums)
    shares = [
        lax.psum_scatter(term, "dp", scatter_dimension=i % 2, tiled=True)
        for i, term in enumerate(sums)
    ]
    mirror = [(i, sections - 1 - i) for i in range(sections)]
    total_in = shares[0] + lax.ppermute(shares[2], "section", mirror)
    total_out = shares[1] + lax.ppermute(shares[3], "section", mirror)
    return (total_in[None], total_out[None])


def solution(mesh):
    in_specs = (
        P("section", None, "dp", None),
        P(None, "dp", None),
        P("section", None, None),
        P("section", None, None, None),
        P("section", None, None, None),
    )
    out_specs = (P("section", "dp", None), P("section", None, "dp"))

    def run(saved, *others):
        share = saved.shape[3] // mesh.shape["dp"]
        count = mesh.shape["dp"]
        pair = mesh.shape["section"] == 2 and share % 128 == 0
        pair = pair and count >= 4 and count & (count - 1) == 0
        on_device = pair_on_device if pair else relay_on_device
        return jax.shard_map(
            on_device, mesh=mesh, in_specs=in_specs, out_specs=out_specs, check_vma=False
        )(saved, *others)

    return run
```

```python
from functools import partial

import jax
import jax.numpy as jnp
from jax import lax
from jax.experimental import pallas as pl
from jax.experimental.pallas import tpu as pltpu
from jax.sharding import PartitionSpec as P

EPS = 1e-05
VMEM_BYTES = 24 * 1024 * 1024
F32 = jnp.float32
BF16 = jnp.bfloat16


MEDIUM = pl.CostEstimate(flops=10**9, bytes_accessed=2**20, transcendentals=0)
LONG = pl.CostEstimate(flops=2 * 10**10, bytes_accessed=2**20, transcendentals=0)


def nn(a, b):
    return lax.dot_general(a, b, (((1,), (0,)), ((), ())), preferred_element_type=F32)


def nt(a, b):
    return lax.dot_general(a, b, (((1,), (1,)), ((), ())), preferred_element_type=F32)


def tn(a, b):
    return lax.dot_general(a, b, (((0,), (0,)), ((), ())), preferred_element_type=F32)


def as_row(column):
    count = column.shape[0]
    return jnp.transpose(jnp.broadcast_to(column, (count, count)))[0:1, :]


def silu_slope(pre):
    sig = jax.nn.sigmoid(pre)
    return sig, sig * (1.0 + pre * (1.0 - sig))


PIECES = 4


def pieces(source, target, sems, first):
    step = target.shape[-1] // PIECES
    copies = []
    for i in range(PIECES):
        cols = pl.ds(i * step, step)
        copies.append(
            pltpu.make_async_copy(source.at[:, cols], target.at[:, cols], sems.at[first + i])
        )
    return copies


def project(x_ref, gain_ref, w_ref, xg_ref, step, copies=()):
    tokens, width = x_ref.shape
    squares = jnp.zeros((tokens, 128), F32)
    pre = jnp.zeros((w_ref.shape[0], tokens), F32)
    for c in range(0, width, step):
        if copies and c % (width // len(copies)) == 0:
            copies[c * len(copies) // width].wait()
        x = x_ref[:, c : c + step].astype(F32)
        for k in range(0, step, 128):
            part = x[:, k : k + 128]
            squares += part * part
        xg = (x * gain_ref[:, c : c + step]).astype(BF16)
        xg_ref[:, c : c + step] = xg
        pre += nt(w_ref[:, c : c + step], xg)
    mean = jnp.sum(squares, axis=1, keepdims=True) * (1.0 / width)
    scale = lax.rsqrt(mean + EPS)
    return scale, pre


def fill(index, matrix, wide_ref, keep_ref, send_ref):
    share = keep_ref.shape[2]
    core = index % 2
    for i in range(wide_ref.shape[1] // share // 2):
        for to_ref, number in ((keep_ref, core), (send_ref, 1 - core)):
            cols = pl.ds(pl.multiple_of((2 * i + number) * share, share), share)
            to_ref[i] = nn(matrix, wide_ref[:, cols]).astype(BF16)


def front_kernel(
    step, place_ref, saved, top, gains, w_in, w_out,
    act0_ref, low_ref, xg0_ref, x1, g, gain1, wi1, wo1,
    x0, gain0, wi0, sems,
):
    lower = place_ref[0]
    upper = 1 - lower
    copies = [
        (gains.at[0, pl.ds(lower, 1)], gain0),
        (w_in.at[0, lower], wi0),
        (gains.at[0, pl.ds(upper, 1)], gain1),
        (w_in.at[0, upper], wi1),
        (w_out.at[0, upper], wo1),
    ]
    copies = [pltpu.make_async_copy(a, b, sems.at[i]) for i, (a, b) in enumerate(copies)]
    first = len(copies)
    copies_x0 = pieces(saved.at[0, lower], x0, sems, first)
    others = pieces(saved.at[0, upper], x1, sems, first + PIECES)
    others += pieces(top.at[upper], g, sems, first + 2 * PIECES)
    for copy in copies[0:2] + copies_x0 + copies[2:5] + others:
        copy.start()
    for copy in copies[0:2]:
        copy.wait()
    scale, raw = project(x0, gain0, wi0, xg0_ref, step, copies_x0)
    row = as_row(scale)
    pre = raw * row
    sig, slope = silu_slope(pre)
    act0_ref[...] = (pre * sig).astype(BF16)
    low_ref[0] = slope
    low_ref[1] = jnp.broadcast_to(row, raw.shape)
    for copy in copies[2:5] + others:
        copy.wait()


def upper_kernel(step, x, g, gain, wi, wo, xg_ref, act_ref, das_ref, da_ref, columns_ref):
    width = x.shape[1]
    scale, raw = project(x, gain, wi, xg_ref, step)
    delta = jnp.zeros(raw.shape, F32)
    for c in range(0, width, step):
        delta += nt(wo[:, c : c + step], g[:, c : c + step])
    row = as_row(scale)
    pre = raw * row
    sig, slope = silu_slope(pre)
    da = (delta * slope).astype(BF16)
    daf = da.astype(F32)
    inner = jnp.sum(daf * pre, axis=0, keepdims=True) * (1.0 / width)
    act_ref[...] = (pre * sig).astype(BF16)
    das_ref[...] = (daf * row).astype(BF16)
    da_ref[...] = da
    square = columns_ref.shape[1:]
    columns_ref[0] = jnp.broadcast_to(scale, square)
    columns_ref[1] = jnp.transpose(jnp.broadcast_to(inner * row * row, square))


def outgoing_kernel(step, x, g, gain, wi, da_ref, columns_ref, flow_ref):
    da = da_ref[...]
    scale = columns_ref[0][:, 0:1]
    pull = columns_ref[1][:, 0:1]
    for c in range(0, x.shape[1], step):
        cols = slice(c, c + step)
        dn = tn(da, wi[:, cols]) * gain[:, cols]
        flow = g[:, cols].astype(F32) + scale * dn - pull * x[:, cols].astype(F32)
        flow_ref[:, cols] = flow.astype(BF16)


def terms1_kernel(index_ref, g, xg_ref, act_ref, das_ref, _, keep_out, send_out, keep_in, send_in):
    fill(index_ref[0], act_ref[...], g, keep_out, send_out)
    fill(index_ref[0], das_ref[...], xg_ref, keep_in, send_in)


def terms_kernel(
    index_ref, flow_ref, act0_ref, keep_out1, send_out1, keep_in1, send_in1, keep_ref, send_ref
):
    fill(index_ref[0], act0_ref[...], flow_ref, keep_ref, send_ref)
    chips = keep_in1.shape[0]
    keep_ref[chips : 2 * chips] = keep_out1[...]
    send_ref[chips : 2 * chips] = send_out1[...]
    keep_ref[2 * chips : 3 * chips] = keep_in1[...]
    send_ref[2 * chips : 3 * chips] = send_in1[...]


def pick_kernel(place_ref, index_ref, w_out, out_ref, sems):
    half = out_ref.shape[1]
    cols = pl.ds(pl.multiple_of((index_ref[0] % 2) * half, half), half)
    copies = pieces(w_out.at[0, place_ref[0], :, cols], out_ref, sems, 0)
    for copy in copies:
        copy.start()
    for copy in copies:
        copy.wait()


def product(step, number, w_ref, flow_ref):
    half = w_ref.shape[1]
    delta = jnp.zeros((w_ref.shape[0], flow_ref.shape[0]), F32)
    for c in range(0, half, step):
        cols = pl.ds(pl.multiple_of(number * half + c, step), step)
        delta += nt(w_ref[:, c : c + step], flow_ref[:, cols])
    return delta


def flow_kernel(step, index_ref, flow_ref, own_ref, part_ref):
    part_ref[...] = product(step, index_ref[0] % 2, own_ref, flow_ref)


def flow_rest_kernel(step, index_ref, flow_ref, other_ref, part_ref, send_ref):
    rest = product(step, 1 - index_ref[0] % 2, other_ref, flow_ref)
    send_ref[...] = (part_ref[...] + rest).astype(BF16)


def lower_kernel(index_ref, xg0_ref, low_ref, got_ref, keep_ref, send_ref):
    da = (got_ref[...].astype(F32) * low_ref[0]).astype(BF16)
    das = (da.astype(F32) * low_ref[1]).astype(BF16)
    fill(index_ref[0], das, xg0_ref, keep_ref, send_ref)


def chip_kernel(place_ref, index_ref, keep, got, _, sum_ref, across):
    for i in range(keep.shape[0]):
        sum_ref[i] = (keep[i].astype(F32) + got[i].astype(F32)).astype(BF16)
    row = (index_ref[0] // 2) % 2
    first = (1 - place_ref[0]) * (2 * across.shape[0]) + 1 - row
    for i in range(across.shape[0]):
        across[i] = sum_ref[first + 2 * i]


def x_first(section, index):
    return section == (index // 2) % 2


def plane_kernel(
    place_ref, index_ref, sums, keep0, got0, own_ref, first_ref, second_ref, across
):
    rank = keep0.shape[1]
    chips = keep0.shape[0]
    row = (index_ref[0] // 2) % 2

    def terms_in(section, block):
        if section == 0:
            return (keep0[block].astype(F32) + got0[block].astype(F32)).astype(BF16)
        return sums[2 * chips + block]

    def order(near, along_x, along_y):
        far = 1 - near
        for i in range(own_ref.shape[0]):
            across[i] = terms_in(far, 2 * i + 1 - row)
            for to_ref, section, number in (
                (along_x, far, row),
                (along_y, near, 1 - row),
                (own_ref, near, row),
            ):
                block = 2 * i + number
                to_ref[i, 0:rank] = terms_in(section, block)
                to_ref[i, rank : 2 * rank] = sums[section * chips + block]

    along_x = x_first(place_ref[0], index_ref[0])
    for place in range(2):
        for x_is_first, ways in ((True, (first_ref, second_ref)), (False, (second_ref, first_ref))):
            pl.when((place_ref[0] == place) & (along_x == x_is_first))(
                partial(order, place, *ways)
            )


def add_kernel(own, across_out, out_ref):
    rank = across_out.shape[1]
    out_ref[:, 0:rank] = own[:, 0:rank]
    for i in range(own.shape[0]):
        total = own[i, rank : 2 * rank].astype(F32) + across_out[i].astype(F32)
        out_ref[i, rank : 2 * rank] = total.astype(BF16)


def layer_routes(layers):
    if layers == 4:
        return [[2, 3, 1, 0], [3, 2, 0, 1], [1, 0, 3, 2]]
    return [[i ^ k for i in range(layers)] for k in range(1, layers)]


def layer_kernel(routes, index_ref, own, first, across_in, second, *out_refs):
    rank = across_in.shape[1]
    layer = index_ref[0] // 4
    for route, out_ref in zip([range(len(out_refs)), *routes], out_refs):
        block = sum(jnp.where(layer == i, target, 0) for i, target in enumerate(route))
        total = sum(ref[block].astype(F32) for ref in (own, first, second))
        out_ref[0:rank] = (total[0:rank] + across_in[block].astype(F32)).astype(BF16)
        out_ref[rank : 2 * rank] = total[rank : 2 * rank].astype(BF16)


def total_kernel(*refs):
    *got, in_far, out_far, in_ref, out_ref, sems = refs
    rank = in_ref.shape[1]
    copies = []
    for i, (ref, far) in enumerate(((in_ref, in_far), (out_ref, out_far))):
        ref[0] = sum(part[i * rank : (i + 1) * rank].astype(F32) for part in got)
        copies.append(pltpu.make_async_copy(ref, far, sems.at[i]))
        copies[i].start()
    for copy in copies:
        copy.wait()


def local(kernel, name, out_shapes, *operands, scratch=(), cost=None, out="near"):
    spaces = {"scalar": pltpu.SMEM, "far": pltpu.HBM, "near": pltpu.VMEM}
    out = pl.pallas_call(
        kernel,
        in_specs=[pl.BlockSpec(memory_space=spaces[kind]) for kind, _ in operands],
        out_specs=[pl.BlockSpec(memory_space=spaces[out])] * len(out_shapes),
        out_shape=[jax.ShapeDtypeStruct(shape, dtype) for shape, dtype in out_shapes],
        scratch_shapes=list(scratch),
        compiler_params=pltpu.CompilerParams(vmem_limit_bytes=VMEM_BYTES),
        cost_estimate=cost,
        name=name,
    )(*[array for _, array in operands])
    return out if len(out) > 1 else out[0]


def near(*arrays):
    return [("near", array) for array in arrays]


def pair_on_device(saved, top_grad, gains, adapter_in, adapter_out):
    count = lax.axis_size("dp")
    tokens, width = saved.shape[2:]
    rank = adapter_in.shape[3]
    share = width // count
    chips, layers = count // 2, count // 4
    place = ("scalar", lax.axis_index("section").astype(jnp.int32)[None])
    index = ("scalar", lax.axis_index("dp").astype(jnp.int32)[None])
    saved, top, gains, w_in, w_out = [
        ("far", pltpu.with_memory_space_constraint(a, pltpu.HBM))
        for a in (saved, top_grad, gains, jnp.swapaxes(adapter_in, 2, 3), adapter_out)
    ]

    def swapped(array, way):
        pairs = []
        for s in range(2):
            for d in range(count):
                over_section, bits = way(s, d) if callable(way) else way
                pairs.append((s * count + d, (s ^ over_section) * count + (d ^ bits)))
        return lax.ppermute(array, ("section", "dp"), pairs)

    def first_way(s, d):
        return (1, 0) if x_first(s, d) else (0, 2)

    def second_way(s, d):
        return (0, 2) if x_first(s, d) else (1, 0)

    sems = pltpu.SemaphoreType.DMA
    wide = ((tokens, width), BF16)
    thin = ((rank, width), BF16)
    gain = ((1, width), F32)
    small = ((rank, tokens), BF16)
    one = ((chips, rank, share), BF16)
    three = ((3 * chips, rank, share), BF16)
    quarter = ((layers, rank, share), BF16)
    double = ((layers, 2 * rank, share), BF16)
    along_x, other_core = (1, 0), (0, 1)

    mine = local(
        pick_kernel, "pick", [((rank, width // 2), BF16)], place, index, w_out, scratch=[sems((PIECES,))]
    )
    own_half = swapped(mine, along_x)
    act0, low, xg0, x1, g, gain1, wi1, wo1 = local(
        partial(front_kernel, share), "front",
        [small, ((2, rank, tokens), F32), wide, wide, wide, gain, thin, thin],
        place, saved, top, gains, w_in, w_out,
        scratch=[pltpu.VMEM(*wide), pltpu.VMEM(*gain), pltpu.VMEM(*thin), sems((5 + 3 * PIECES,))],
    )
    got_act0 = swapped(act0, along_x)
    xg1, act1, das1, da1, columns = local(
        partial(upper_kernel, share), "upper",
        [wide, small, small, small, ((2, tokens, tokens), F32)],
        *near(x1, g, gain1, wi1, wo1),
    )
    own_half, da1 = lax.optimization_barrier((own_half, da1))
    other_half = swapped(own_half, other_core)
    flow = local(
        partial(outgoing_kernel, share), "outgoing", [wide], *near(x1, g, gain1, wi1, da1, columns),
        cost=LONG,
    )
    part = local(
        partial(flow_kernel, share), "flow", [((rank, tokens), F32)], index, *near(flow, own_half)
    )
    delta = local(
        partial(flow_rest_kernel, share), "flow_rest", [small],
        index, *near(flow, other_half, part),
    )
    got_delta = swapped(delta, along_x)
    terms1 = local(
        terms1_kernel, "terms1", [one] * 4, index, *near(g, xg1, act1, das1, delta)
    )
    keep, send = local(
        terms_kernel, "terms", [three, three], index, *near(flow, got_act0, *terms1)
    )
    got = swapped(send, other_core)
    keep0, send0 = local(
        lower_kernel, "lower", [one, one], index, *near(xg0, low, got_delta), cost=LONG
    )
    got0 = swapped(send0, other_core)
    sums, across_out = local(
        chip_kernel, "chip", [three, quarter], place, index, *near(keep, got, keep0)
    )
    across_out = swapped(across_out, (1, 2))
    own, first, second, across_in = local(
        plane_kernel, "plane", [double, double, double, quarter],
        place, index, *near(sums, keep0, got0),
    )
    first = swapped(first, first_way)
    across_in = swapped(across_in, (1, 2))
    second = swapped(second, second_way)
    own = local(add_kernel, "add", [double], *near(own, across_out), cost=MEDIUM)
    routes = layer_routes(layers)
    mine, *others = local(
        partial(layer_kernel, routes), "layer", [((2 * rank, share), BF16)] * layers,
        index, *near(own, first, across_in, second),
    )
    others = [
        lax.ppermute(
            other,
            ("section", "dp"),
            [
                (s * count + d, s * count + 4 * route[d // 4] + d % 4)
                for s in range(2)
                for d in range(count)
            ],
        )
        for route, other in zip(routes, others)
    ]
    block = ((1, rank, share), F32)
    total_in, total_out = local(
        total_kernel, "total", [block, block], *near(mine, *others),
        scratch=[pltpu.VMEM(*block), pltpu.VMEM(*block), sems((2,))], out="far",
    )
    return (jnp.swapaxes(total_in, 1, 2), total_out)


def section_back(x, gain, weight_in, weight_out, upstream):
    xf = x.astype(F32)
    scale = lax.rsqrt(jnp.mean(xf * xf, axis=-1, keepdims=True) + EPS)
    normed = xf * scale
    hidden = (normed * gain).astype(BF16)
    pre = jnp.dot(hidden, weight_in, preferred_element_type=F32)
    sig, slope = silu_slope(pre)
    active = (pre * sig).astype(BF16)
    delta_act = jnp.dot(upstream, weight_out.T, preferred_element_type=F32)
    delta_pre = (delta_act * slope).astype(BF16)
    delta_norm = jnp.dot(delta_pre, weight_in.T, preferred_element_type=F32) * gain
    inner = jnp.mean(delta_norm * normed, axis=-1, keepdims=True)
    result = (upstream.astype(F32) + scale * (delta_norm - normed * inner)).astype(BF16)
    term_in = jnp.dot(hidden.T, delta_pre, preferred_element_type=F32)
    term_out = jnp.dot(active.T, upstream, preferred_element_type=F32)
    return (result, term_in, term_out)


def relay_on_device(saved, top_grad, gains, adapter_in, adapter_out):
    sections = lax.axis_size("section")
    place = lax.axis_index("section")
    width = top_grad.shape[2]
    rank = adapter_in.shape[3]
    zero_in = jnp.zeros((width, rank), F32)
    zero_out = jnp.zeros((rank, width), F32)

    def step(turn, flows, sums):
        leaving, added = [], []
        for replica in (0, 1):
            serves = place == (sections - 1 - turn if replica == 0 else turn)
            result, term_in, term_out = lax.cond(
                serves,
                partial(
                    section_back,
                    saved[0, replica],
                    gains[0, replica],
                    adapter_in[0, replica],
                    adapter_out[0, replica],
                ),
                lambda flow: (flow, zero_in, zero_out),
                flows[replica],
            )
            leaving.append(result)
            added += [sums[2 * replica] + term_in, sums[2 * replica + 1] + term_out]
        return leaving, added

    down = [(i, i - 1) for i in range(1, sections)]
    up = [(i, i + 1) for i in range(sections - 1)]

    def turn_and_pass(turn, carry):
        leaving, sums = step(turn, carry[0], carry[1])
        return (
            [lax.ppermute(leaving[0], "section", down), lax.ppermute(leaving[1], "section", up)],
            sums,
        )

    start = ([top_grad[0], top_grad[1]], [zero_in, zero_out, zero_in, zero_out])
    flows, sums = lax.fori_loop(0, sections - 1, turn_and_pass, start)
    _, sums = step(sections - 1, flows, sums)
    shares = [
        lax.psum_scatter(term, "dp", scatter_dimension=i % 2, tiled=True)
        for i, term in enumerate(sums)
    ]
    mirror = [(i, sections - 1 - i) for i in range(sections)]
    total_in = shares[0] + lax.ppermute(shares[2], "section", mirror)
    total_out = shares[1] + lax.ppermute(shares[3], "section", mirror)
    return (total_in[None], total_out[None])


def solution(mesh):
    in_specs = (
        P("section", None, "dp", None),
        P(None, "dp", None),
        P("section", None, None),
        P("section", None, None, None),
        P("section", None, None, None),
    )
    out_specs = (P("section", "dp", None), P("section", None, "dp"))

    def run(saved, *others):
        share = saved.shape[3] // mesh.shape["dp"]
        count = mesh.shape["dp"]
        pair = mesh.shape["section"] == 2 and share % 128 == 0
        pair = pair and count >= 4 and count & (count - 1) == 0
        on_device = pair_on_device if pair else relay_on_device
        return jax.shard_map(
            on_device, mesh=mesh, in_specs=in_specs, out_specs=out_specs, check_vma=False
        )(saved, *others)

    return run
```

```python
from functools import partial

import jax
import jax.numpy as jnp
from jax import lax
from jax.experimental import pallas as pl
from jax.experimental.pallas import tpu as pltpu
from jax.sharding import PartitionSpec as P

EPS = 1e-05
VMEM_BYTES = 24 * 1024 * 1024
F32 = jnp.float32
BF16 = jnp.bfloat16


MEDIUM = pl.CostEstimate(flops=10**9, bytes_accessed=2**20, transcendentals=0)
LONG = pl.CostEstimate(flops=2 * 10**10, bytes_accessed=2**20, transcendentals=0)


def nn(a, b):
    return lax.dot_general(a, b, (((1,), (0,)), ((), ())), preferred_element_type=F32)


def nt(a, b):
    return lax.dot_general(a, b, (((1,), (1,)), ((), ())), preferred_element_type=F32)


def tn(a, b):
    return lax.dot_general(a, b, (((0,), (0,)), ((), ())), preferred_element_type=F32)


def as_row(column):
    count = column.shape[0]
    return jnp.transpose(jnp.broadcast_to(column, (count, count)))[0:1, :]


def silu_slope(pre):
    sig = jax.nn.sigmoid(pre)
    return sig, sig * (1.0 + pre * (1.0 - sig))


PIECES = 4


def pieces(source, target, sems, first):
    step = target.shape[-1] // PIECES
    copies = []
    for i in range(PIECES):
        cols = pl.ds(i * step, step)
        copies.append(
            pltpu.make_async_copy(source.at[:, cols], target.at[:, cols], sems.at[first + i])
        )
    return copies


def project(x_ref, gain_ref, w_ref, xg_ref, step, copies=()):
    tokens, width = x_ref.shape
    squares = jnp.zeros((tokens, 128), F32)
    pre = jnp.zeros((w_ref.shape[0], tokens), F32)
    for c in range(0, width, step):
        if copies and c % (width // len(copies)) == 0:
            copies[c * len(copies) // width].wait()
        x = x_ref[:, c : c + step].astype(F32)
        for k in range(0, step, 128):
            part = x[:, k : k + 128]
            squares += part * part
        xg = (x * gain_ref[:, c : c + step]).astype(BF16)
        xg_ref[:, c : c + step] = xg
        pre += nt(w_ref[:, c : c + step], xg)
    mean = jnp.sum(squares, axis=1, keepdims=True) * (1.0 / width)
    scale = lax.rsqrt(mean + EPS)
    return scale, pre


def fill(index, matrix, wide_ref, keep_ref, send_ref):
    share = keep_ref.shape[2]
    core = index % 2
    for i in range(wide_ref.shape[1] // share // 2):
        for to_ref, number in ((keep_ref, core), (send_ref, 1 - core)):
            cols = pl.ds(pl.multiple_of((2 * i + number) * share, share), share)
            to_ref[i] = nn(matrix, wide_ref[:, cols]).astype(BF16)


def front_kernel(
    step, place_ref, saved, top, gains, w_in, w_out,
    act0_ref, low_ref, xg0_ref, x1, g, gain1, wi1, wo1,
    x0, gain0, wi0, sems,
):
    lower = place_ref[0]
    upper = 1 - lower
    copies = [
        (gains.at[0, pl.ds(lower, 1)], gain0),
        (w_in.at[0, lower], wi0),
        (gains.at[0, pl.ds(upper, 1)], gain1),
        (w_in.at[0, upper], wi1),
        (w_out.at[0, upper], wo1),
    ]
    copies = [pltpu.make_async_copy(a, b, sems.at[i]) for i, (a, b) in enumerate(copies)]
    first = len(copies)
    copies_x0 = pieces(saved.at[0, lower], x0, sems, first)
    others = pieces(saved.at[0, upper], x1, sems, first + PIECES)
    others += pieces(top.at[upper], g, sems, first + 2 * PIECES)
    for copy in copies[0:2] + copies_x0 + copies[2:5] + others:
        copy.start()
    for copy in copies[0:2]:
        copy.wait()
    scale, raw = project(x0, gain0, wi0, xg0_ref, step, copies_x0)
    row = as_row(scale)
    pre = raw * row
    sig, slope = silu_slope(pre)
    act0_ref[...] = (pre * sig).astype(BF16)
    low_ref[0] = slope
    low_ref[1] = jnp.broadcast_to(row, raw.shape)
    for copy in copies[2:5] + others:
        copy.wait()


def upper_kernel(step, x, g, gain, wi, wo, xg_ref, act_ref, das_ref, da_ref, columns_ref):
    width = x.shape[1]
    scale, raw = project(x, gain, wi, xg_ref, step)
    delta = jnp.zeros(raw.shape, F32)
    for c in range(0, width, step):
        delta += nt(wo[:, c : c + step], g[:, c : c + step])
    row = as_row(scale)
    pre = raw * row
    sig, slope = silu_slope(pre)
    da = (delta * slope).astype(BF16)
    daf = da.astype(F32)
    inner = jnp.sum(daf * pre, axis=0, keepdims=True) * (1.0 / width)
    act_ref[...] = (pre * sig).astype(BF16)
    das_ref[...] = (daf * row).astype(BF16)
    da_ref[...] = da
    square = columns_ref.shape[1:]
    columns_ref[0] = jnp.broadcast_to(scale, square)
    columns_ref[1] = jnp.transpose(jnp.broadcast_to(inner * row * row, square))


def outgoing_kernel(step, x, g, gain, wi, da_ref, columns_ref, flow_ref):
    da = da_ref[...]
    scale = columns_ref[0][:, 0:1]
    pull = columns_ref[1][:, 0:1]
    for c in range(0, x.shape[1], step):
        cols = slice(c, c + step)
        dn = tn(da, wi[:, cols]) * gain[:, cols]
        flow = g[:, cols].astype(F32) + scale * dn - pull * x[:, cols].astype(F32)
        flow_ref[:, cols] = flow.astype(BF16)


def terms1_kernel(index_ref, g, xg_ref, act_ref, das_ref, _, keep_out, send_out, keep_in, send_in):
    fill(index_ref[0], act_ref[...], g, keep_out, send_out)
    fill(index_ref[0], das_ref[...], xg_ref, keep_in, send_in)


def terms_kernel(
    index_ref, flow_ref, act0_ref, keep_out1, send_out1, keep_in1, send_in1, keep_ref, send_ref
):
    fill(index_ref[0], act0_ref[...], flow_ref, keep_ref, send_ref)
    chips = keep_in1.shape[0]
    keep_ref[chips : 2 * chips] = keep_out1[...]
    send_ref[chips : 2 * chips] = send_out1[...]
    keep_ref[2 * chips : 3 * chips] = keep_in1[...]
    send_ref[2 * chips : 3 * chips] = send_in1[...]


def pick_kernel(place_ref, index_ref, w_out, out_ref, sems):
    half = out_ref.shape[1]
    cols = pl.ds(pl.multiple_of((index_ref[0] % 2) * half, half), half)
    copies = pieces(w_out.at[0, place_ref[0], :, cols], out_ref, sems, 0)
    for copy in copies:
        copy.start()
    for copy in copies:
        copy.wait()


def product(step, number, w_ref, flow_ref):
    half = w_ref.shape[1]
    delta = jnp.zeros((w_ref.shape[0], flow_ref.shape[0]), F32)
    for c in range(0, half, step):
        cols = pl.ds(pl.multiple_of(number * half + c, step), step)
        delta += nt(w_ref[:, c : c + step], flow_ref[:, cols])
    return delta


def flow_kernel(step, index_ref, flow_ref, own_ref, part_ref):
    part_ref[...] = product(step, index_ref[0] % 2, own_ref, flow_ref)


def flow_rest_kernel(step, index_ref, flow_ref, other_ref, part_ref, send_ref):
    rest = product(step, 1 - index_ref[0] % 2, other_ref, flow_ref)
    send_ref[...] = (part_ref[...] + rest).astype(BF16)


def lower_kernel(index_ref, xg0_ref, low_ref, got_ref, keep_ref, send_ref):
    da = (got_ref[...].astype(F32) * low_ref[0]).astype(BF16)
    das = (da.astype(F32) * low_ref[1]).astype(BF16)
    fill(index_ref[0], das, xg0_ref, keep_ref, send_ref)


def chip_kernel(place_ref, index_ref, keep, got, _, sum_ref, across):
    for i in range(keep.shape[0]):
        sum_ref[i] = (keep[i].astype(F32) + got[i].astype(F32)).astype(BF16)
    row = (index_ref[0] // 2) % 2
    first = (1 - place_ref[0]) * (2 * across.shape[0]) + 1 - row
    for i in range(across.shape[0]):
        across[i] = sum_ref[first + 2 * i]


def x_first(section, index):
    return (index % 2 == 0) | (section == (index // 2) % 2)


def plane_kernel(
    place_ref, index_ref, sums, keep0, got0, own_ref, first_ref, second_ref, across
):
    rank = keep0.shape[1]
    chips = keep0.shape[0]
    row = (index_ref[0] // 2) % 2

    def terms_in(section, block):
        if section == 0:
            return (keep0[block].astype(F32) + got0[block].astype(F32)).astype(BF16)
        return sums[2 * chips + block]

    def order(near, along_x, along_y):
        far = 1 - near
        for i in range(own_ref.shape[0]):
            across[i] = terms_in(far, 2 * i + 1 - row)
            for to_ref, section, number in (
                (along_x, far, row),
                (along_y, near, 1 - row),
                (own_ref, near, row),
            ):
                block = 2 * i + number
                to_ref[i, 0:rank] = terms_in(section, block)
                to_ref[i, rank : 2 * rank] = sums[section * chips + block]

    along_x = x_first(place_ref[0], index_ref[0])
    for place in range(2):
        for x_is_first, ways in ((True, (first_ref, second_ref)), (False, (second_ref, first_ref))):
            pl.when((place_ref[0] == place) & (along_x == x_is_first))(
                partial(order, place, *ways)
            )


def add_kernel(own, across_out, out_ref):
    rank = across_out.shape[1]
    out_ref[:, 0:rank] = own[:, 0:rank]
    for i in range(own.shape[0]):
        total = own[i, rank : 2 * rank].astype(F32) + across_out[i].astype(F32)
        out_ref[i, rank : 2 * rank] = total.astype(BF16)


def layer_routes(layers):
    if layers == 4:
        return [[None, None, None, 0], [1, 0, 3, 2], [2, 3, 0, 1], [3, 2, 1, None]]
    return [[i ^ k for i in range(layers)] for k in range(1, layers)]


def layer_kernel(routes, index_ref, own, first, across_in, second, *out_refs):
    rank = across_in.shape[1]
    layer = index_ref[0] // 4
    for route, out_ref in zip([range(own.shape[0]), *routes], out_refs):
        block = sum(jnp.where(layer == i, target or 0, 0) for i, target in enumerate(route))
        total = sum(ref[block].astype(F32) for ref in (own, first, second))
        out_ref[0:rank] = (total[0:rank] + across_in[block].astype(F32)).astype(BF16)
        out_ref[rank : 2 * rank] = total[rank : 2 * rank].astype(BF16)


def total_kernel(*refs):
    *got, in_far, out_far, in_ref, out_ref, sems = refs
    rank = in_ref.shape[1]
    copies = []
    for i, (ref, far) in enumerate(((in_ref, in_far), (out_ref, out_far))):
        ref[0] = sum(part[i * rank : (i + 1) * rank].astype(F32) for part in got)
        copies.append(pltpu.make_async_copy(ref, far, sems.at[i]))
        copies[i].start()
    for copy in copies:
        copy.wait()


def local(kernel, name, out_shapes, *operands, scratch=(), cost=None, out="near"):
    spaces = {"scalar": pltpu.SMEM, "far": pltpu.HBM, "near": pltpu.VMEM}
    out = pl.pallas_call(
        kernel,
        in_specs=[pl.BlockSpec(memory_space=spaces[kind]) for kind, _ in operands],
        out_specs=[pl.BlockSpec(memory_space=spaces[out])] * len(out_shapes),
        out_shape=[jax.ShapeDtypeStruct(shape, dtype) for shape, dtype in out_shapes],
        scratch_shapes=list(scratch),
        compiler_params=pltpu.CompilerParams(vmem_limit_bytes=VMEM_BYTES),
        cost_estimate=cost,
        name=name,
    )(*[array for _, array in operands])
    return out if len(out) > 1 else out[0]


def near(*arrays):
    return [("near", array) for array in arrays]


def pair_on_device(saved, top_grad, gains, adapter_in, adapter_out):
    count = lax.axis_size("dp")
    tokens, width = saved.shape[2:]
    rank = adapter_in.shape[3]
    share = width // count
    chips, layers = count // 2, count // 4
    place = ("scalar", lax.axis_index("section").astype(jnp.int32)[None])
    index = ("scalar", lax.axis_index("dp").astype(jnp.int32)[None])
    saved, top, gains, w_in, w_out = [
        ("far", pltpu.with_memory_space_constraint(a, pltpu.HBM))
        for a in (saved, top_grad, gains, jnp.swapaxes(adapter_in, 2, 3), adapter_out)
    ]

    def swapped(array, way):
        pairs = []
        for s in range(2):
            for d in range(count):
                over_section, bits = way(s, d) if callable(way) else way
                pairs.append((s * count + d, (s ^ over_section) * count + (d ^ bits)))
        return lax.ppermute(array, ("section", "dp"), pairs)

    def first_way(s, d):
        return (1, 0) if x_first(s, d) else (0, 2)

    def second_way(s, d):
        return (0, 2) if x_first(s, d) else (1, 0)

    sems = pltpu.SemaphoreType.DMA
    wide = ((tokens, width), BF16)
    thin = ((rank, width), BF16)
    gain = ((1, width), F32)
    small = ((rank, tokens), BF16)
    one = ((chips, rank, share), BF16)
    three = ((3 * chips, rank, share), BF16)
    quarter = ((layers, rank, share), BF16)
    double = ((layers, 2 * rank, share), BF16)
    along_x, other_core = (1, 0), (0, 1)

    mine = local(
        pick_kernel, "pick", [((rank, width // 2), BF16)], place, index, w_out, scratch=[sems((PIECES,))]
    )
    own_half = swapped(mine, along_x)
    act0, low, xg0, x1, g, gain1, wi1, wo1 = local(
        partial(front_kernel, share), "front",
        [small, ((2, rank, tokens), F32), wide, wide, wide, gain, thin, thin],
        place, saved, top, gains, w_in, w_out,
        scratch=[pltpu.VMEM(*wide), pltpu.VMEM(*gain), pltpu.VMEM(*thin), sems((5 + 3 * PIECES,))],
    )
    got_act0 = swapped(act0, along_x)
    xg1, act1, das1, da1, columns = local(
        partial(upper_kernel, share), "upper",
        [wide, small, small, small, ((2, tokens, tokens), F32)],
        *near(x1, g, gain1, wi1, wo1),
    )
    own_half, da1 = lax.optimization_barrier((own_half, da1))
    other_half = swapped(own_half, other_core)
    flow = local(
        partial(outgoing_kernel, share), "outgoing", [wide], *near(x1, g, gain1, wi1, da1, columns),
        cost=LONG,
    )
    part = local(
        partial(flow_kernel, share), "flow", [((rank, tokens), F32)], index, *near(flow, own_half)
    )
    delta = local(
        partial(flow_rest_kernel, share), "flow_rest", [small],
        index, *near(flow, other_half, part),
    )
    got_delta = swapped(delta, along_x)
    terms1 = local(
        terms1_kernel, "terms1", [one] * 4, index, *near(g, xg1, act1, das1, delta)
    )
    keep, send = local(
        terms_kernel, "terms", [three, three], index, *near(flow, got_act0, *terms1)
    )
    got = swapped(send, other_core)
    keep0, send0 = local(
        lower_kernel, "lower", [one, one], index, *near(xg0, low, got_delta), cost=LONG
    )
    got0 = swapped(send0, other_core)
    sums, across_out = local(
        chip_kernel, "chip", [three, quarter], place, index, *near(keep, got, keep0)
    )
    across_out = swapped(across_out, (1, 2))
    own, first, second, across_in = local(
        plane_kernel, "plane", [double, double, double, quarter],
        place, index, *near(sums, keep0, got0),
    )
    first = swapped(first, first_way)
    across_in = swapped(across_in, (1, 2))
    second = swapped(second, second_way)
    own = local(add_kernel, "add", [double], *near(own, across_out), cost=MEDIUM)
    routes = layer_routes(layers)
    mine, *others = local(
        partial(layer_kernel, routes), "layer", [((2 * rank, share), BF16)] * (1 + len(routes)),
        index, *near(own, first, across_in, second),
    )
    others = [
        lax.ppermute(
            other,
            ("section", "dp"),
            [
                (s * count + d, s * count + 4 * route[d // 4] + d % 4)
                for s in range(2)
                for d in range(count)
                if route[d // 4] is not None
            ],
        )
        for route, other in zip(routes, others)
    ]
    block = ((1, rank, share), F32)
    total_in, total_out = local(
        total_kernel, "total", [block, block], *near(mine, *others),
        scratch=[pltpu.VMEM(*block), pltpu.VMEM(*block), sems((2,))], out="far",
    )
    return (jnp.swapaxes(total_in, 1, 2), total_out)


def section_back(x, gain, weight_in, weight_out, upstream):
    xf = x.astype(F32)
    scale = lax.rsqrt(jnp.mean(xf * xf, axis=-1, keepdims=True) + EPS)
    normed = xf * scale
    hidden = (normed * gain).astype(BF16)
    pre = jnp.dot(hidden, weight_in, preferred_element_type=F32)
    sig, slope = silu_slope(pre)
    active = (pre * sig).astype(BF16)
    delta_act = jnp.dot(upstream, weight_out.T, preferred_element_type=F32)
    delta_pre = (delta_act * slope).astype(BF16)
    delta_norm = jnp.dot(delta_pre, weight_in.T, preferred_element_type=F32) * gain
    inner = jnp.mean(delta_norm * normed, axis=-1, keepdims=True)
    result = (upstream.astype(F32) + scale * (delta_norm - normed * inner)).astype(BF16)
    term_in = jnp.dot(hidden.T, delta_pre, preferred_element_type=F32)
    term_out = jnp.dot(active.T, upstream, preferred_element_type=F32)
    return (result, term_in, term_out)


def relay_on_device(saved, top_grad, gains, adapter_in, adapter_out):
    sections = lax.axis_size("section")
    place = lax.axis_index("section")
    width = top_grad.shape[2]
    rank = adapter_in.shape[3]
    zero_in = jnp.zeros((width, rank), F32)
    zero_out = jnp.zeros((rank, width), F32)

    def step(turn, flows, sums):
        leaving, added = [], []
        for replica in (0, 1):
            serves = place == (sections - 1 - turn if replica == 0 else turn)
            result, term_in, term_out = lax.cond(
                serves,
                partial(
                    section_back,
                    saved[0, replica],
                    gains[0, replica],
                    adapter_in[0, replica],
                    adapter_out[0, replica],
                ),
                lambda flow: (flow, zero_in, zero_out),
                flows[replica],
            )
            leaving.append(result)
            added += [sums[2 * replica] + term_in, sums[2 * replica + 1] + term_out]
        return leaving, added

    down = [(i, i - 1) for i in range(1, sections)]
    up = [(i, i + 1) for i in range(sections - 1)]

    def turn_and_pass(turn, carry):
        leaving, sums = step(turn, carry[0], carry[1])
        return (
            [lax.ppermute(leaving[0], "section", down), lax.ppermute(leaving[1], "section", up)],
            sums,
        )

    start = ([top_grad[0], top_grad[1]], [zero_in, zero_out, zero_in, zero_out])
    flows, sums = lax.fori_loop(0, sections - 1, turn_and_pass, start)
    _, sums = step(sections - 1, flows, sums)
    shares = [
        lax.psum_scatter(term, "dp", scatter_dimension=i % 2, tiled=True)
        for i, term in enumerate(sums)
    ]
    mirror = [(i, sections - 1 - i) for i in range(sections)]
    total_in = shares[0] + lax.ppermute(shares[2], "section", mirror)
    total_out = shares[1] + lax.ppermute(shares[3], "section", mirror)
    return (total_in[None], total_out[None])


def solution(mesh):
    in_specs = (
        P("section", None, "dp", None),
        P(None, "dp", None),
        P("section", None, None),
        P("section", None, None, None),
        P("section", None, None, None),
    )
    out_specs = (P("section", "dp", None), P("section", None, "dp"))

    def run(saved, *others):
        share = saved.shape[3] // mesh.shape["dp"]
        count = mesh.shape["dp"]
        pair = mesh.shape["section"] == 2 and share % 128 == 0
        pair = pair and count >= 4 and count & (count - 1) == 0
        on_device = pair_on_device if pair else relay_on_device
        return jax.shard_map(
            on_device, mesh=mesh, in_specs=in_specs, out_specs=out_specs, check_vma=False
        )(saved, *others)

    return run
```

```python
from functools import partial

import jax
import jax.numpy as jnp
from jax import lax
from jax.experimental import pallas as pl
from jax.experimental.pallas import tpu as pltpu
from jax.sharding import PartitionSpec as P

EPS = 1e-05
VMEM_BYTES = 24 * 1024 * 1024
F32 = jnp.float32
BF16 = jnp.bfloat16


MEDIUM = pl.CostEstimate(flops=10**9, bytes_accessed=2**20, transcendentals=0)
LONG = pl.CostEstimate(flops=2 * 10**10, bytes_accessed=2**20, transcendentals=0)


def nn(a, b):
    return lax.dot_general(a, b, (((1,), (0,)), ((), ())), preferred_element_type=F32)


def nt(a, b):
    return lax.dot_general(a, b, (((1,), (1,)), ((), ())), preferred_element_type=F32)


def tn(a, b):
    return lax.dot_general(a, b, (((0,), (0,)), ((), ())), preferred_element_type=F32)


def as_row(column):
    count = column.shape[0]
    return jnp.transpose(jnp.broadcast_to(column, (count, count)))[0:1, :]


def silu_slope(pre):
    sig = jax.nn.sigmoid(pre)
    return sig, sig * (1.0 + pre * (1.0 - sig))


PIECES = 4


def pieces(source, target, sems, first):
    step = target.shape[-1] // PIECES
    copies = []
    for i in range(PIECES):
        cols = pl.ds(i * step, step)
        copies.append(
            pltpu.make_async_copy(source.at[:, cols], target.at[:, cols], sems.at[first + i])
        )
    return copies


def project(x_ref, gain_ref, w_ref, xg_ref, step, copies=()):
    tokens, width = x_ref.shape
    squares = jnp.zeros((tokens, 128), F32)
    pre = jnp.zeros((w_ref.shape[0], tokens), F32)
    for c in range(0, width, step):
        if copies and c % (width // len(copies)) == 0:
            copies[c * len(copies) // width].wait()
        x = x_ref[:, c : c + step].astype(F32)
        for k in range(0, step, 128):
            part = x[:, k : k + 128]
            squares += part * part
        xg = (x * gain_ref[:, c : c + step]).astype(BF16)
        xg_ref[:, c : c + step] = xg
        pre += nt(w_ref[:, c : c + step], xg)
    mean = jnp.sum(squares, axis=1, keepdims=True) * (1.0 / width)
    scale = lax.rsqrt(mean + EPS)
    return scale, pre


def fill(index, matrix, wide_ref, keep_ref, send_ref):
    share = keep_ref.shape[2]
    core = index % 2
    for i in range(wide_ref.shape[1] // share // 2):
        for to_ref, number in ((keep_ref, core), (send_ref, 1 - core)):
            cols = pl.ds(pl.multiple_of((2 * i + number) * share, share), share)
            to_ref[i] = nn(matrix, wide_ref[:, cols]).astype(BF16)


def front_kernel(
    step, place_ref, saved, top, gains, w_in, w_out,
    act0_ref, low_ref, xg0_ref, x1, g, gain1, wi1, wo1,
    x0, gain0, wi0, sems,
):
    lower = place_ref[0]
    upper = 1 - lower
    copies = [
        (gains.at[0, pl.ds(lower, 1)], gain0),
        (w_in.at[0, lower], wi0),
        (gains.at[0, pl.ds(upper, 1)], gain1),
        (w_in.at[0, upper], wi1),
        (w_out.at[0, upper], wo1),
    ]
    copies = [pltpu.make_async_copy(a, b, sems.at[i]) for i, (a, b) in enumerate(copies)]
    first = len(copies)
    copies_x0 = pieces(saved.at[0, lower], x0, sems, first)
    others = pieces(saved.at[0, upper], x1, sems, first + PIECES)
    others += pieces(top.at[upper], g, sems, first + 2 * PIECES)
    for copy in copies[0:2] + copies_x0 + copies[2:5] + others:
        copy.start()
    for copy in copies[0:2]:
        copy.wait()
    scale, raw = project(x0, gain0, wi0, xg0_ref, step, copies_x0)
    row = as_row(scale)
    pre = raw * row
    sig, slope = silu_slope(pre)
    act0_ref[...] = (pre * sig).astype(BF16)
    low_ref[0] = slope
    low_ref[1] = jnp.broadcast_to(row, raw.shape)
    for copy in copies[2:5] + others:
        copy.wait()


def upper_kernel(step, x, g, gain, wi, wo, xg_ref, act_ref, das_ref, da_ref, columns_ref):
    width = x.shape[1]
    scale, raw = project(x, gain, wi, xg_ref, step)
    delta = jnp.zeros(raw.shape, F32)
    for c in range(0, width, step):
        delta += nt(wo[:, c : c + step], g[:, c : c + step])
    row = as_row(scale)
    pre = raw * row
    sig, slope = silu_slope(pre)
    da = (delta * slope).astype(BF16)
    daf = da.astype(F32)
    inner = jnp.sum(daf * pre, axis=0, keepdims=True) * (1.0 / width)
    act_ref[...] = (pre * sig).astype(BF16)
    das_ref[...] = (daf * row).astype(BF16)
    da_ref[...] = da
    square = columns_ref.shape[1:]
    columns_ref[0] = jnp.broadcast_to(scale, square)
    columns_ref[1] = jnp.transpose(jnp.broadcast_to(inner * row * row, square))


def outgoing_kernel(step, x, g, gain, wi, da_ref, columns_ref, flow_ref):
    da = da_ref[...]
    scale = columns_ref[0][:, 0:1]
    pull = columns_ref[1][:, 0:1]
    for c in range(0, x.shape[1], step):
        cols = slice(c, c + step)
        dn = tn(da, wi[:, cols]) * gain[:, cols]
        flow = g[:, cols].astype(F32) + scale * dn - pull * x[:, cols].astype(F32)
        flow_ref[:, cols] = flow.astype(BF16)


def terms1_kernel(index_ref, g, xg_ref, act_ref, das_ref, _, keep_out, send_out, keep_in, send_in):
    fill(index_ref[0], act_ref[...], g, keep_out, send_out)
    fill(index_ref[0], das_ref[...], xg_ref, keep_in, send_in)


def terms_kernel(
    index_ref, flow_ref, act0_ref, keep_out1, send_out1, keep_in1, send_in1, keep_ref, send_ref
):
    fill(index_ref[0], act0_ref[...], flow_ref, keep_ref, send_ref)
    chips = keep_in1.shape[0]
    keep_ref[chips : 2 * chips] = keep_out1[...]
    send_ref[chips : 2 * chips] = send_out1[...]
    keep_ref[2 * chips : 3 * chips] = keep_in1[...]
    send_ref[2 * chips : 3 * chips] = send_in1[...]


def pick_kernel(place_ref, index_ref, w_out, out_ref, sems):
    half = out_ref.shape[1]
    cols = pl.ds(pl.multiple_of((index_ref[0] % 2) * half, half), half)
    copies = pieces(w_out.at[0, place_ref[0], :, cols], out_ref, sems, 0)
    for copy in copies:
        copy.start()
    for copy in copies:
        copy.wait()


def product(step, number, w_ref, flow_ref):
    half = w_ref.shape[1]
    delta = jnp.zeros((w_ref.shape[0], flow_ref.shape[0]), F32)
    for c in range(0, half, step):
        cols = pl.ds(pl.multiple_of(number * half + c, step), step)
        delta += nt(w_ref[:, c : c + step], flow_ref[:, cols])
    return delta


def flow_kernel(step, index_ref, flow_ref, own_ref, part_ref):
    part_ref[...] = product(step, index_ref[0] % 2, own_ref, flow_ref)


def flow_rest_kernel(step, index_ref, flow_ref, other_ref, part_ref, send_ref):
    rest = product(step, 1 - index_ref[0] % 2, other_ref, flow_ref)
    send_ref[...] = (part_ref[...] + rest).astype(BF16)


def lower_kernel(index_ref, xg0_ref, low_ref, got_ref, keep_ref, send_ref):
    da = (got_ref[...].astype(F32) * low_ref[0]).astype(BF16)
    das = (da.astype(F32) * low_ref[1]).astype(BF16)
    fill(index_ref[0], das, xg0_ref, keep_ref, send_ref)


def chip_kernel(place_ref, index_ref, keep, got, _, sum_ref, across):
    for i in range(keep.shape[0]):
        sum_ref[i] = (keep[i].astype(F32) + got[i].astype(F32)).astype(BF16)
    row = (index_ref[0] // 2) % 2
    first = (1 - place_ref[0]) * (2 * across.shape[0]) + 1 - row
    for i in range(across.shape[0]):
        across[i] = sum_ref[first + 2 * i]


def x_first(section, index):
    return section == (index // 2) % 2


def plane_kernel(
    place_ref, index_ref, sums, keep0, got0, own_ref, first_ref, second_ref, across
):
    rank = keep0.shape[1]
    chips = keep0.shape[0]
    row = (index_ref[0] // 2) % 2

    def terms_in(section, block):
        if section == 0:
            return (keep0[block].astype(F32) + got0[block].astype(F32)).astype(BF16)
        return sums[2 * chips + block]

    def order(near, along_x, along_y):
        far = 1 - near
        for i in range(own_ref.shape[0]):
            across[i] = terms_in(far, 2 * i + 1 - row)
            for to_ref, section, number in (
                (along_x, far, row),
                (along_y, near, 1 - row),
                (own_ref, near, row),
            ):
                block = 2 * i + number
                to_ref[i, 0:rank] = terms_in(section, block)
                to_ref[i, rank : 2 * rank] = sums[section * chips + block]

    along_x = x_first(place_ref[0], index_ref[0])
    for place in range(2):
        for x_is_first, ways in ((True, (first_ref, second_ref)), (False, (second_ref, first_ref))):
            pl.when((place_ref[0] == place) & (along_x == x_is_first))(
                partial(order, place, *ways)
            )


def add_kernel(own, across_out, out_ref):
    rank = across_out.shape[1]
    out_ref[:, 0:rank] = own[:, 0:rank]
    for i in range(own.shape[0]):
        total = own[i, rank : 2 * rank].astype(F32) + across_out[i].astype(F32)
        out_ref[i, rank : 2 * rank] = total.astype(BF16)


def layer_routes(layers):
    if layers == 4:
        even = [[2, 3, 1, 0], [3, 2, 0, 1], [1, 0, 3, 2]]
        odd = [[1, 3, 0, 2], [3, 2, 1, 0], [2, 0, 3, 1]]
    else:
        even = odd = [[i ^ k for i in range(layers)] for k in range(1, layers)]
    return list(zip(even, odd))


def layer_kernel(routes, index_ref, own, first, across_in, second, *out_refs):
    rank = across_in.shape[1]
    layer = index_ref[0] // 4
    core = index_ref[0] % 2
    own_way = range(len(out_refs))
    for ways, out_ref in zip([(own_way, own_way), *routes], out_refs):
        block = sum(
            jnp.where((layer == i) & (core == k), target, 0)
            for k, route in enumerate(ways)
            for i, target in enumerate(route)
        )
        total = sum(ref[block].astype(F32) for ref in (own, first, second))
        out_ref[0:rank] = (total[0:rank] + across_in[block].astype(F32)).astype(BF16)
        out_ref[rank : 2 * rank] = total[rank : 2 * rank].astype(BF16)


def total_kernel(*refs):
    *got, in_far, out_far, in_ref, out_ref, sems = refs
    rank = in_ref.shape[1]
    copies = []
    for i, (ref, far) in enumerate(((in_ref, in_far), (out_ref, out_far))):
        ref[0] = sum(part[i * rank : (i + 1) * rank].astype(F32) for part in got)
        copies.append(pltpu.make_async_copy(ref, far, sems.at[i]))
        copies[i].start()
    for copy in copies:
        copy.wait()


def local(kernel, name, out_shapes, *operands, scratch=(), cost=None, out="near"):
    spaces = {"scalar": pltpu.SMEM, "far": pltpu.HBM, "near": pltpu.VMEM}
    out = pl.pallas_call(
        kernel,
        in_specs=[pl.BlockSpec(memory_space=spaces[kind]) for kind, _ in operands],
        out_specs=[pl.BlockSpec(memory_space=spaces[out])] * len(out_shapes),
        out_shape=[jax.ShapeDtypeStruct(shape, dtype) for shape, dtype in out_shapes],
        scratch_shapes=list(scratch),
        compiler_params=pltpu.CompilerParams(vmem_limit_bytes=VMEM_BYTES),
        cost_estimate=cost,
        name=name,
    )(*[array for _, array in operands])
    return out if len(out) > 1 else out[0]


def near(*arrays):
    return [("near", array) for array in arrays]


def pair_on_device(saved, top_grad, gains, adapter_in, adapter_out):
    count = lax.axis_size("dp")
    tokens, width = saved.shape[2:]
    rank = adapter_in.shape[3]
    share = width // count
    chips, layers = count // 2, count // 4
    place = ("scalar", lax.axis_index("section").astype(jnp.int32)[None])
    index = ("scalar", lax.axis_index("dp").astype(jnp.int32)[None])
    saved, top, gains, w_in, w_out = [
        ("far", pltpu.with_memory_space_constraint(a, pltpu.HBM))
        for a in (saved, top_grad, gains, jnp.swapaxes(adapter_in, 2, 3), adapter_out)
    ]

    def swapped(array, way):
        pairs = []
        for s in range(2):
            for d in range(count):
                over_section, bits = way(s, d) if callable(way) else way
                pairs.append((s * count + d, (s ^ over_section) * count + (d ^ bits)))
        return lax.ppermute(array, ("section", "dp"), pairs)

    def first_way(s, d):
        return (1, 0) if x_first(s, d) else (0, 2)

    def second_way(s, d):
        return (0, 2) if x_first(s, d) else (1, 0)

    sems = pltpu.SemaphoreType.DMA
    wide = ((tokens, width), BF16)
    thin = ((rank, width), BF16)
    gain = ((1, width), F32)
    small = ((rank, tokens), BF16)
    one = ((chips, rank, share), BF16)
    three = ((3 * chips, rank, share), BF16)
    quarter = ((layers, rank, share), BF16)
    double = ((layers, 2 * rank, share), BF16)
    along_x, other_core = (1, 0), (0, 1)

    mine = local(
        pick_kernel, "pick", [((rank, width // 2), BF16)], place, index, w_out, scratch=[sems((PIECES,))]
    )
    own_half = swapped(mine, along_x)
    act0, low, xg0, x1, g, gain1, wi1, wo1 = local(
        partial(front_kernel, share), "front",
        [small, ((2, rank, tokens), F32), wide, wide, wide, gain, thin, thin],
        place, saved, top, gains, w_in, w_out,
        scratch=[pltpu.VMEM(*wide), pltpu.VMEM(*gain), pltpu.VMEM(*thin), sems((5 + 3 * PIECES,))],
    )
    got_act0 = swapped(act0, along_x)
    xg1, act1, das1, da1, columns = local(
        partial(upper_kernel, share), "upper",
        [wide, small, small, small, ((2, tokens, tokens), F32)],
        *near(x1, g, gain1, wi1, wo1),
    )
    own_half, da1 = lax.optimization_barrier((own_half, da1))
    other_half = swapped(own_half, other_core)
    flow = local(
        partial(outgoing_kernel, share), "outgoing", [wide], *near(x1, g, gain1, wi1, da1, columns),
        cost=LONG,
    )
    part = local(
        partial(flow_kernel, share), "flow", [((rank, tokens), F32)], index, *near(flow, own_half)
    )
    delta = local(
        partial(flow_rest_kernel, share), "flow_rest", [small],
        index, *near(flow, other_half, part),
    )
    got_delta = swapped(delta, along_x)
    terms1 = local(
        terms1_kernel, "terms1", [one] * 4, index, *near(g, xg1, act1, das1, delta)
    )
    keep, send = local(
        terms_kernel, "terms", [three, three], index, *near(flow, got_act0, *terms1)
    )
    got = swapped(send, other_core)
    keep0, send0 = local(
        lower_kernel, "lower", [one, one], index, *near(xg0, low, got_delta), cost=LONG
    )
    got0 = swapped(send0, other_core)
    sums, across_out = local(
        chip_kernel, "chip", [three, quarter], place, index, *near(keep, got, keep0)
    )
    across_out = swapped(across_out, (1, 2))
    own, first, second, across_in = local(
        plane_kernel, "plane", [double, double, double, quarter],
        place, index, *near(sums, keep0, got0),
    )
    first = swapped(first, first_way)
    across_in = swapped(across_in, (1, 2))
    second = swapped(second, second_way)
    own = local(add_kernel, "add", [double], *near(own, across_out), cost=MEDIUM)
    routes = layer_routes(layers)
    mine, *others = local(
        partial(layer_kernel, routes), "layer", [((2 * rank, share), BF16)] * layers,
        index, *near(own, first, across_in, second),
    )
    others = [
        lax.ppermute(
            other,
            ("section", "dp"),
            [
                (s * count + d, s * count + 4 * ways[d % 2][d // 4] + d % 4)
                for s in range(2)
                for d in range(count)
            ],
        )
        for ways, other in zip(routes, others)
    ]
    block = ((1, rank, share), F32)
    total_in, total_out = local(
        total_kernel, "total", [block, block], *near(mine, *others),
        scratch=[pltpu.VMEM(*block), pltpu.VMEM(*block), sems((2,))], out="far",
    )
    return (jnp.swapaxes(total_in, 1, 2), total_out)


def section_back(x, gain, weight_in, weight_out, upstream):
    xf = x.astype(F32)
    scale = lax.rsqrt(jnp.mean(xf * xf, axis=-1, keepdims=True) + EPS)
    normed = xf * scale
    hidden = (normed * gain).astype(BF16)
    pre = jnp.dot(hidden, weight_in, preferred_element_type=F32)
    sig, slope = silu_slope(pre)
    active = (pre * sig).astype(BF16)
    delta_act = jnp.dot(upstream, weight_out.T, preferred_element_type=F32)
    delta_pre = (delta_act * slope).astype(BF16)
    delta_norm = jnp.dot(delta_pre, weight_in.T, preferred_element_type=F32) * gain
    inner = jnp.mean(delta_norm * normed, axis=-1, keepdims=True)
    result = (upstream.astype(F32) + scale * (delta_norm - normed * inner)).astype(BF16)
    term_in = jnp.dot(hidden.T, delta_pre, preferred_element_type=F32)
    term_out = jnp.dot(active.T, upstream, preferred_element_type=F32)
    return (result, term_in, term_out)


def relay_on_device(saved, top_grad, gains, adapter_in, adapter_out):
    sections = lax.axis_size("section")
    place = lax.axis_index("section")
    width = top_grad.shape[2]
    rank = adapter_in.shape[3]
    zero_in = jnp.zeros((width, rank), F32)
    zero_out = jnp.zeros((rank, width), F32)

    def step(turn, flows, sums):
        leaving, added = [], []
        for replica in (0, 1):
            serves = place == (sections - 1 - turn if replica == 0 else turn)
            result, term_in, term_out = lax.cond(
                serves,
                partial(
                    section_back,
                    saved[0, replica],
                    gains[0, replica],
                    adapter_in[0, replica],
                    adapter_out[0, replica],
                ),
                lambda flow: (flow, zero_in, zero_out),
                flows[replica],
            )
            leaving.append(result)
            added += [sums[2 * replica] + term_in, sums[2 * replica + 1] + term_out]
        return leaving, added

    down = [(i, i - 1) for i in range(1, sections)]
    up = [(i, i + 1) for i in range(sections - 1)]

    def turn_and_pass(turn, carry):
        leaving, sums = step(turn, carry[0], carry[1])
        return (
            [lax.ppermute(leaving[0], "section", down), lax.ppermute(leaving[1], "section", up)],
            sums,
        )

    start = ([top_grad[0], top_grad[1]], [zero_in, zero_out, zero_in, zero_out])
    flows, sums = lax.fori_loop(0, sections - 1, turn_and_pass, start)
    _, sums = step(sections - 1, flows, sums)
    shares = [
        lax.psum_scatter(term, "dp", scatter_dimension=i % 2, tiled=True)
        for i, term in enumerate(sums)
    ]
    mirror = [(i, sections - 1 - i) for i in range(sections)]
    total_in = shares[0] + lax.ppermute(shares[2], "section", mirror)
    total_out = shares[1] + lax.ppermute(shares[3], "section", mirror)
    return (total_in[None], total_out[None])


def solution(mesh):
    in_specs = (
        P("section", None, "dp", None),
        P(None, "dp", None),
        P("section", None, None),
        P("section", None, None, None),
        P("section", None, None, None),
    )
    out_specs = (P("section", "dp", None), P("section", None, "dp"))

    def run(saved, *others):
        share = saved.shape[3] // mesh.shape["dp"]
        count = mesh.shape["dp"]
        pair = mesh.shape["section"] == 2 and share % 128 == 0
        pair = pair and count >= 4 and count & (count - 1) == 0
        on_device = pair_on_device if pair else relay_on_device
        return jax.shard_map(
            on_device, mesh=mesh, in_specs=in_specs, out_specs=out_specs, check_vma=False
        )(saved, *others)

    return run
```

```python
from functools import partial

import jax
import jax.numpy as jnp
from jax import lax
from jax.experimental import pallas as pl
from jax.experimental.pallas import tpu as pltpu
from jax.sharding import PartitionSpec as P

EPS = 1e-05
VMEM_BYTES = 24 * 1024 * 1024
F32 = jnp.float32
BF16 = jnp.bfloat16


MEDIUM = pl.CostEstimate(flops=10**9, bytes_accessed=2**20, transcendentals=0)
LONG = pl.CostEstimate(flops=2 * 10**10, bytes_accessed=2**20, transcendentals=0)


def nn(a, b):
    return lax.dot_general(a, b, (((1,), (0,)), ((), ())), preferred_element_type=F32)


def nt(a, b):
    return lax.dot_general(a, b, (((1,), (1,)), ((), ())), preferred_element_type=F32)


def tn(a, b):
    return lax.dot_general(a, b, (((0,), (0,)), ((), ())), preferred_element_type=F32)


def as_row(column):
    count = column.shape[0]
    return jnp.transpose(jnp.broadcast_to(column, (count, count)))[0:1, :]


def silu_slope(pre):
    sig = jax.nn.sigmoid(pre)
    return sig, sig * (1.0 + pre * (1.0 - sig))


PIECES = 8


def pieces(source, target, sems, first):
    step = target.shape[-1] // PIECES
    copies = []
    for i in range(PIECES):
        cols = pl.ds(i * step, step)
        copies.append(
            pltpu.make_async_copy(source.at[:, cols], target.at[:, cols], sems.at[first + i])
        )
    return copies


def project(x_ref, gain_ref, w_ref, xg_ref, step, copies=()):
    tokens, width = x_ref.shape
    squares = jnp.zeros((tokens, 128), F32)
    pre = jnp.zeros((w_ref.shape[0], tokens), F32)
    for c in range(0, width, step):
        if copies and c % (width // len(copies)) == 0:
            copies[c * len(copies) // width].wait()
        x = x_ref[:, c : c + step].astype(F32)
        for k in range(0, step, 128):
            part = x[:, k : k + 128]
            squares += part * part
        xg = (x * gain_ref[:, c : c + step]).astype(BF16)
        xg_ref[:, c : c + step] = xg
        pre += nt(w_ref[:, c : c + step], xg)
    mean = jnp.sum(squares, axis=1, keepdims=True) * (1.0 / width)
    scale = lax.rsqrt(mean + EPS)
    return scale, pre


def fill(index, matrix, wide_ref, keep_ref, send_ref):
    share = keep_ref.shape[2]
    core = index % 2
    for i in range(wide_ref.shape[1] // share // 2):
        for to_ref, number in ((keep_ref, core), (send_ref, 1 - core)):
            cols = pl.ds(pl.multiple_of((2 * i + number) * share, share), share)
            to_ref[i] = nn(matrix, wide_ref[:, cols]).astype(BF16)


def front_kernel(
    step, place_ref, saved, top, gains, w_in, w_out,
    act0_ref, low_ref, xg0_ref, x1, g, gain1, wi1, wo1,
    x0, gain0, wi0, sems,
):
    lower = place_ref[0]
    upper = 1 - lower
    copies = [
        (gains.at[0, pl.ds(lower, 1)], gain0),
        (w_in.at[0, lower], wi0),
        (gains.at[0, pl.ds(upper, 1)], gain1),
        (w_in.at[0, upper], wi1),
        (w_out.at[0, upper], wo1),
    ]
    copies = [pltpu.make_async_copy(a, b, sems.at[i]) for i, (a, b) in enumerate(copies)]
    first = len(copies)
    copies_x0 = pieces(saved.at[0, lower], x0, sems, first)
    others = pieces(saved.at[0, upper], x1, sems, first + PIECES)
    others += pieces(top.at[upper], g, sems, first + 2 * PIECES)
    for copy in copies[0:2] + copies_x0 + copies[2:5] + others:
        copy.start()
    for copy in copies[0:2]:
        copy.wait()
    scale, raw = project(x0, gain0, wi0, xg0_ref, step, copies_x0)
    row = as_row(scale)
    pre = raw * row
    sig, slope = silu_slope(pre)
    act0_ref[...] = (pre * sig).astype(BF16)
    low_ref[0] = slope
    low_ref[1] = jnp.broadcast_to(row, raw.shape)
    for copy in copies[2:5] + others:
        copy.wait()


def upper_kernel(step, x, g, gain, wi, wo, xg_ref, act_ref, das_ref, da_ref, columns_ref):
    width = x.shape[1]
    scale, raw = project(x, gain, wi, xg_ref, step)
    delta = jnp.zeros(raw.shape, F32)
    for c in range(0, width, step):
        delta += nt(wo[:, c : c + step], g[:, c : c + step])
    row = as_row(scale)
    pre = raw * row
    sig, slope = silu_slope(pre)
    da = (delta * slope).astype(BF16)
    daf = da.astype(F32)
    inner = jnp.sum(daf * pre, axis=0, keepdims=True) * (1.0 / width)
    act_ref[...] = (pre * sig).astype(BF16)
    das_ref[...] = (daf * row).astype(BF16)
    da_ref[...] = da
    square = columns_ref.shape[1:]
    columns_ref[0] = jnp.broadcast_to(scale, square)
    columns_ref[1] = jnp.transpose(jnp.broadcast_to(inner * row * row, square))


def outgoing_kernel(step, x, g, gain, wi, da_ref, columns_ref, flow_ref):
    da = da_ref[...]
    scale = columns_ref[0][:, 0:1]
    pull = columns_ref[1][:, 0:1]
    for c in range(0, x.shape[1], step):
        cols = slice(c, c + step)
        dn = tn(da, wi[:, cols]) * gain[:, cols]
        flow = g[:, cols].astype(F32) + scale * dn - pull * x[:, cols].astype(F32)
        flow_ref[:, cols] = flow.astype(BF16)


def terms1_kernel(index_ref, g, xg_ref, act_ref, das_ref, _, keep_out, send_out, keep_in, send_in):
    fill(index_ref[0], act_ref[...], g, keep_out, send_out)
    fill(index_ref[0], das_ref[...], xg_ref, keep_in, send_in)


def terms_kernel(
    index_ref, flow_ref, act0_ref, keep_out1, send_out1, keep_in1, send_in1, keep_ref, send_ref
):
    fill(index_ref[0], act0_ref[...], flow_ref, keep_ref, send_ref)
    chips = keep_in1.shape[0]
    keep_ref[chips : 2 * chips] = keep_out1[...]
    send_ref[chips : 2 * chips] = send_out1[...]
    keep_ref[2 * chips : 3 * chips] = keep_in1[...]
    send_ref[2 * chips : 3 * chips] = send_in1[...]


def pick_kernel(place_ref, index_ref, w_out, out_ref, sems):
    half = out_ref.shape[1]
    cols = pl.ds(pl.multiple_of((index_ref[0] % 2) * half, half), half)
    copies = pieces(w_out.at[0, place_ref[0], :, cols], out_ref, sems, 0)
    for copy in copies:
        copy.start()
    for copy in copies:
        copy.wait()


def product(step, number, w_ref, flow_ref):
    half = w_ref.shape[1]
    delta = jnp.zeros((w_ref.shape[0], flow_ref.shape[0]), F32)
    for c in range(0, half, step):
        cols = pl.ds(pl.multiple_of(number * half + c, step), step)
        delta += nt(w_ref[:, c : c + step], flow_ref[:, cols])
    return delta


def flow_kernel(step, index_ref, flow_ref, own_ref, part_ref):
    part_ref[...] = product(step, index_ref[0] % 2, own_ref, flow_ref)


def flow_rest_kernel(step, index_ref, flow_ref, other_ref, part_ref, send_ref):
    rest = product(step, 1 - index_ref[0] % 2, other_ref, flow_ref)
    send_ref[...] = (part_ref[...] + rest).astype(BF16)


def lower_kernel(index_ref, xg0_ref, low_ref, got_ref, keep_ref, send_ref):
    da = (got_ref[...].astype(F32) * low_ref[0]).astype(BF16)
    das = (da.astype(F32) * low_ref[1]).astype(BF16)
    fill(index_ref[0], das, xg0_ref, keep_ref, send_ref)


def chip_kernel(place_ref, index_ref, keep, got, _, sum_ref, across):
    for i in range(keep.shape[0]):
        sum_ref[i] = (keep[i].astype(F32) + got[i].astype(F32)).astype(BF16)
    row = (index_ref[0] // 2) % 2
    first = (1 - place_ref[0]) * (2 * across.shape[0]) + 1 - row
    for i in range(across.shape[0]):
        across[i] = sum_ref[first + 2 * i]


def x_first(section, index):
    return section == (index // 2) % 2


def plane_kernel(
    place_ref, index_ref, sums, keep0, got0, own_ref, first_ref, second_ref, across
):
    rank = keep0.shape[1]
    chips = keep0.shape[0]
    row = (index_ref[0] // 2) % 2

    def terms_in(section, block):
        if section == 0:
            return (keep0[block].astype(F32) + got0[block].astype(F32)).astype(BF16)
        return sums[2 * chips + block]

    def order(near, along_x, along_y):
        far = 1 - near
        for i in range(own_ref.shape[0]):
            across[i] = terms_in(far, 2 * i + 1 - row)
            for to_ref, section, number in (
                (along_x, far, row),
                (along_y, near, 1 - row),
                (own_ref, near, row),
            ):
                block = 2 * i + number
                to_ref[i, 0:rank] = terms_in(section, block)
                to_ref[i, rank : 2 * rank] = sums[section * chips + block]

    along_x = x_first(place_ref[0], index_ref[0])
    for place in range(2):
        for x_is_first, ways in ((True, (first_ref, second_ref)), (False, (second_ref, first_ref))):
            pl.when((place_ref[0] == place) & (along_x == x_is_first))(
                partial(order, place, *ways)
            )


def add_kernel(own, across_out, out_ref):
    rank = across_out.shape[1]
    out_ref[:, 0:rank] = own[:, 0:rank]
    for i in range(own.shape[0]):
        total = own[i, rank : 2 * rank].astype(F32) + across_out[i].astype(F32)
        out_ref[i, rank : 2 * rank] = total.astype(BF16)


def layer_routes(layers):
    if layers == 4:
        return [[2, 3, 1, 0], [3, 2, 0, 1], [1, 0, 3, 2]]
    return [[i ^ k for i in range(layers)] for k in range(1, layers)]


def layer_kernel(routes, index_ref, own, first, across_in, second, *out_refs):
    rank = across_in.shape[1]
    layer = index_ref[0] // 4
    for route, out_ref in zip([range(len(out_refs)), *routes], out_refs):
        block = sum(jnp.where(layer == i, target, 0) for i, target in enumerate(route))
        total = sum(ref[block].astype(F32) for ref in (own, first, second))
        out_ref[0:rank] = (total[0:rank] + across_in[block].astype(F32)).astype(BF16)
        out_ref[rank : 2 * rank] = total[rank : 2 * rank].astype(BF16)


def total_kernel(*refs):
    *got, in_far, out_far, in_ref, out_ref, sems = refs
    rank = in_ref.shape[1]
    copies = []
    for i, (ref, far) in enumerate(((in_ref, in_far), (out_ref, out_far))):
        ref[0] = sum(part[i * rank : (i + 1) * rank].astype(F32) for part in got)
        copies.append(pltpu.make_async_copy(ref, far, sems.at[i]))
        copies[i].start()
    for copy in copies:
        copy.wait()


def local(kernel, name, out_shapes, *operands, scratch=(), cost=None, out="near"):
    spaces = {"scalar": pltpu.SMEM, "far": pltpu.HBM, "near": pltpu.VMEM}
    out = pl.pallas_call(
        kernel,
        in_specs=[pl.BlockSpec(memory_space=spaces[kind]) for kind, _ in operands],
        out_specs=[pl.BlockSpec(memory_space=spaces[out])] * len(out_shapes),
        out_shape=[jax.ShapeDtypeStruct(shape, dtype) for shape, dtype in out_shapes],
        scratch_shapes=list(scratch),
        compiler_params=pltpu.CompilerParams(vmem_limit_bytes=VMEM_BYTES),
        cost_estimate=cost,
        name=name,
    )(*[array for _, array in operands])
    return out if len(out) > 1 else out[0]


def near(*arrays):
    return [("near", array) for array in arrays]


def pair_on_device(saved, top_grad, gains, adapter_in, adapter_out):
    count = lax.axis_size("dp")
    tokens, width = saved.shape[2:]
    rank = adapter_in.shape[3]
    share = width // count
    chips, layers = count // 2, count // 4
    place = ("scalar", lax.axis_index("section").astype(jnp.int32)[None])
    index = ("scalar", lax.axis_index("dp").astype(jnp.int32)[None])
    saved, top, gains, w_in, w_out = [
        ("far", pltpu.with_memory_space_constraint(a, pltpu.HBM))
        for a in (saved, top_grad, gains, jnp.swapaxes(adapter_in, 2, 3), adapter_out)
    ]

    def swapped(array, way):
        pairs = []
        for s in range(2):
            for d in range(count):
                over_section, bits = way(s, d) if callable(way) else way
                pairs.append((s * count + d, (s ^ over_section) * count + (d ^ bits)))
        return lax.ppermute(array, ("section", "dp"), pairs)

    def first_way(s, d):
        return (1, 0) if x_first(s, d) else (0, 2)

    def second_way(s, d):
        return (0, 2) if x_first(s, d) else (1, 0)

    sems = pltpu.SemaphoreType.DMA
    wide = ((tokens, width), BF16)
    thin = ((rank, width), BF16)
    gain = ((1, width), F32)
    small = ((rank, tokens), BF16)
    one = ((chips, rank, share), BF16)
    three = ((3 * chips, rank, share), BF16)
    quarter = ((layers, rank, share), BF16)
    double = ((layers, 2 * rank, share), BF16)
    along_x, other_core = (1, 0), (0, 1)

    mine = local(
        pick_kernel, "pick", [((rank, width // 2), BF16)], place, index, w_out, scratch=[sems((PIECES,))]
    )
    own_half = swapped(mine, along_x)
    act0, low, xg0, x1, g, gain1, wi1, wo1 = local(
        partial(front_kernel, share), "front",
        [small, ((2, rank, tokens), F32), wide, wide, wide, gain, thin, thin],
        place, saved, top, gains, w_in, w_out,
        scratch=[pltpu.VMEM(*wide), pltpu.VMEM(*gain), pltpu.VMEM(*thin), sems((5 + 3 * PIECES,))],
    )
    got_act0 = swapped(act0, along_x)
    xg1, act1, das1, da1, columns = local(
        partial(upper_kernel, share), "upper",
        [wide, small, small, small, ((2, tokens, tokens), F32)],
        *near(x1, g, gain1, wi1, wo1),
    )
    own_half, da1 = lax.optimization_barrier((own_half, da1))
    other_half = swapped(own_half, other_core)
    flow = local(
        partial(outgoing_kernel, share), "outgoing", [wide], *near(x1, g, gain1, wi1, da1, columns),
        cost=LONG,
    )
    part = local(
        partial(flow_kernel, share), "flow", [((rank, tokens), F32)], index, *near(flow, own_half)
    )
    delta = local(
        partial(flow_rest_kernel, share), "flow_rest", [small],
        index, *near(flow, other_half, part),
    )
    got_delta = swapped(delta, along_x)
    terms1 = local(
        terms1_kernel, "terms1", [one] * 4, index, *near(g, xg1, act1, das1, delta)
    )
    keep, send = local(
        terms_kernel, "terms", [three, three], index, *near(flow, got_act0, *terms1)
    )
    got = swapped(send, other_core)
    keep0, send0 = local(
        lower_kernel, "lower", [one, one], index, *near(xg0, low, got_delta), cost=LONG
    )
    got0 = swapped(send0, other_core)
    sums, across_out = local(
        chip_kernel, "chip", [three, quarter], place, index, *near(keep, got, keep0)
    )
    across_out = swapped(across_out, (1, 2))
    own, first, second, across_in = local(
        plane_kernel, "plane", [double, double, double, quarter],
        place, index, *near(sums, keep0, got0),
    )
    first = swapped(first, first_way)
    across_in = swapped(across_in, (1, 2))
    second = swapped(second, second_way)
    own = local(add_kernel, "add", [double], *near(own, across_out), cost=MEDIUM)
    routes = layer_routes(layers)
    mine, *others = local(
        partial(layer_kernel, routes), "layer", [((2 * rank, share), BF16)] * layers,
        index, *near(own, first, across_in, second),
    )
    others = [
        lax.ppermute(
            other,
            ("section", "dp"),
            [
                (s * count + d, s * count + 4 * route[d // 4] + d % 4)
                for s in range(2)
                for d in range(count)
            ],
        )
        for route, other in zip(routes, others)
    ]
    block = ((1, rank, share), F32)
    total_in, total_out = local(
        total_kernel, "total", [block, block], *near(mine, *others),
        scratch=[pltpu.VMEM(*block), pltpu.VMEM(*block), sems((2,))], out="far",
    )
    return (jnp.swapaxes(total_in, 1, 2), total_out)


def section_back(x, gain, weight_in, weight_out, upstream):
    xf = x.astype(F32)
    scale = lax.rsqrt(jnp.mean(xf * xf, axis=-1, keepdims=True) + EPS)
    normed = xf * scale
    hidden = (normed * gain).astype(BF16)
    pre = jnp.dot(hidden, weight_in, preferred_element_type=F32)
    sig, slope = silu_slope(pre)
    active = (pre * sig).astype(BF16)
    delta_act = jnp.dot(upstream, weight_out.T, preferred_element_type=F32)
    delta_pre = (delta_act * slope).astype(BF16)
    delta_norm = jnp.dot(delta_pre, weight_in.T, preferred_element_type=F32) * gain
    inner = jnp.mean(delta_norm * normed, axis=-1, keepdims=True)
    result = (upstream.astype(F32) + scale * (delta_norm - normed * inner)).astype(BF16)
    term_in = jnp.dot(hidden.T, delta_pre, preferred_element_type=F32)
    term_out = jnp.dot(active.T, upstream, preferred_element_type=F32)
    return (result, term_in, term_out)


def relay_on_device(saved, top_grad, gains, adapter_in, adapter_out):
    sections = lax.axis_size("section")
    place = lax.axis_index("section")
    width = top_grad.shape[2]
    rank = adapter_in.shape[3]
    zero_in = jnp.zeros((width, rank), F32)
    zero_out = jnp.zeros((rank, width), F32)

    def step(turn, flows, sums):
        leaving, added = [], []
        for replica in (0, 1):
            serves = place == (sections - 1 - turn if replica == 0 else turn)
            result, term_in, term_out = lax.cond(
                serves,
                partial(
                    section_back,
                    saved[0, replica],
                    gains[0, replica],
                    adapter_in[0, replica],
                    adapter_out[0, replica],
                ),
                lambda flow: (flow, zero_in, zero_out),
                flows[replica],
            )
            leaving.append(result)
            added += [sums[2 * replica] + term_in, sums[2 * replica + 1] + term_out]
        return leaving, added

    down = [(i, i - 1) for i in range(1, sections)]
    up = [(i, i + 1) for i in range(sections - 1)]

    def turn_and_pass(turn, carry):
        leaving, sums = step(turn, carry[0], carry[1])
        return (
            [lax.ppermute(leaving[0], "section", down), lax.ppermute(leaving[1], "section", up)],
            sums,
        )

    start = ([top_grad[0], top_grad[1]], [zero_in, zero_out, zero_in, zero_out])
    flows, sums = lax.fori_loop(0, sections - 1, turn_and_pass, start)
    _, sums = step(sections - 1, flows, sums)
    shares = [
        lax.psum_scatter(term, "dp", scatter_dimension=i % 2, tiled=True)
        for i, term in enumerate(sums)
    ]
    mirror = [(i, sections - 1 - i) for i in range(sections)]
    total_in = shares[0] + lax.ppermute(shares[2], "section", mirror)
    total_out = shares[1] + lax.ppermute(shares[3], "section", mirror)
    return (total_in[None], total_out[None])


def solution(mesh):
    in_specs = (
        P("section", None, "dp", None),
        P(None, "dp", None),
        P("section", None, None),
        P("section", None, None, None),
        P("section", None, None, None),
    )
    out_specs = (P("section", "dp", None), P("section", None, "dp"))

    def run(saved, *others):
        share = saved.shape[3] // mesh.shape["dp"]
        count = mesh.shape["dp"]
        pair = mesh.shape["section"] == 2 and share % 128 == 0
        pair = pair and count >= 4 and count & (count - 1) == 0
        on_device = pair_on_device if pair else relay_on_device
        return jax.shard_map(
            on_device, mesh=mesh, in_specs=in_specs, out_specs=out_specs, check_vma=False
        )(saved, *others)

    return run
```
